32 devices in a mesh: series: 4 (over y, core), tm: 8 (over z, x).
Axes of the slice: x: 2, y: 2, z: 4, core: 2. Of those that a mesh axis runs over, the one named last changes fastest.
Arguments:
- inputs: bfloat16 [4, 3072, 512], P('series', 'tm'), may hold values from -6 to 6
- lengths: int32 [4, 4], P('series'), may hold values from 1 to 32, 64 in all within a row
- stride_weight_twelve: bfloat16 [6144, 512], P('tm'), may hold values from -0.078125 to 0.078125
- stride_bias_twelve: float32 [512], replicated, may hold values from -3 to 3
- isometric_weight_twelve: bfloat16 [8192, 512], P('tm'), may hold values from -0.0625 to 0.0625
- isometric_bias_twelve: float32 [512], replicated, may hold values from -3 to 3
- upsample_weight_twelve: bfloat16 [6144, 512], P('tm'), may hold values from -0.25 to 0.25
- upsample_bias_twelve: float32 [512], replicated, may hold values from -3 to 3
- stride_weight_sixteen: bfloat16 [8192, 512], P('tm'), may hold values from -0.0625 to 0.0625
- stride_bias_sixteen: float32 [512], replicated, may hold values from -3 to 3
- isometric_weight_sixteen: bfloat16 [6144, 512], P('tm'), may hold values from -0.078125 to 0.078125
- isometric_bias_sixteen: float32 [512], replicated, may hold values from -3 to 3
- upsample_weight_sixteen: bfloat16 [8192, 512], P('tm'), may hold values from -0.25 to 0.25
- upsample_bias_sixteen: float32 [512], replicated, may hold values from -3 to 3
- mix_gain: float32 [512], replicated, may hold values from 0.5 to 1.5
- mix_shift: float32 [512], replicated, may hold values from -2 to 2
- merge_weight: bfloat16 [1024, 512], P('tm'), may hold values from -0.1875 to 0.1875
- merge_bias: float32 [512], replicated, may hold values from -3 to 3
- feed_gain: float32 [512], replicated, may hold values from 0.5 to 1.5
- feed_shift: float32 [512], replicated, may hold values from -2 to 2
- expand_weight: bfloat16 [2048, 512], P('tm'), may hold values from -0.25 to 0.25
- expand_bias: float32 [2048], replicated, may hold values from -3 to 3
- project_weight: bfloat16 [2048, 512], P('tm'), may hold values from -0.125 to 0.125
- project_bias: float32 [512], replicated, may hold values from -3 to 3
- final_gain: float32 [512], replicated, may hold values from 0.5 to 1.5
- final_shift: float32 [512], replicated, may hold values from -2 to 2
- cotangent: bfloat16 [4, 3072, 512], P('series', 'tm'), may hold values from -6 to 6
Outputs:
- output: bfloat16 [4, 3072, 512], P('series', 'tm')
- input_grad: bfloat16 [4, 3072, 512], P('series', 'tm')
- stride_weight_twelve_grad: float32 [6144, 512], P('tm')
- stride_bias_twelve_grad: float32 [512], replicated
- isometric_weight_twelve_grad: float32 [8192, 512], P('tm')
- isometric_bias_twelve_grad: float32 [512], replicated
- upsample_weight_twelve_grad: float32 [6144, 512], P('tm')
- upsample_bias_twelve_grad: float32 [512], replicated
- stride_weight_sixteen_grad: float32 [8192, 512], P('tm')
- stride_bias_sixteen_grad: float32 [512], replicated
- isometric_weight_sixteen_grad: float32 [6144, 512], P('tm')
- isometric_bias_sixteen_grad: float32 [512], replicated
- upsample_weight_sixteen_grad: float32 [8192, 512], P('tm')
- upsample_bias_sixteen_grad: float32 [512], replicated
- mix_gain_grad: float32 [512], replicated
- mix_shift_grad: float32 [512], replicated
- merge_weight_grad: float32 [1024, 512], P('tm')
- merge_bias_grad: float32 [512], replicated
- feed_gain_grad: float32 [512], replicated
- feed_shift_grad: float32 [512], replicated
- expand_weight_grad: float32 [2048, 512], P('tm')
- expand_bias_grad: float32 [2048], replicated
- project_weight_grad: float32 [2048, 512], P('tm')
- project_bias_grad: float32 [512], replicated
- final_gain_grad: float32 [512], replicated
- final_shift_grad: float32 [512], replicated
The draws below stay inside these ranges and needn't reach their ends.
Inputs may be any that keep to these rules, and one draw needn't show every extreme that they name: Each row lists the lengths of one group's series in order, in units of 48 time steps; a row sums to 64 and its longest series has exactly 32.
All inputs are finite; a program needn't handle non-finite values.
Results may differ from the reference program's by a relative error of at most 0.017.
Values may be sent and summed in bfloat16 or wider, within the bound.
No kernel may reach another device: no remote copies, remote signals or barrier semaphores. Data moves between devices by JAX's collectives and lax.ppermute only.
A program may use at most 320 MiB of HBM per device.

```python
import math
import jax
import jax.numpy as jnp
import numpy as np
from jax import lax

D = 512
DFF = 2048
SCALE_ONE = 12
SCALE_TWO = 16
MA_ONE = 13
MA_TWO = 17
ISO_ONE = 16
ISO_TWO = 12
UNIT = 48
TOK_DEV = 384
GROUPS = 4
TOKENS = 3072
UNITS_GROUP = 64
SER_MOST = 32
NSEQ = 4


def block_levels(own_key, dims, cuts, least, top_value):
    def one(axis_at, shards_of):
        heights = jax.random.uniform(jax.random.fold_in(jax.random.fold_in(own_key, 6), axis_at), (shards_of,), jnp.float32, least / len(cuts), top_value / len(cuts))
        return jnp.repeat(jnp.exp(heights), dims[axis_at] // shards_of).reshape((-1,) + (1,) * (len(dims) - axis_at - 1))

    loudness = one(*cuts[0])
    for cut in cuts[1:]:
        loudness = loudness * one(*cut)
    return loudness


def length_profile(number_of, total, limit, lean):
    weights = [(1 << 20) // math.isqrt(standing ** lean) + 1 for standing in range(2, number_of + 1)]
    rest, given = total - limit - (number_of - 1), [1] * (number_of - 1)
    while rest > 0:
        free = [i for i in range(number_of - 1) if given[i] < limit]
        pool, left = sum([weights[i] for i in free]), rest
        for i in free:
            extra = min(limit - given[i], max(1, left * weights[i] // pool), rest)
            given[i] = given[i] + extra
            rest = rest - extra
    return np.array([limit] + given)


def ragged(own_key, count, total, limit, lean):
    if count == 2:
        one = jax.random.randint(own_key, (), max(1, total - limit), min(limit, total - 1) + 1)
        return jnp.stack([one, total - one])
    sizes = jnp.asarray(length_profile(count, total, limit, lean), jnp.int32)
    pairs = (count - 1) // 2
    source_of, sink = sizes[1:1 + 2 * pairs:2], sizes[2:2 + 2 * pairs:2]
    slack = jnp.minimum(source_of - 1, limit - sink)
    moved = jax.random.randint(jax.random.fold_in(own_key, 1), (pairs,), 0, 1 << 20) % (slack + 1)
    sizes = sizes.at[1:1 + 2 * pairs:2].set(source_of - moved).at[2:2 + 2 * pairs:2].set(sink + moved)
    return sizes[jax.random.permutation(jax.random.fold_in(own_key, 2), count)]


def noise(key, extent, deviation, most, cuts=(), kind=jnp.bfloat16):
    gain = block_levels(key, extent, cuts, -0.22, 0.18) if cuts else 1.0
    entries = jax.random.normal(key, extent, jnp.float32) * deviation * gain
    return jnp.minimum(jnp.maximum(entries, -most), most).astype(kind)


def setup_inputs(seed: int = 0) -> dict:
    arg_keys = jax.random.split(jax.random.key(seed), 28)
    return {
        "inputs": noise(arg_keys[0], (GROUPS, TOKENS, D), 1.0, 6.0, ((0, 4), (1, 8))),
        "lengths": jax.vmap(lambda own: ragged(own, NSEQ, UNITS_GROUP, SER_MOST, 2))(jax.random.split(arg_keys[1], GROUPS)).reshape((GROUPS, NSEQ)).astype(jnp.int32),
        "stride_weight_twelve": noise(arg_keys[2], (SCALE_ONE * D, D), (SCALE_ONE * D) ** -0.5, 0.078125, ((0, 8),)),
        "stride_bias_twelve": noise(arg_keys[3], (D,), 0.5, 3.0, (), jnp.float32),
        "isometric_weight_twelve": noise(arg_keys[4], (ISO_ONE * D, D), (ISO_ONE * D) ** -0.5, 0.0625, ((0, 8),)),
        "isometric_bias_twelve": noise(arg_keys[5], (D,), 0.5, 3.0, (), jnp.float32),
        "upsample_weight_twelve": noise(arg_keys[6], (SCALE_ONE * D, D), D ** -0.5, 0.25, ((0, 8),)),
        "upsample_bias_twelve": noise(arg_keys[7], (D,), 0.5, 3.0, (), jnp.float32),
        "stride_weight_sixteen": noise(arg_keys[8], (SCALE_TWO * D, D), (SCALE_TWO * D) ** -0.5, 0.0625, ((0, 8),)),
        "stride_bias_sixteen": noise(arg_keys[9], (D,), 0.5, 3.0, (), jnp.float32),
        "isometric_weight_sixteen": noise(arg_keys[10], (ISO_TWO * D, D), (ISO_TWO * D) ** -0.5, 0.078125, ((0, 8),)),
        "isometric_bias_sixteen": noise(arg_keys[11], (D,), 0.5, 3.0, (), jnp.float32),
        "upsample_weight_sixteen": noise(arg_keys[12], (SCALE_TWO * D, D), D ** -0.5, 0.25, ((0, 8),)),
        "upsample_bias_sixteen": noise(arg_keys[13], (D,), 0.5, 3.0, (), jnp.float32),
        "mix_gain": jnp.clip(1.0 + 0.1 * jax.random.normal(arg_keys[14], (D,), jnp.float32), 0.5, 1.5),
        "mix_shift": noise(arg_keys[15], (D,), 0.3, 2.0, (), jnp.float32),
        "merge_weight": noise(arg_keys[16], (2 * D, D), (2 * D) ** -0.5, 0.1875, ((0, 8),)),
        "merge_bias": noise(arg_keys[17], (D,), 0.5, 3.0, (), jnp.float32),
        "feed_gain": jnp.clip(1.0 + 0.1 * jax.random.normal(arg_keys[18], (D,), jnp.float32), 0.5, 1.5),
        "feed_shift": noise(arg_keys[19], (D,), 0.3, 2.0, (), jnp.float32),
        "expand_weight": noise(arg_keys[20], (DFF, D), D ** -0.5, 0.25, ((0, 8),)),
        "expand_bias": noise(arg_keys[21], (DFF,), 0.5, 3.0, (), jnp.float32),
        "project_weight": noise(arg_keys[22], (DFF, D), DFF ** -0.5, 0.125, ((0, 8),)),
        "project_bias": noise(arg_keys[23], (D,), 0.5, 3.0, (), jnp.float32),
        "final_gain": jnp.clip(1.0 + 0.1 * jax.random.normal(arg_keys[24], (D,), jnp.float32), 0.5, 1.5),
        "final_shift": noise(arg_keys[25], (D,), 0.3, 2.0, (), jnp.float32),
        "cotangent": noise(arg_keys[26], (GROUPS, TOKENS, D), 1.0, 6.0, ((0, 4), (1, 8))),
    }


EPSILON = 1e-05

@jax.custom_vjp
def low(v):
    return lax.optimization_barrier(v.astype(jnp.bfloat16)).astype(jnp.float32)

@jax.custom_vjp
def low_back(v):
    return v

def low_keep(v):
    return (low(v), None)

def low_pass(kept, grad):
    return (grad,)

def back_keep(v):
    return (v, None)

def back_low(kept, grad):
    return (low(grad),)
low.defvjp(low_keep, low_pass)
low_back.defvjp(back_keep, back_low)

def matmul(left, right):
    return jnp.dot(left, right, precision=lax.Precision.HIGHEST, preferred_element_type=jnp.float32)

def layer_norm(values, scale_gain, offset_shift):
    average = lax.optimization_barrier(jnp.mean(values, axis=-1, keepdims=True))
    centered = values - average
    variance = lax.optimization_barrier(jnp.mean(centered * centered, axis=-1, keepdims=True))
    return centered * lax.rsqrt(variance + EPSILON) * scale_gain + offset_shift

def series_bounds(lengths_row, places):
    ends = (UNIT * jnp.cumsum(lengths_row)).astype(jnp.int32)
    starts = (ends - UNIT * lengths_row).astype(jnp.int32)
    inside = (starts[None, :] <= places[:, None]) & (places[:, None] < ends[None, :])
    zero = jnp.zeros((), jnp.int32)
    series_first = lax.optimization_barrier(jnp.sum(jnp.where(inside, starts[None, :], zero), axis=1)).astype(jnp.int32)
    series_last = lax.optimization_barrier(jnp.sum(jnp.where(inside, ends[None, :], zero), axis=1)).astype(jnp.int32)
    return (series_first, series_last)

def branch(tokens, series_first, series_last, weights, mix_gain, mix_shift, scale, average_kernel, tap_count):
    stride_weight, stride_bias, iso_weight, iso_bias, up_weight, up_bias = weights
    row_count = tokens.shape[0]
    channels = tokens.shape[1]
    places = jnp.arange(row_count, dtype=jnp.int32)
    reach = average_kernel // 2
    trend_sum = jnp.zeros((row_count, channels), jnp.float32)
    for offset in range(-reach, reach + 1):
        gather_index = jnp.clip(places + offset, series_first, series_last - 1).astype(jnp.int32)
        trend_sum = trend_sum + tokens[gather_index]
    season = tokens - trend_sum / average_kernel
    season_low = low(season)
    half_scale = scale // 2
    step_count = row_count // scale
    padded = jnp.concatenate([jnp.zeros((half_scale, channels), jnp.float32), season_low[:row_count - half_scale]], axis=0)
    block_first = series_first[::scale]
    at_start = block_first == places[::scale]
    keep_mask = jnp.logical_not(at_start[:, None] & (jnp.arange(scale, dtype=jnp.int32)[None, :] < half_scale))
    windows = (padded.reshape(step_count, scale, channels) * keep_mask[:, :, None].astype(jnp.float32)).reshape(step_count, scale * channels)
    hidden_one = jnp.tanh(low_back(matmul(windows, stride_weight)) + stride_bias)
    hidden_low = low(hidden_one)
    lag = tap_count - 1
    hidden_ext = jnp.concatenate([jnp.zeros((lag, channels), jnp.float32), hidden_low], axis=0)
    start_step = (block_first // scale).astype(jnp.int32)
    step_index = jnp.arange(step_count, dtype=jnp.int32)
    pieces = []
    for position in range(tap_count):
        tap_valid = (step_index - lag + position >= start_step).astype(jnp.float32)
        pieces.append(hidden_ext[position:position + step_count] * tap_valid[:, None])
    stacked = jnp.concatenate(pieces, axis=1)
    hidden_two = jnp.tanh(low_back(matmul(stacked, iso_weight)) + iso_bias)
    mixed_low = low(layer_norm(hidden_two + hidden_one, mix_gain, mix_shift))
    upsampled = jnp.tanh(low_back(matmul(mixed_low, up_weight.T)).reshape(row_count, channels) + up_bias)
    return low(layer_norm(upsampled + season, mix_gain, mix_shift))

def head(merge_in, head_params):
    merge_weight, merge_bias, feed_gain, feed_shift, expand_weight, expand_bias, project_weight, project_bias, final_gain, final_shift = head_params
    merged = low_back(matmul(merge_in, merge_weight)) + merge_bias
    normed_low = low(layer_norm(merged, feed_gain, feed_shift))
    activ_low = low(jax.nn.gelu(low_back(matmul(normed_low, expand_weight.T)) + expand_bias, approximate=False))
    summed = merged + low_back(matmul(activ_low, project_weight)) + project_bias
    return layer_norm(summed, final_gain, final_shift)

def forward(tokens, params, series_first, series_last):
    branch_twelve = params[0:6]
    branch_sixteen = params[6:12]
    mix_gain, mix_shift = (params[12], params[13])
    head_params = params[14:24]
    row_count = tokens.shape[0]
    channels = tokens.shape[1]
    first_out = branch(tokens, series_first, series_last, branch_twelve, mix_gain, mix_shift, SCALE_ONE, MA_ONE, ISO_ONE)
    second_out = branch(tokens, series_first, series_last, branch_sixteen, mix_gain, mix_shift, SCALE_TWO, MA_TWO, ISO_TWO)
    merge_in = jnp.concatenate([first_out, second_out], axis=1)
    blocks = merge_in.reshape(row_count // TOK_DEV, TOK_DEV, 2 * channels)
    head_block = jax.checkpoint(lambda block: head(block, head_params))
    results = lax.map(head_block, blocks)
    return results.reshape(row_count, channels)

def reference(inputs, lengths, stride_weight_twelve, stride_bias_twelve, isometric_weight_twelve, isometric_bias_twelve, upsample_weight_twelve, upsample_bias_twelve, stride_weight_sixteen, stride_bias_sixteen, isometric_weight_sixteen, isometric_bias_sixteen, upsample_weight_sixteen, upsample_bias_sixteen, mix_gain, mix_shift, merge_weight, merge_bias, feed_gain, feed_shift, expand_weight, expand_bias, project_weight, project_bias, final_gain, final_shift, cotangent):
    params = tuple((item.astype(jnp.float32) for item in (stride_weight_twelve, stride_bias_twelve, isometric_weight_twelve, isometric_bias_twelve, upsample_weight_twelve, upsample_bias_twelve, stride_weight_sixteen, stride_bias_sixteen, isometric_weight_sixteen, isometric_bias_sixteen, upsample_weight_sixteen, upsample_bias_sixteen, mix_gain, mix_shift, merge_weight, merge_bias, feed_gain, feed_shift, expand_weight, expand_bias, project_weight, project_bias, final_gain, final_shift)))
    outputs_list = []
    input_grads = []
    totals = None
    for group_index in range(inputs.shape[0]):
        places = jnp.arange(inputs.shape[1], dtype=jnp.int32)
        series_first, series_last = series_bounds(lengths[group_index], places)

        def layer(tokens, *weights):
            return forward(tokens, weights, series_first, series_last)
        result, pullback = jax.vjp(layer, inputs[group_index].astype(jnp.float32), *params)
        gradients = pullback(cotangent[group_index].astype(jnp.float32))
        outputs_list.append(result.astype(jnp.bfloat16))
        input_grads.append(gradients[0].astype(jnp.bfloat16))
        if totals is None:
            totals = list(gradients[1:])
        else:
            totals = [left + right for left, right in zip(totals, gradients[1:])]
    return (jnp.stack(outputs_list), jnp.stack(input_grads), totals[0], totals[1], totals[2], totals[3], totals[4], totals[5], totals[6], totals[7], totals[8], totals[9], totals[10], totals[11], totals[12], totals[13], totals[14], totals[15], totals[16], totals[17], totals[18], totals[19], totals[20], totals[21], totals[22], totals[23])
```

```python
import functools
import math

import jax
import jax.numpy as jnp
from jax import lax
from jax.experimental import pallas as pl
from jax.experimental.pallas import tpu as pltpu
from jax.sharding import PartitionSpec as P

SCALES = (12, 16)
AVERAGES = (13, 17)
TAPS = (16, 12)
UNIT = 48
EPSILON = 1e-05
HALO = 16
FFN_CHUNK = 512

BF = jnp.bfloat16
F32 = jnp.float32
I32 = jnp.int32


def dot(left, right):
    return lax.dot_general(left, right, (((1,), (0,)), ((), ())), preferred_element_type=F32)


def dot_nt(left, right):
    return lax.dot_general(left, right, (((1,), (1,)), ((), ())), preferred_element_type=F32)


def dot_tn(left, right):
    return lax.dot_general(left, right, (((0,), (0,)), ((), ())), preferred_element_type=F32)


def kernel_call(body, outs, args, mib, scalars=(), scratch=()):
    specs = [
        pl.BlockSpec(memory_space=pltpu.SMEM if i in scalars else pltpu.VMEM)
        for i in range(len(args))
    ]
    return pl.pallas_call(
        body,
        out_shape=[jax.ShapeDtypeStruct(shape, dtype) for shape, dtype in outs],
        in_specs=specs,
        out_specs=[pl.BlockSpec(memory_space=pltpu.VMEM) for _ in outs],
        scratch_shapes=list(scratch),
        compiler_params=pltpu.CompilerParams(vmem_limit_bytes=mib << 20),
    )(*args)


def tap_to_payload(x, scale, q, n):
    rows, channels = x.shape
    m, h = rows // scale, channels // q
    parts = [x[:, c * q : (c + 1) * q].reshape(scale, 1, m, q) for c in range(h)]
    whole = parts[0] if h == 1 else jnp.concatenate(parts, axis=1)
    return whole.reshape(n, scale * h * m // n, q)


def payload_to_tap(p, scale, channels):
    n, rows, q = p.shape
    h = channels // q
    m = n * rows // (scale * h)
    p = p.reshape(scale, h, m, q)
    parts = [p[:, c].reshape(scale * m, q) for c in range(h)]
    return parts[0] if h == 1 else jnp.concatenate(parts, axis=1)


def payload_units(p, m):
    n, rows, q = p.shape
    p = p.reshape(n, rows // m, m, q)
    return [p[:, i].reshape(n * m, q).astype(BF) for i in range(rows // m)]


def units_to_payload(units, n):
    parts = [u.reshape(n, u.shape[0] // n, u.shape[1]) for u in units]
    return parts[0] if len(parts) == 1 else jnp.concatenate(parts, axis=1)


def store_payload(refs, parts):
    if len(refs) == 1:
        low = parts[0].shape[1]
        refs[0][:, :low, :] = parts[0].astype(BF)
        refs[0][:, low:, :] = parts[1].astype(BF)
    else:
        for ref, part in zip(refs, parts):
            ref[...] = part.astype(BF)


def load_payload(refs, low):
    if len(refs) == 1:
        return [refs[0][:, :low, :].astype(F32), refs[0][:, low:, :].astype(F32)]
    return [ref[...].astype(F32) for ref in refs]


def split_steps(ref, counts):
    whole = ref[...].astype(F32)
    n, _, channels = whole.shape
    first = whole[:, : counts[0], :].reshape(n * counts[0], channels)
    return [first, whole[:, counts[0] :, :].reshape(n * counts[1], channels)]


def join_steps(parts, n):
    return jnp.concatenate([p.reshape(n, p.shape[0] // n, p.shape[1]) for p in parts], axis=1)


def norm_stats(v):
    mean = jnp.mean(v, axis=-1, keepdims=True)
    centered = v - mean
    rstd = lax.rsqrt(jnp.mean(centered * centered, axis=-1, keepdims=True) + EPSILON)
    return centered * rstd, rstd


def norm_back(d, gain, xhat, rstd):
    dg = d * gain
    mean_d = jnp.mean(dg, axis=-1, keepdims=True)
    mean_dx = jnp.mean(dg * xhat, axis=-1, keepdims=True)
    return rstd * (dg - mean_d - xhat * mean_dx)


def column_sum(v):
    return jnp.sum(v, axis=0, keepdims=True)


def average_counts(info, kernel, columns):
    place, first, last = info[:, 0:1], info[:, 1:2], info[:, 2:3]
    reach = kernel // 2
    column = lax.broadcasted_iota(I32, (info.shape[0], columns), 1)
    away = column - place
    inside = (jnp.abs(away) <= reach) & (column >= first) & (column <= last)
    counts = jnp.where(inside, 1, 0)
    counts = counts + jnp.where(column == first, jnp.maximum(reach - (place - first), 0), 0)
    counts = counts + jnp.where(column == last, jnp.maximum(reach - (last - place), 0), 0)
    return counts, away == 0


def season_matrix(info, kernel, columns):
    counts, own = average_counts(info, kernel, columns)
    values = jnp.where(own, kernel, 0) - counts
    values = jnp.where(info[:, 0:1] >= info[:, 1:2], values, 0)
    return values.astype(F32).astype(BF)


def token_order(rows, scale):
    m = rows // scale
    place = lax.broadcasted_iota(I32, (rows, rows), 0)
    column = lax.broadcasted_iota(I32, (rows, rows), 1)
    tap = jnp.zeros_like(column)
    for k in range(1, scale):
        tap = tap + jnp.where(column >= k * m, 1, 0)
    return jnp.where(place == scale * (column - tap * m) + tap, 1.0, 0.0).astype(BF)


def windows_body(geo, tok, left, right, info_one, info_two, *outs):
    x = jnp.concatenate([left[...], tok[...], right[...]], axis=0)
    parts = []
    for b, info in enumerate((info_one, info_two)):
        matrix = season_matrix(info[...], AVERAGES[b], x.shape[0])
        parts.append(dot(matrix, x) * (1.0 / AVERAGES[b]))
    if geo["aligned"]:
        parts = [tap_to_payload(p, SCALES[b], geo["q"][b], geo["n"]) for b, p in enumerate(parts)]
        store_payload(outs, parts)
    else:
        for out, part in zip(outs, parts):
            out[...] = part.astype(BF)


def season_body(tok, left, right, info, out):
    x = jnp.concatenate([left[...], tok[...], right[...]], axis=0)
    wide = tok[...].astype(F32)
    for b in range(2):
        counts, _ = average_counts(info[...], AVERAGES[b], x.shape[0])
        out[b] = wide - dot(counts.astype(F32).astype(BF), x) * (1.0 / AVERAGES[b])


def slab_in_body(geo, transposed, *refs):
    pays, weights, out = refs[: geo["pays"]], refs[-3:-1], refs[-1]
    parts = []
    for b, p in enumerate(load_payload(pays, geo["pay_rows"][0])):
        total = None
        q = geo["q"][b]
        for i, unit in enumerate(payload_units(p, geo["m"][b])):
            term = dot(unit, weights[b][i * q : (i + 1) * q, :])
            total = term if total is None else total + term
        parts.append(total)
    out[...] = join_steps(parts, geo["n"]).astype(BF)


def slab_out_body(geo, steps, weight_one, weight_two, *outs):
    parts = []
    for b, (x, weight) in enumerate(zip(split_steps(steps, geo["m"]), (weight_one, weight_two))):
        q = geo["q"][b]
        low = x.astype(BF)
        units = [
            dot_nt(low, weight[i * q : (i + 1) * q, :]) for i in range(weight.shape[0] // q)
        ]
        parts.append(units_to_payload(units, geo["n"]))
    store_payload(outs, parts)


def slab_grad_body(geo, *refs):
    pays, steps, outs = refs[: geo["pays"]], refs[geo["pays"]], refs[-2:]
    step_parts = split_steps(steps, geo["m"])
    for b, p in enumerate(load_payload(pays, geo["pay_rows"][0])):
        q = geo["q"][b]
        right = step_parts[b].astype(BF)
        for i, unit in enumerate(payload_units(p, geo["m"][b])):
            outs[b][i * q : (i + 1) * q, :] = dot_tn(unit, right).astype(BF)


def tap_inputs(geo, b, shifts, hidden, start):
    count = hidden.shape[0]
    step = lax.broadcasted_iota(I32, (count, 1), 0)
    pieces = []
    for i in range(geo["touched"][b]):
        shift = jnp.maximum(shifts[b] - i, 0)
        moved = pltpu.roll(hidden, shift, 0)
        pieces.append(jnp.where(step - shift >= start, moved, 0.0).astype(BF))
    return pieces


def iso_body(geo, shifts, steps, start_one, start_two, weight_one, weight_two, out):
    parts = []
    hiddens = split_steps(steps, geo["m"])
    for b, (start, weight) in enumerate(((start_one, weight_one), (start_two, weight_two))):
        total = None
        channels = hiddens[b].shape[1]
        for i, piece in enumerate(tap_inputs(geo, b, shifts, hiddens[b], start[...])):
            term = dot(piece, weight[i * channels : (i + 1) * channels, :])
            total = term if total is None else total + term
        parts.append(total)
    out[...] = join_steps(parts, geo["n"]).astype(BF)


def iso_back_body(geo, shifts, d_iso, start_one, start_two, weight_one, weight_two, out):
    parts = []
    for b, (d, start, weight) in enumerate(
        zip(split_steps(d_iso, geo["m"]), (start_one, start_two), (weight_one, weight_two))
    ):
        count, channels = d.shape
        low = d.astype(BF)
        step = lax.broadcasted_iota(I32, (count, 1), 0)
        total = None
        for i in range(geo["touched"][b]):
            shift = jnp.maximum(shifts[b] - i, 0)
            stacked = dot_nt(low, weight[i * channels : (i + 1) * channels, :])
            stacked = jnp.where(step - shift >= start[...], stacked, 0.0)
            moved = pltpu.roll(stacked, lax.rem(count - shift, count), 0)
            total = moved if total is None else total + moved
        parts.append(total)
    out[...] = join_steps(parts, geo["n"]).astype(BF)


def iso_grad_body(geo, shifts, steps, d_iso, start_one, start_two, out_one, out_two):
    hiddens, ds = split_steps(steps, geo["m"]), split_steps(d_iso, geo["m"])
    for b, (start, out) in enumerate(((start_one, out_one), (start_two, out_two))):
        channels = hiddens[b].shape[1]
        right = ds[b].astype(BF)
        for i, piece in enumerate(tap_inputs(geo, b, shifts, hiddens[b], start[...])):
            out[i * channels : (i + 1) * channels, :] = dot_tn(piece, right).astype(BF)


def branch_rows(pair, counts):
    total = sum(counts)
    step = lax.broadcasted_iota(I32, (total, 1), 0)
    return jnp.where(step < counts[0], pair[0:1, :], pair[1:2, :])


def hidden_one_body(geo, parts, bias, hidden, low):
    value = jnp.tanh(jnp.sum(parts[...].astype(F32), axis=0) + branch_rows(bias, geo["m"]))
    hidden[...] = value
    low[...] = value.astype(BF)


def mix_body(geo, parts, bias, hidden_one, gain, shift, hidden, mixed):
    value = jnp.tanh(jnp.sum(parts[...].astype(F32), axis=0) + branch_rows(bias, geo["m"]))
    hidden[...] = value
    xhat, _ = norm_stats(value + hidden_one[...])
    mixed[...] = (xhat * gain[...] + shift[...]).astype(BF)


def mix_back_body(geo, parts, hidden_one, hidden_two, gain, d_pair, d_iso, sums):
    d = jnp.sum(parts[...].astype(F32), axis=0)
    two = hidden_two[...]
    xhat, rstd = norm_stats(two + hidden_one[...])
    pair = norm_back(d, gain[...], xhat, rstd)
    iso = (1.0 - two * two) * pair
    d_pair[...] = pair
    d_iso[...] = iso.astype(BF)
    low = geo["m"][0]
    sums[0:1, :] = column_sum(d * xhat)
    sums[1:2, :] = column_sum(d)
    sums[2:3, :] = column_sum(iso[:low])
    sums[3:4, :] = column_sum(iso[low:])


def conv_back_body(geo, parts, d_pair, hidden_one, d_conv, sums):
    one = hidden_one[...]
    d = (jnp.sum(parts[...].astype(F32), axis=0) + d_pair[...]) * (1.0 - one * one)
    d_conv[...] = d.astype(BF)
    low = geo["m"][0]
    sums[0:1, :] = column_sum(d[:low])
    sums[1:2, :] = column_sum(d[low:])


def head_body(geo, *refs):
    pays = refs[: geo["taps"]]
    (
        season, cotangent, up_bias, mix_gain, mix_shift, merge_weight, merge_bias, feed_gain, feed_shift,
        expand_weight, expand_bias, project_weight, project_bias, final_gain, final_shift,
    ) = refs[geo["taps"] : geo["taps"] + 15]
    outs = refs[geo["taps"] + 15 :]
    d_pays, outs = outs[: geo["taps"]], outs[geo["taps"] :]
    (
        result, d_res_out, merge_in, normed_out, activ_out, d_sum_out, d_pre_out, d_merged_out, sums, expand_sums,
        slope,
    ) = outs
    rows, channels = cotangent.shape
    width = FFN_CHUNK
    chunks = expand_weight.shape[0] // width
    if geo["aligned"]:
        taps = [
            payload_to_tap(p, SCALES[b], channels)
            for b, p in enumerate(load_payload(pays, geo["pay_rows"][0]))
        ]
    else:
        taps = [p[...] for p in pays]
    ups, kept = [], []
    for b in range(2):
        order = token_order(rows, SCALES[b])
        up = jnp.tanh(dot(order, taps[b].astype(BF)) + up_bias[b : b + 1, :])
        xhat, rstd = norm_stats(up + season[b])
        ups.append(up)
        kept.append((xhat, rstd))
        merge_in[:, b * channels : (b + 1) * channels] = (
            xhat * mix_gain[...] + mix_shift[...]
        ).astype(BF)
    merged = dot(merge_in[...], merge_weight[...]) + merge_bias[...]
    feed_hat, feed_rstd = norm_stats(merged)
    normed_out[...] = (feed_hat * feed_gain[...] + feed_shift[...]).astype(BF)

    def forward_chunk(c, total):
        at = pl.ds(pl.multiple_of(c * width, width), width)
        pre = dot_nt(normed_out[...], expand_weight[at, :]) + expand_bias[:, at]
        half = 0.5 + 0.5 * lax.erf(pre * math.sqrt(0.5))
        slope[c] = half + pre * (jnp.exp(-0.5 * pre * pre) * (1.0 / math.sqrt(2.0 * math.pi)))
        activ_out[:, at] = (pre * half).astype(BF)
        return total + dot(activ_out[:, at], project_weight[at, :])

    summed = lax.fori_loop(0, chunks, forward_chunk, merged + project_bias[...])
    final_hat, final_rstd = norm_stats(summed)
    result[...] = (final_hat * final_gain[...] + final_shift[...]).astype(BF)

    d_out = cotangent[...].astype(F32)
    sums[0:1, :] = column_sum(d_out * final_hat)
    sums[1:2, :] = column_sum(d_out)
    d_sum = norm_back(d_out, final_gain[...], final_hat, final_rstd)
    sums[2:3, :] = column_sum(d_sum)
    d_sum_out[...] = d_sum.astype(BF)

    def backward_chunk(c, total):
        at = pl.ds(pl.multiple_of(c * width, width), width)
        d_pre = slope[c] * dot_nt(d_sum_out[...], project_weight[at, :])
        expand_sums[:, at] = column_sum(d_pre)
        d_pre_out[:, at] = d_pre.astype(BF)
        return total + dot(d_pre_out[:, at], expand_weight[at, :])

    d_normed = lax.fori_loop(0, chunks, backward_chunk, jnp.zeros((rows, channels), F32))
    sums[3:4, :] = column_sum(d_normed * feed_hat)
    sums[4:5, :] = column_sum(d_normed)
    d_merged = d_sum + norm_back(d_normed, feed_gain[...], feed_hat, feed_rstd)
    sums[5:6, :] = column_sum(d_merged)
    d_merged_out[...] = d_merged.astype(BF)
    gain_sum, shift_sum = 0.0, 0.0
    d_taps = []
    for b in range(2):
        d = dot_nt(d_merged_out[...], merge_weight[b * channels : (b + 1) * channels, :])
        xhat, rstd = kept[b]
        gain_sum = gain_sum + column_sum(d * xhat)
        shift_sum = shift_sum + column_sum(d)
        d_res = norm_back(d, mix_gain[...], xhat, rstd)
        d_res_out[b] = d_res
        d_up = (1.0 - ups[b] * ups[b]) * d_res
        sums[8 + b : 9 + b, :] = column_sum(d_up)
        d_taps.append(dot_tn(token_order(rows, SCALES[b]), d_up.astype(BF)))
    sums[6:7, :] = gain_sum
    sums[7:8, :] = shift_sum
    if geo["aligned"]:
        d_taps = [tap_to_payload(d, SCALES[b], geo["q"][b], geo["n"]) for b, d in enumerate(d_taps)]
        store_payload(d_pays, d_taps)
    else:
        for out, part in zip(d_pays, d_taps):
            out[...] = part.astype(BF)


def head_grad_body(merge_in, normed, activ, d_sum, d_pre, d_merged, out):
    n = out.shape[0]
    at = 0
    for left, right in ((merge_in, d_merged), (d_pre, normed), (activ, d_sum)):
        grad = dot_tn(left[...], right[...]).astype(BF)
        size = grad.shape[0] // n
        out[:, at : at + size, :] = grad.reshape(n, size, grad.shape[1])
        at += size


def residual_body(d_res, info, out):
    rows = d_res.shape[1]
    columns = rows + 2 * HALO
    total = jnp.zeros((columns, d_res.shape[2]), F32)
    for b in range(2):
        counts, _ = average_counts(info[...], AVERAGES[b], columns)
        adjoint = dot_tn(counts.astype(F32).astype(BF), d_res[b].astype(BF))
        total = total - adjoint * (1.0 / AVERAGES[b])
    out[0:HALO, :] = total[0:HALO]
    out[HALO : HALO + rows, :] = total[HALO : HALO + rows] + d_res[0] + d_res[1]
    out[HALO + rows :, :] = total[HALO + rows :]


def input_back_body(geo, *refs):
    pays = refs[: geo["taps"]]
    info_one, info_two, residual, own, left, right = refs[geo["taps"] :]
    columns, channels = residual.shape
    rows = columns - 2 * HALO
    if geo["aligned"]:
        taps = [
            payload_to_tap(p, SCALES[b], channels)
            for b, p in enumerate(load_payload(pays, geo["pay_rows"][0]))
        ]
    else:
        taps = [p[...] for p in pays]
    total = residual[...]
    for b, info in enumerate((info_one, info_two)):
        matrix = season_matrix(info[...], AVERAGES[b], columns)
        total = total + dot_tn(matrix, taps[b].astype(BF)) * (1.0 / AVERAGES[b])
    left[...] = total[0:HALO]
    own[...] = total[HALO : HALO + rows]
    right[...] = total[HALO + rows :]


def swap(x):
    return lax.all_to_all(x, "tm", 0, 0)


def to_all(x):
    n = lax.axis_size("tm")
    return lax.all_to_all(jnp.broadcast_to(x[None], (n,) + x.shape), "tm", 0, 0)


def neighbours(n):
    up = [(i, i + 1) for i in range(n - 1)]
    return up, [(j, i) for i, j in up]


def on_device(
    inputs, lengths,
    stride_weight_twelve, stride_bias_twelve, isometric_weight_twelve, isometric_bias_twelve,
    upsample_weight_twelve, upsample_bias_twelve,
    stride_weight_sixteen, stride_bias_sixteen, isometric_weight_sixteen, isometric_bias_sixteen,
    upsample_weight_sixteen, upsample_bias_sixteen,
    mix_gain, mix_shift, merge_weight, merge_bias, feed_gain, feed_shift,
    expand_weight, expand_bias, project_weight, project_bias, final_gain, final_shift, cotangent,
):
    n = lax.axis_size("tm")
    me = lax.axis_index("tm")
    rows, channels = inputs.shape[1:]
    stride_weights = (stride_weight_twelve, stride_weight_sixteen)
    iso_weights = (isometric_weight_twelve, isometric_weight_sixteen)
    up_weights = (upsample_weight_twelve, upsample_weight_sixteen)
    m = [rows // s for s in SCALES]
    slab = [w.shape[0] for w in stride_weights]
    q = [math.gcd(*slab, channels)] * 2
    pay_rows = [slab[b] // q[b] * m[b] for b in range(2)]
    combined = q[0] == q[1]
    iso_slab = [w.shape[0] for w in iso_weights]
    iso_q = [math.gcd(r, channels) for r in iso_slab]
    touched = [-(-(iso_slab[b] + channels - iso_q[b]) // channels) for b in range(2)]
    geo = {
        "n": n, "m": m, "q": q, "pay_rows": pay_rows, "pays": 1 if combined else 2,
        "aligned": combined and q[0] % 128 == 0, "touched": touched,
    }
    if combined:
        pay_outs = [((n, sum(pay_rows), q[0]), BF)]
    else:
        pay_outs = [((n, pay_rows[b], q[b]), BF) for b in range(2)]
    tap_outs = pay_outs if geo["aligned"] else [((rows, channels), BF)] * 2
    geo["taps"] = len(tap_outs)

    def as_payload(parts):
        if geo["aligned"]:
            return parts
        parts = [tap_to_payload(p, SCALES[b], q[b], n) for b, p in enumerate(parts)]
        return [jnp.concatenate(parts, axis=1)] if combined else parts

    def as_taps(parts):
        if geo["aligned"]:
            return parts
        if combined:
            parts = [parts[0][:, : pay_rows[0]], parts[0][:, pay_rows[0] :]]
        return [payload_to_tap(p, SCALES[b], channels) for b, p in enumerate(parts)]

    lengths_row = lengths[0]
    count = lengths_row.shape[0]
    upto = jnp.arange(count)[None, :] <= jnp.arange(count)[:, None]
    ends = UNIT * jnp.sum(jnp.where(upto, lengths_row[None, :], 0), axis=1)
    starts = ends - UNIT * lengths_row

    def bounds(places):
        inside = (starts[None, :] <= places[:, None]) & (places[:, None] < ends[None, :])
        first = jnp.sum(jnp.where(inside, starts[None, :], 0), axis=1)
        return first, jnp.sum(jnp.where(inside, ends[None, :], 0), axis=1)

    base = me * rows
    local = jnp.arange(rows, dtype=I32)

    def info_of(places, anchors):
        first, last = bounds(anchors + base)
        shift = base - HALO
        return jnp.stack([places + HALO, first - shift, last - 1 - shift], axis=1)

    token_info = info_of(local, local)
    window_infos, step_starts = [], []
    for b in range(2):
        tap, step = local // m[b], local % m[b]
        anchor = SCALES[b] * step
        window_infos.append(info_of(anchor - SCALES[b] // 2 + tap, anchor))
        all_steps = jnp.arange(n * m[b], dtype=I32)
        step_starts.append((bounds(SCALES[b] * all_steps)[0] // SCALES[b])[:, None])

    head_rows = [w.shape[0] for w in (merge_weight, expand_weight, project_weight)]
    head_all = lax.all_gather(
        jnp.concatenate([merge_weight, expand_weight, project_weight], axis=0), "tm", axis=0
    )
    head_parts, at = [], 0
    for size in head_rows:
        head_parts.append(head_all[:, at : at + size].reshape(n * size, channels))
        at += size
    merge_all, expand_all, project_all = head_parts

    iso_first = [(iso_slab[b] * me) // channels for b in range(2)]
    iso_offset = [iso_slab[b] * me - iso_first[b] * channels for b in range(2)]
    iso_wide = []
    for b in range(2):
        if touched[b] * channels == iso_slab[b]:
            iso_wide.append(iso_weights[b])
        else:
            blank = jnp.zeros((touched[b] * channels, channels), BF)
            iso_wide.append(lax.dynamic_update_slice(blank, iso_weights[b], (iso_offset[b], 0)))
    shifts = jnp.stack([TAPS[b] - 1 - iso_first[b] for b in range(2)]).astype(I32)

    def row(v):
        return v[None, :]

    up_route, down_route = neighbours(n)
    tokens = inputs[0]
    left = lax.ppermute(tokens[rows - HALO :], "tm", up_route)
    right = lax.ppermute(tokens[:HALO], "tm", down_route)
    windows = kernel_call(
        functools.partial(windows_body, geo), tap_outs, (tokens, left, right, *window_infos), 24
    )
    windows = [swap(w) for w in as_payload(windows)]
    (season,) = kernel_call(
        season_body, [((2, rows, channels), F32)], (tokens, left, right, token_info), 24
    )
    step_block = [((n, sum(m), channels), BF)]
    own_steps = (sum(m), channels)
    (partial,) = kernel_call(
        functools.partial(slab_in_body, geo, False), step_block, (*windows, *stride_weights), 24
    )
    hidden_one, hidden_low = kernel_call(
        functools.partial(hidden_one_body, geo),
        [(own_steps, F32), (own_steps, BF)],
        (swap(partial), jnp.stack([stride_bias_twelve, stride_bias_sixteen])),
        8,
    )
    hidden_all = to_all(hidden_low)
    (partial,) = kernel_call(
        functools.partial(iso_body, geo),
        step_block,
        (shifts, hidden_all, *step_starts, *iso_wide),
        32,
        scalars=(0,),
    )
    hidden_two, mixed_low = kernel_call(
        functools.partial(mix_body, geo),
        [(own_steps, F32), (own_steps, BF)],
        (
            swap(partial),
            jnp.stack([isometric_bias_twelve, isometric_bias_sixteen]),
            hidden_one,
            row(mix_gain),
            row(mix_shift),
        ),
        8,
    )
    mixed_all = to_all(mixed_low)
    ups = kernel_call(
        functools.partial(slab_out_body, geo), pay_outs, (mixed_all, *up_weights), 24
    )
    ups = as_taps([swap(u) for u in ups])
    hidden_units = expand_all.shape[0]
    head = kernel_call(
        functools.partial(head_body, geo),
        [
            *tap_outs,
            ((rows, channels), BF),
            ((2, rows, channels), F32),
            ((rows, 2 * channels), BF),
            ((rows, channels), BF),
            ((rows, hidden_units), BF),
            ((rows, channels), BF),
            ((rows, hidden_units), BF),
            ((rows, channels), BF),
            ((10, channels), F32),
            ((1, hidden_units), F32),
        ],
        (
            *ups, season, cotangent[0], jnp.stack([upsample_bias_twelve, upsample_bias_sixteen]),
            row(mix_gain), row(mix_shift), merge_all, row(merge_bias), row(feed_gain), row(feed_shift),
            expand_all, row(expand_bias), project_all, row(project_bias), row(final_gain), row(final_shift),
        ),
        48,
        scratch=[pltpu.VMEM((hidden_units // FFN_CHUNK, rows, FFN_CHUNK), F32)],
    )
    d_ups, head = head[: len(tap_outs)], head[len(tap_outs) :]
    result, d_res, merge_in, normed_low, activ_low, d_sum_low, d_pre_low, d_merged_low, head_sums, expand_sums = head

    d_ups = [swap(d) for d in as_payload(d_ups)]
    (head_grad,) = kernel_call(
        head_grad_body,
        [((n, sum(head_rows), channels), BF)],
        (merge_in, normed_low, activ_low, d_sum_low, d_pre_low, d_merged_low),
        32,
    )
    head_grad = lax.psum_scatter(head_grad, "tm", scatter_dimension=0)
    head_grad = lax.psum(head_grad, "series").astype(F32)
    (residual,) = kernel_call(
        residual_body, [((rows + 2 * HALO, channels), F32)], (d_res, token_info), 24
    )
    (partial,) = kernel_call(
        functools.partial(slab_in_body, geo, True), step_block, (*d_ups, *up_weights), 24
    )
    d_pair, d_iso, mix_sums = kernel_call(
        functools.partial(mix_back_body, geo),
        [(own_steps, F32), (own_steps, BF), ((4, channels), F32)],
        (swap(partial), hidden_one, hidden_two, row(mix_gain)),
        8,
    )
    slab_outs = [((slab[b], channels), BF) for b in range(2)]
    up_grads = kernel_call(
        functools.partial(slab_grad_body, geo), slab_outs, (*d_ups, mixed_all), 24
    )
    d_iso_all = to_all(d_iso)
    (partial,) = kernel_call(
        functools.partial(iso_back_body, geo),
        step_block,
        (shifts, d_iso_all, *step_starts, *iso_wide),
        32,
        scalars=(0,),
    )
    d_conv, conv_sums = kernel_call(
        functools.partial(conv_back_body, geo),
        [(own_steps, BF), ((2, channels), F32)],
        (swap(partial), d_pair, hidden_one),
        8,
    )
    iso_grads = kernel_call(
        functools.partial(iso_grad_body, geo),
        [((touched[b] * channels, channels), BF) for b in range(2)],
        (shifts, hidden_all, d_iso_all, *step_starts),
        32,
        scalars=(0,),
    )
    iso_grads = [
        g
        if g.shape[0] == iso_slab[b]
        else lax.dynamic_slice(g, (iso_offset[b], 0), (iso_slab[b], channels))
        for b, g in enumerate(iso_grads)
    ]
    d_conv_all = to_all(d_conv)
    d_windows = kernel_call(
        functools.partial(slab_out_body, geo), pay_outs, (d_conv_all, *stride_weights), 24
    )
    d_windows = as_taps([swap(d) for d in d_windows])
    stride_grads = kernel_call(
        functools.partial(slab_grad_body, geo), slab_outs, (*windows, d_conv_all), 24
    )
    edge = ((HALO, channels), F32)
    own, to_left, to_right = kernel_call(
        functools.partial(input_back_body, geo),
        [((rows, channels), F32), edge, edge],
        (*d_windows, *window_infos, residual),
        24,
    )
    from_right = lax.ppermute(to_left, "tm", down_route)
    from_left = lax.ppermute(to_right, "tm", up_route)
    input_grad = jnp.concatenate(
        [own[:HALO] + from_left, own[HALO : rows - HALO], own[rows - HALO :] + from_right], axis=0
    ).astype(BF)

    sums = lax.psum(
        jnp.concatenate([conv_sums, mix_sums, head_sums, expand_sums.reshape(-1, channels)], axis=0),
        ("series", "tm"),
    )
    up_grads = [lax.psum(g, "series").astype(F32) for g in up_grads]
    iso_grads = [lax.psum(g, "series").astype(F32) for g in iso_grads]
    stride_grads = [lax.psum(g, "series").astype(F32) for g in stride_grads]
    head_grads, at = [], 0
    for size in head_rows:
        head_grads.append(head_grad[at : at + size])
        at += size
    return (
        result[None],
        input_grad[None],
        stride_grads[0], sums[0], iso_grads[0], sums[4], up_grads[0], sums[14],
        stride_grads[1], sums[1], iso_grads[1], sums[5], up_grads[1], sums[15],
        sums[2] + sums[12], sums[3] + sums[13],
        head_grads[0], sums[11], sums[9], sums[10],
        head_grads[1], sums[16:].reshape(-1), head_grads[2], sums[8], sums[6], sums[7],
    )


def solution(mesh):
    tokens, weight, whole = P("series", "tm", None), P("tm", None), P()
    pair = (weight, whole)
    return jax.shard_map(
        on_device,
        mesh=mesh,
        in_specs=(
            tokens, P("series", None), *(pair * 6), whole, whole, *pair, whole, whole, *pair, *pair, whole, whole,
            tokens,
        ),
        out_specs=(tokens, tokens, *(pair * 6), whole, whole, *pair, whole, whole, *pair, *pair, whole, whole),
        check_vma=False,
    )
```

```python
import functools
import math

import jax
import jax.numpy as jnp
from jax import lax
from jax.experimental import pallas as pl
from jax.experimental.pallas import tpu as pltpu
from jax.sharding import PartitionSpec as P

SCALES = (12, 16)
AVERAGES = (13, 17)
TAPS = (16, 12)
UNIT = 48
EPSILON = 1e-05
HALO = 16
FFN_CHUNK = 512
SUM_ROWS = 16

BF = jnp.bfloat16
F32 = jnp.float32
I32 = jnp.int32


def dot(left, right):
    return lax.dot_general(left, right, (((1,), (0,)), ((), ())), preferred_element_type=F32)


def dot_nt(left, right):
    return lax.dot_general(left, right, (((1,), (1,)), ((), ())), preferred_element_type=F32)


def dot_tn(left, right):
    return lax.dot_general(left, right, (((0,), (0,)), ((), ())), preferred_element_type=F32)


def kernel_call(body, outs, args, mib, scalars=(), scratch=()):
    specs = [
        pl.BlockSpec(memory_space=pltpu.SMEM if i in scalars else pltpu.VMEM)
        for i in range(len(args))
    ]
    return pl.pallas_call(
        body,
        out_shape=[jax.ShapeDtypeStruct(shape, dtype) for shape, dtype in outs],
        in_specs=specs,
        out_specs=[pl.BlockSpec(memory_space=pltpu.VMEM) for _ in outs],
        scratch_shapes=list(scratch),
        compiler_params=pltpu.CompilerParams(vmem_limit_bytes=mib << 20),
    )(*args)


def tap_to_payload(x, scale, q, n):
    rows, channels = x.shape
    m, h = rows // scale, channels // q
    parts = [x[:, c * q : (c + 1) * q].reshape(scale, 1, m, q) for c in range(h)]
    whole = parts[0] if h == 1 else jnp.concatenate(parts, axis=1)
    return whole.reshape(n, scale * h * m // n, q)


def payload_to_tap(p, scale, channels):
    n, rows, q = p.shape
    h = channels // q
    m = n * rows // (scale * h)
    p = p.reshape(scale, h, m, q)
    parts = [p[:, c].reshape(scale * m, q) for c in range(h)]
    return parts[0] if h == 1 else jnp.concatenate(parts, axis=1)


def payload_units(p, m):
    n, rows, q = p.shape
    p = p.reshape(n, rows // m, m, q)
    return [p[:, i].reshape(n * m, q).astype(BF) for i in range(rows // m)]


def units_to_payload(units, n):
    parts = [u.reshape(n, u.shape[0] // n, u.shape[1]) for u in units]
    return parts[0] if len(parts) == 1 else jnp.concatenate(parts, axis=1)


def split_steps(ref, counts):
    whole = ref[...].astype(F32)
    n, _, channels = whole.shape
    first = whole[:, : counts[0], :].reshape(n * counts[0], channels)
    return [first, whole[:, counts[0] : sum(counts), :].reshape(n * counts[1], channels)]


def join_steps(parts, n):
    return jnp.concatenate([p.reshape(n, p.shape[0] // n, p.shape[1]) for p in parts], axis=1)


def norm_stats(v):
    mean = jnp.mean(v, axis=-1, keepdims=True)
    centered = v - mean
    rstd = lax.rsqrt(jnp.mean(centered * centered, axis=-1, keepdims=True) + EPSILON)
    return centered * rstd, rstd


def norm_back(d, gain, xhat, rstd):
    dg = d * gain
    mean_d = jnp.mean(dg, axis=-1, keepdims=True)
    mean_dx = jnp.mean(dg * xhat, axis=-1, keepdims=True)
    return rstd * (dg - mean_d - xhat * mean_dx)


def column_sum(v):
    return jnp.sum(v, axis=0, keepdims=True)


def average_counts(info, kernel, columns):
    place, first, last = info[:, 0:1], info[:, 1:2], info[:, 2:3]
    reach = kernel // 2
    column = lax.broadcasted_iota(I32, (info.shape[0], columns), 1)
    away = column - place
    inside = (jnp.abs(away) <= reach) & (column >= first) & (column <= last)
    counts = jnp.where(inside, 1, 0)
    counts = counts + jnp.where(column == first, jnp.maximum(reach - (place - first), 0), 0)
    counts = counts + jnp.where(column == last, jnp.maximum(reach - (last - place), 0), 0)
    return counts, away == 0


def season_matrix(info, kernel, columns):
    counts, own = average_counts(info, kernel, columns)
    values = jnp.where(own, kernel, 0) - counts
    values = jnp.where(info[:, 0:1] >= info[:, 1:2], values, 0)
    return values.astype(F32).astype(BF)


def token_order(rows, scale):
    m = rows // scale
    place = lax.broadcasted_iota(I32, (rows, rows), 0)
    column = lax.broadcasted_iota(I32, (rows, rows), 1)
    tap = jnp.zeros_like(column)
    for k in range(1, scale):
        tap = tap + jnp.where(column >= k * m, 1, 0)
    return jnp.where(place == scale * (column - tap * m) + tap, 1.0, 0.0).astype(BF)


def join_payload(geo, taps):
    return jnp.concatenate(
        [tap_to_payload(t, SCALES[b], geo["q"], geo["n"]) for b, t in enumerate(taps)], axis=1
    )


def split_payload(geo, payload, channels):
    low = geo["pay_rows"][0]
    parts = (payload[:, :low], payload[:, low:])
    return [payload_to_tap(p, SCALES[b], channels) for b, p in enumerate(parts)]


def store_taps(geo, outs, taps):
    if not geo["aligned"]:
        for out, tap in zip(outs, taps):
            out[...] = tap.astype(BF)
        return
    outs[0][...] = join_payload(geo, taps).astype(BF)


def load_taps(geo, pays, channels):
    if not geo["aligned"]:
        return [p[...] for p in pays]
    whole = pays[0][...].astype(F32)
    return [t.astype(BF) for t in split_payload(geo, whole, channels)]


def windows_body(geo, tok, left, right, info_one, info_two, *outs):
    x = jnp.concatenate([left[...], tok[...], right[...]], axis=0)
    parts = []
    for b, info in enumerate((info_one, info_two)):
        matrix = season_matrix(info[...], AVERAGES[b], x.shape[0])
        parts.append(dot(matrix, x) * (1.0 / AVERAGES[b]))
    store_taps(geo, outs, parts)


def season_body(tok, left, right, info, out):
    x = jnp.concatenate([left[...], tok[...], right[...]], axis=0)
    wide = tok[...].astype(F32)
    for b in range(2):
        counts, _ = average_counts(info[...], AVERAGES[b], x.shape[0])
        out[b] = wide - dot(counts.astype(F32).astype(BF), x) * (1.0 / AVERAGES[b])


def slab_starts(geo):
    return (0, geo["slab"][0])


def units_against(geo, payload, weight, totals):
    low = geo["pay_rows"][0]
    for b, p in enumerate((payload[:, :low], payload[:, low:])):
        q, start = geo["q"], slab_starts(geo)[b]
        for i, unit in enumerate(payload_units(p, geo["m"][b])):
            term = dot(unit, weight[start + i * q : start + (i + 1) * q, :])
            totals[b] = term if totals[b] is None else totals[b] + term


def slab_in_body(geo, payload, weight, out):
    totals = [None, None]
    units_against(geo, payload[...].astype(F32), weight, totals)
    out[...] = join_steps(totals, geo["n"]).astype(BF)


def steps_against(geo, lows, weight, n):
    q = geo["q"]
    parts = []
    for b, low in enumerate(lows):
        start = slab_starts(geo)[b]
        units = [
            dot_nt(low, weight[start + i * q : start + (i + 1) * q, :])
            for i in range(geo["slab"][b] // q)
        ]
        parts.append(units_to_payload(units, n))
    return jnp.concatenate(parts, axis=1).astype(BF)


def slab_out_body(geo, steps, own, out):
    lows = [x.astype(BF) for x in split_steps(steps, geo["m"])]
    out[...] = steps_against(geo, lows, own, geo["n"])


def store_halved(out, start, size, at, value):
    step = math.gcd(value.shape[0], size // 2)
    for i in range(0, value.shape[0], step):
        h, r = divmod(at + i, size // 2)
        out[h, start + r : start + r + step, :] = value[i : i + step].astype(BF)


def store_core_parts(core, halves, rows, own, sent):
    blank = jnp.zeros((SUM_ROWS - len(rows), halves.shape[2]), F32)
    halves[0, halves.shape[1] - SUM_ROWS :, :] = jnp.concatenate([*rows, blank], axis=0).astype(BF)
    halves[1, halves.shape[1] - SUM_ROWS :, :] = jnp.zeros((SUM_ROWS, halves.shape[2]), BF)
    own[...] = halves[core]
    sent[...] = halves[1 - core]


def slab_grad_body(geo, core, payload, steps, own, sent, halves):
    low, q, slab = geo["pay_rows"][0], geo["q"], geo["slab"]
    rights = split_steps(steps, geo["m"])
    wide = payload[...].astype(F32)
    for b in range(2):
        right = rights[b].astype(BF)
        part = wide[:, :low] if b == 0 else wide[:, low:]
        for i, unit in enumerate(payload_units(part, geo["m"][b])):
            store_halved(halves, slab_starts(geo)[b] // 2, slab[b], i * q, dot_tn(unit, right))
    store_core_parts(core[0], halves, [column_sum(r) for r in rights], own, sent)


def join_body(core, part, got, out_one, out_two, sums):
    at = 0
    for out in (out_one, out_two, sums):
        rows = out.shape[0] // 2
        for which, value in ((core[0], part), (1 - core[0], got)):
            begin = pl.multiple_of(which * rows, math.gcd(rows, 512))
            out[pl.ds(begin, rows), :] = value[at : at + rows, :].astype(F32)
        at += rows


def tap_inputs(geo, b, shifts, hidden, start):
    count = hidden.shape[0]
    step = lax.broadcasted_iota(I32, (count, 1), 0)
    pieces = []
    for i in range(geo["touched"][b]):
        shift = jnp.maximum(shifts[b] - i, 0)
        moved = pltpu.roll(hidden, shift, 0)
        pieces.append(jnp.where(step - shift >= start, moved, 0.0).astype(BF))
    return pieces


def iso_body(geo, shifts, steps, start_one, start_two, weight_one, weight_two, out):
    parts = []
    hiddens = split_steps(steps, geo["m"])
    for b, (start, weight) in enumerate(((start_one, weight_one), (start_two, weight_two))):
        total = None
        channels = hiddens[b].shape[1]
        for i, piece in enumerate(tap_inputs(geo, b, shifts, hiddens[b], start[...])):
            term = dot(piece, weight[i * channels : (i + 1) * channels, :])
            total = term if total is None else total + term
        parts.append(total)
    out[...] = join_steps(parts, geo["n"]).astype(BF)


def iso_back_body(geo, shifts, d_iso, start_one, start_two, weight_one, weight_two, out):
    parts = []
    for b, (d, start, weight) in enumerate(
        zip(split_steps(d_iso, geo["m"]), (start_one, start_two), (weight_one, weight_two))
    ):
        count, channels = d.shape
        low = d.astype(BF)
        step = lax.broadcasted_iota(I32, (count, 1), 0)
        total = None
        for i in range(geo["touched"][b]):
            shift = jnp.maximum(shifts[b] - i, 0)
            stacked = dot_nt(low, weight[i * channels : (i + 1) * channels, :])
            stacked = jnp.where(step - shift >= start[...], stacked, 0.0)
            moved = pltpu.roll(stacked, lax.rem(count - shift, count), 0)
            total = moved if total is None else total + moved
        parts.append(total)
    out[...] = join_steps(parts, geo["n"]).astype(BF)


def iso_grad_body(geo, shifts, steps, d_iso, start_one, start_two, own, sent, wide_one, wide_two, halves):
    hiddens, ds = split_steps(steps, geo["m"]), split_steps(d_iso, geo["m"])
    begin = 0
    for b, (start, wide) in enumerate(((start_one, wide_one), (start_two, wide_two))):
        channels = hiddens[b].shape[1]
        right = ds[b].astype(BF)
        for i, piece in enumerate(tap_inputs(geo, b, shifts, hiddens[b], start[...])):
            wide[i * channels : (i + 1) * channels, :] = dot_tn(piece, right)
        part = geo["iso_slab"][b] // 2
        for h in range(2):
            at = pl.multiple_of(shifts[2 + b] + h * part, math.gcd(geo["iso_q"][b], part))
            halves[h, begin : begin + part, :] = wide[pl.ds(at, part), :].astype(BF)
        begin += part
    at = sum(geo["m"])
    norm_sums = jnp.sum(d_iso[:, at:, :].astype(F32), axis=0)
    rows = [*(column_sum(d) for d in ds), norm_sums[0:1], norm_sums[1:2]]
    store_core_parts(shifts[4], halves, rows, own, sent)


def branch_rows(pair, counts):
    total = sum(counts)
    step = lax.broadcasted_iota(I32, (total, 1), 0)
    return jnp.where(step < counts[0], pair[0:1, :], pair[1:2, :])


def hidden_one_body(geo, parts, bias, hidden, low):
    value = jnp.tanh(jnp.sum(parts[...].astype(F32), axis=0) + branch_rows(bias, geo["m"]))
    hidden[...] = value
    low[...] = jnp.broadcast_to(value.astype(BF)[None], low.shape)


def mix_body(geo, parts, bias, hidden_one, gain, shift, hidden, mixed):
    value = jnp.tanh(jnp.sum(parts[...].astype(F32), axis=0) + branch_rows(bias, geo["m"]))
    hidden[...] = value
    xhat, _ = norm_stats(value + hidden_one[...])
    low = (xhat * gain[...] + shift[...]).astype(BF)
    mixed[...] = jnp.broadcast_to(low[None], mixed.shape)


def mix_back_body(geo, parts, hidden_one, hidden_two, gain, d_pair, d_iso):
    d = jnp.sum(parts[...].astype(F32), axis=0)
    two = hidden_two[...]
    xhat, rstd = norm_stats(two + hidden_one[...])
    pair = norm_back(d, gain[...], xhat, rstd)
    iso = (1.0 - two * two) * pair
    d_pair[...] = pair
    blank = jnp.zeros((d_iso.shape[1] - iso.shape[0] - 2, iso.shape[1]), F32)
    low = jnp.concatenate([iso, column_sum(d * xhat), column_sum(d), blank], axis=0).astype(BF)
    d_iso[...] = jnp.broadcast_to(low[None], d_iso.shape)


def conv_back_body(geo, parts, d_pair, hidden_one, d_conv):
    one = hidden_one[...]
    d = (jnp.sum(parts[...].astype(F32), axis=0) + d_pair[...]) * (1.0 - one * one)
    d_conv[...] = jnp.broadcast_to(d.astype(BF)[None], d_conv.shape)


def place_head(geo, order, pieces, merge, expand, project):
    m_rows, h_rows = geo["quarter_rows"][:2]
    for first, begin, piece in pieces:
        for i in range(piece.shape[0]):
            block = first + 2 * (begin + i)
            at = pl.multiple_of(order[block] * m_rows, m_rows)
            merge[pl.ds(at, m_rows), :] = piece[i, :m_rows, :]
            at = pl.ds(pl.multiple_of(order[block] * h_rows, h_rows), h_rows)
            expand[at, :] = piece[i, m_rows : m_rows + h_rows, :]
            project[at, :] = piece[i, m_rows + h_rows :, :]


def head_body(geo, *refs):
    taps = geo["taps"]
    pays, refs = refs[:taps], refs[taps:]
    (
        season, cotangent, up_bias, mix_gain, mix_shift, merge_bias, feed_gain, feed_shift,
        expand_bias, project_bias, final_gain, final_shift,
    ) = refs[:12]
    refs = refs[12:]
    if geo["fits"]:
        order, pieces, refs = refs[0], refs[1 : 1 + geo["pieces"]], refs[1 + geo["pieces"] :]
        merge_weight, expand_weight, project_weight = refs[-3:]
        refs = refs[:-3]
        pieces = [(*at, piece) for at, piece in zip(geo["piece_starts"], pieces)]
        place_head(geo, order, pieces, merge_weight, expand_weight, project_weight)
    else:
        (merge_weight, expand_weight, project_weight), refs = refs[:3], refs[3:]
    d_pays, outs = refs[:taps], refs[taps:]
    (
        result, d_res_out, merge_in, normed_out, activ_out, d_sum_out, d_pre_out, d_merged_out, sums, expand_sums,
        slope,
    ) = outs
    rows, channels = cotangent.shape
    width = FFN_CHUNK
    chunks = expand_weight.shape[0] // width
    taps = load_taps(geo, pays, channels)
    ups, kept = [], []
    for b in range(2):
        order = token_order(rows, SCALES[b])
        up = jnp.tanh(dot(order, taps[b]) + up_bias[b : b + 1, :])
        xhat, rstd = norm_stats(up + season[b])
        ups.append(up)
        kept.append((xhat, rstd))
        merge_in[:, b * channels : (b + 1) * channels] = (
            xhat * mix_gain[...] + mix_shift[...]
        ).astype(BF)
    merged = dot(merge_in[...], merge_weight[...]) + merge_bias[...]
    feed_hat, feed_rstd = norm_stats(merged)
    normed_out[...] = (feed_hat * feed_gain[...] + feed_shift[...]).astype(BF)

    def forward_chunk(c, total):
        at = pl.ds(pl.multiple_of(c * width, width), width)
        pre = dot_nt(normed_out[...], expand_weight[at, :]) + expand_bias[:, at]
        half = 0.5 + 0.5 * lax.erf(pre * math.sqrt(0.5))
        slope[c] = half + pre * (jnp.exp(-0.5 * pre * pre) * (1.0 / math.sqrt(2.0 * math.pi)))
        activ_out[:, at] = (pre * half).astype(BF)
        return total + dot(activ_out[:, at], project_weight[at, :])

    summed = lax.fori_loop(0, chunks, forward_chunk, merged + project_bias[...])
    final_hat, final_rstd = norm_stats(summed)
    result[...] = (final_hat * final_gain[...] + final_shift[...]).astype(BF)

    d_out = cotangent[...].astype(F32)
    sums[0:1, :] = column_sum(d_out * final_hat)
    sums[1:2, :] = column_sum(d_out)
    d_sum = norm_back(d_out, final_gain[...], final_hat, final_rstd)
    sums[2:3, :] = column_sum(d_sum)
    d_sum_out[...] = d_sum.astype(BF)

    def backward_chunk(c, total):
        at = pl.ds(pl.multiple_of(c * width, width), width)
        d_pre = slope[c] * dot_nt(d_sum_out[...], project_weight[at, :])
        expand_sums[:, at] = column_sum(d_pre)
        d_pre_out[:, at] = d_pre.astype(BF)
        return total + dot(d_pre_out[:, at], expand_weight[at, :])

    d_normed = lax.fori_loop(0, chunks, backward_chunk, jnp.zeros((rows, channels), F32))
    sums[3:4, :] = column_sum(d_normed * feed_hat)
    sums[4:5, :] = column_sum(d_normed)
    d_merged = d_sum + norm_back(d_normed, feed_gain[...], feed_hat, feed_rstd)
    sums[5:6, :] = column_sum(d_merged)
    d_merged_out[...] = d_merged.astype(BF)
    gain_sum, shift_sum = 0.0, 0.0
    d_taps = []
    for b in range(2):
        d = dot_nt(d_merged_out[...], merge_weight[b * channels : (b + 1) * channels, :])
        xhat, rstd = kept[b]
        gain_sum = gain_sum + column_sum(d * xhat)
        shift_sum = shift_sum + column_sum(d)
        d_res = norm_back(d, mix_gain[...], xhat, rstd)
        d_res_out[b] = d_res
        d_up = (1.0 - ups[b] * ups[b]) * d_res
        sums[8 + b : 9 + b, :] = column_sum(d_up)
        d_taps.append(dot_tn(token_order(rows, SCALES[b]), d_up.astype(BF)))
    sums[6:7, :] = gain_sum
    sums[7:8, :] = shift_sum
    store_taps(geo, d_pays, d_taps)


def head_grad_body(geo, *refs):
    lefts = refs[:6]
    merge_in, normed, activ, d_sum, d_pre, d_merged = lefts
    pairs = ((merge_in, d_merged), (d_pre, normed), (activ, d_sum))
    if not geo["fits"]:
        for out, (left, right) in zip(refs[6:], pairs):
            out[...] = dot_tn(left[...], right[...]).astype(BF)
        return
    sums, expand_sums, order, own, other, merge, hidden = refs[6:]
    blocks, _, channels = own.shape
    m_rows, h_rows = geo["quarter_rows"][:2]
    at = m_rows + 2 * h_rows
    count = sums.shape[0] + expand_sums.shape[0]
    rows = jnp.concatenate(
        [sums[...], expand_sums[...], jnp.zeros((SUM_ROWS - count, channels), F32)], axis=0
    ).astype(BF)
    start = 0
    for (left, right), grads, size in zip(pairs, (merge, hidden, hidden), (m_rows, h_rows, h_rows)):
        grads[...] = dot_tn(left[...], right[...]).astype(BF)
        for h, out in enumerate((own, other)):
            for i in range(blocks):
                begin = pl.multiple_of(order[h * blocks + i] * size, size)
                out[i, start : start + size, :] = grads[pl.ds(begin, size), :]
        start += size
    for out in (own, other):
        out[:, at:, :] = jnp.broadcast_to(rows, (blocks, *rows.shape))


def residual_body(d_res, info, out):
    rows = d_res.shape[1]
    columns = rows + 2 * HALO
    total = jnp.zeros((columns, d_res.shape[2]), F32)
    for b in range(2):
        counts, _ = average_counts(info[...], AVERAGES[b], columns)
        adjoint = dot_tn(counts.astype(F32).astype(BF), d_res[b].astype(BF))
        total = total - adjoint * (1.0 / AVERAGES[b])
    out[0:HALO, :] = total[0:HALO]
    out[HALO : HALO + rows, :] = total[HALO : HALO + rows] + d_res[0] + d_res[1]
    out[HALO + rows :, :] = total[HALO + rows :]


def input_back_body(geo, *refs):
    pays = refs[: geo["taps"]]
    info_one, info_two, residual, own, left, right = refs[geo["taps"] :]
    columns, channels = residual.shape
    rows = columns - 2 * HALO
    taps = load_taps(geo, pays, channels)
    total = residual[...]
    for b, info in enumerate((info_one, info_two)):
        matrix = season_matrix(info[...], AVERAGES[b], columns)
        total = total + dot_tn(matrix, taps[b]) * (1.0 / AVERAGES[b])
    left[...] = total[0:HALO]
    own[...] = total[HALO : HALO + rows]
    right[...] = total[HALO + rows :]


def swap(x):
    return lax.all_to_all(x, "tm", 0, 0)


def together(*values):
    return lax.optimization_barrier(values)


def after(x, dep):
    return lax.optimization_barrier((x, dep))[0]


def across(x, axis, bit):
    return lax.ppermute(x, axis, [(i, i ^ bit) for i in range(lax.axis_size(axis))])


def bit_of(axis, bit):
    return (lax.axis_index(axis) & bit) // bit


def by_replica(x):
    x = jnp.where(bit_of("series", 1) == 1, x[::-1], x)
    return jnp.where(bit_of("series", 2) == 1, x[:, :, ::-1], x)


def summed(*parts):
    return sum(p.astype(F32) for p in parts).astype(BF)


def neighbours(n):
    up = [(i, i + 1) for i in range(n - 1)]
    return up, [(j, i) for i, j in up]


def on_device(
    inputs, lengths,
    stride_weight_twelve, stride_bias_twelve, isometric_weight_twelve, isometric_bias_twelve,
    upsample_weight_twelve, upsample_bias_twelve,
    stride_weight_sixteen, stride_bias_sixteen, isometric_weight_sixteen, isometric_bias_sixteen,
    upsample_weight_sixteen, upsample_bias_sixteen,
    mix_gain, mix_shift, merge_weight, merge_bias, feed_gain, feed_shift,
    expand_weight, expand_bias, project_weight, project_bias, final_gain, final_shift, cotangent,
):
    n = lax.axis_size("tm")
    me = lax.axis_index("tm")
    rows, channels = inputs.shape[1:]
    stride_weights = (stride_weight_twelve, stride_weight_sixteen)
    iso_weights = (isometric_weight_twelve, isometric_weight_sixteen)
    up_weights = (upsample_weight_twelve, upsample_weight_sixteen)
    m = [rows // s for s in SCALES]
    slab = [w.shape[0] for w in stride_weights]
    q = math.gcd(*slab, channels)
    pay_rows = [slab[b] // q * m[b] for b in range(2)]
    iso_slab = [w.shape[0] for w in iso_weights]
    iso_q = [math.gcd(r, channels) for r in iso_slab]
    touched = [-(-(iso_slab[b] + channels - iso_q[b]) // channels) for b in range(2)]
    half = n // 2
    geo = {
        "n": n, "half": half, "m": m, "q": q, "slab": slab, "pay_rows": pay_rows, "touched": touched,
        "iso_slab": iso_slab, "iso_q": iso_q,
        "aligned": q % 128 == 0,
    }
    geo["taps"] = 1 if geo["aligned"] else 2
    pay_shape = (n, sum(pay_rows), q)
    pay_outs = [(pay_shape, BF)] if geo["aligned"] else [((rows, channels), BF)] * 2

    def as_payload(parts):
        return parts[0] if geo["aligned"] else join_payload(geo, parts)

    def as_taps(payload):
        return [payload] if geo["aligned"] else split_payload(geo, payload, channels)

    def row(v):
        return v[None, :]

    lengths_row = lengths[0]
    count = lengths_row.shape[0]
    upto = jnp.arange(count)[None, :] <= jnp.arange(count)[:, None]
    ends = UNIT * jnp.sum(jnp.where(upto, lengths_row[None, :], 0), axis=1)
    starts = ends - UNIT * lengths_row

    def bounds(places):
        inside = (starts[None, :] <= places[:, None]) & (places[:, None] < ends[None, :])
        first = jnp.sum(jnp.where(inside, starts[None, :], 0), axis=1)
        return first, jnp.sum(jnp.where(inside, ends[None, :], 0), axis=1)

    base = me * rows
    local = jnp.arange(rows, dtype=I32)

    def info_of(places, anchors):
        first, last = bounds(anchors + base)
        shift = base - HALO
        return jnp.stack([places + HALO, first - shift, last - 1 - shift], axis=1)

    token_info = info_of(local, local)
    window_infos, step_starts = [], []
    for b in range(2):
        tap, step = local // m[b], local % m[b]
        anchor = SCALES[b] * step
        window_infos.append(info_of(anchor - SCALES[b] // 2 + tap, anchor))
        all_steps = jnp.arange(n * m[b], dtype=I32)
        step_starts.append((bounds(SCALES[b] * all_steps)[0] // SCALES[b])[:, None])

    replica = lax.axis_index("series")

    head_weights = (merge_weight, expand_weight, project_weight)
    head_rows = [w.shape[0] for w in head_weights]
    quarter_rows = [r // 4 for r in head_rows]
    geo["quarter_rows"] = quarter_rows
    geo["fits"] = all(r % 16 == 0 for r in quarter_rows)
    quarter = jnp.concatenate(
        [lax.dynamic_slice_in_dim(w, replica * r, r) for w, r in zip(head_weights, quarter_rows)], axis=0
    )
    stride_own = jnp.concatenate(stride_weights, axis=0)
    up_own = jnp.concatenate(up_weights, axis=0)

    devices = jnp.arange(n, dtype=I32)
    offset = jnp.asarray([[0, 2], [1, 3]], I32) ^ replica
    order = (4 * devices[None, :, None] + offset[:, None, :]).reshape(-1)
    iso_first = [(iso_slab[b] * me) // channels for b in range(2)]
    iso_offset = [iso_slab[b] * me - iso_first[b] * channels for b in range(2)]
    iso_wide = []
    for b in range(2):
        if touched[b] * channels == iso_slab[b]:
            iso_wide.append(iso_weights[b])
        else:
            blank = jnp.zeros((touched[b] * channels, channels), BF)
            iso_wide.append(lax.dynamic_update_slice(blank, iso_weights[b], (iso_offset[b], 0)))
    shifts = jnp.stack([*(TAPS[b] - 1 - iso_first[b] for b in range(2)), *iso_offset, replica & 1]).astype(I32)

    up_route, down_route = neighbours(n)
    tokens = inputs[0]
    step_block = [((n, sum(m), channels), BF)]
    own_steps = (sum(m), channels)
    left = lax.ppermute(tokens[rows - HALO :], "tm", up_route)
    right = lax.ppermute(tokens[:HALO], "tm", down_route)
    windows = kernel_call(
        functools.partial(windows_body, geo), pay_outs, (tokens, left, right, *window_infos), 24
    )
    windows = swap(as_payload(windows))
    (partial,) = kernel_call(
        functools.partial(slab_in_body, geo), step_block, (windows, stride_own), 24
    )
    partial = swap(partial)
    hidden_one, hidden_low = kernel_call(
        functools.partial(hidden_one_body, geo),
        [(own_steps, F32), ((n, *own_steps), BF)],
        (partial, jnp.stack([stride_bias_twelve, stride_bias_sixteen])),
        8,
    )
    blocks = lax.all_gather(quarter, "tm", axis=0)
    hidden_all, blocks = together(swap(hidden_low), blocks)
    (partial,) = kernel_call(
        functools.partial(iso_body, geo),
        step_block,
        (shifts, hidden_all, *step_starts, *iso_wide),
        32,
        scalars=(0,),
    )
    partial, blocks_a = together(swap(partial), across(blocks[:half], "series", 2))
    hidden_two, mixed_low = kernel_call(
        functools.partial(mix_body, geo),
        [(own_steps, F32), ((n, *own_steps), BF)],
        (
            partial,
            jnp.stack([isometric_bias_twelve, isometric_bias_sixteen]),
            hidden_one,
            row(mix_gain),
            row(mix_shift),
        ),
        8,
    )
    (season,) = kernel_call(
        season_body, [((2, rows, channels), F32)], (tokens, left, right, token_info), 24
    )
    mixed_all, season, blocks_b, blocks_core = together(
        swap(mixed_low), season, across(blocks[half:], "series", 2), across(blocks, "series", 1)
    )
    (ups,) = kernel_call(
        functools.partial(slab_out_body, geo), [(pay_shape, BF)], (mixed_all, up_own), 24
    )
    ups, core_a, core_b = together(
        swap(ups), across(blocks_a, "series", 1), across(blocks_b, "series", 1)
    )
    head_pieces = [blocks, blocks_a, blocks_b, blocks_core, core_a, core_b]
    geo["piece_starts"] = [(0, 0), (1, 0), (1, half), (2 * n, 0), (2 * n + 1, 0), (2 * n + 1, half)]
    geo["pieces"] = len(head_pieces)
    hidden_units = 4 * n * quarter_rows[1]
    head_args = [
        *as_taps(ups), season, cotangent[0], jnp.stack([upsample_bias_twelve, upsample_bias_sixteen]),
        row(mix_gain), row(mix_shift), row(merge_bias), row(feed_gain), row(feed_shift),
        row(expand_bias), row(project_bias), row(final_gain), row(final_shift),
    ]
    head_scratch = [pltpu.VMEM((hidden_units // FFN_CHUNK, rows, FFN_CHUNK), F32)]
    scalars = ()
    if geo["fits"]:
        scalars = (len(head_args),)
        head_args += [order, *head_pieces]
        head_scratch += [pltpu.VMEM((2 * channels, channels), BF)]
        head_scratch += [pltpu.VMEM((hidden_units, channels), BF)] * 2
    else:
        whole = [
            jnp.stack([own, jnp.concatenate(other)], axis=1)
            for own, *other in (head_pieces[:3], head_pieces[3:])
        ]
        whole = by_replica(jnp.stack(whole))
        whole = jnp.moveaxis(whole, 0, 2).reshape(4 * n, *blocks.shape[1:])
        cuts = [quarter_rows[0], sum(quarter_rows[:2])]
        head_args += [w.reshape(-1, channels) for w in jnp.split(whole, cuts, axis=1)]
    head = kernel_call(
        functools.partial(head_body, geo),
        [
            *pay_outs,
            ((rows, channels), BF),
            ((2, rows, channels), F32),
            ((rows, 2 * channels), BF),
            ((rows, channels), BF),
            ((rows, hidden_units), BF),
            ((rows, channels), BF),
            ((rows, hidden_units), BF),
            ((rows, channels), BF),
            ((10, channels), F32),
            ((1, hidden_units), F32),
        ],
        head_args,
        44,
        scalars=scalars,
        scratch=head_scratch,
    )
    d_ups, head = head[: geo["taps"]], head[geo["taps"] :]
    result, d_res, *head_lefts, head_sums, expand_sums = head
    merge_in, normed_low, activ_low, d_sum_low, d_pre_low, d_merged_low = head_lefts

    expand_sums = expand_sums.reshape(-1, channels)
    half_blocks = (2 * n, sum(quarter_rows) + SUM_ROWS, channels)
    if geo["fits"]:
        head_own, head_other = kernel_call(
            functools.partial(head_grad_body, geo),
            [(half_blocks, BF)] * 2,
            (*head_lefts, head_sums, expand_sums, order),
            28,
            scalars=(8,),
            scratch=[
                pltpu.VMEM((2 * channels, channels), BF),
                pltpu.VMEM((hidden_units, channels), BF),
            ],
        )
    else:
        whole = kernel_call(
            functools.partial(head_grad_body, geo), [((4 * r * n, channels), BF) for r in quarter_rows],
            head_lefts, 48,
        )
        whole = [jnp.moveaxis(g.reshape(n, 2, 2, -1, channels), 2, 0) for g in whole]
        whole = [by_replica(g).reshape(4 * n, -1, channels) for g in whole]
        extra = jnp.concatenate([head_sums, expand_sums], axis=0).astype(BF)
        extra = jnp.pad(extra, ((0, SUM_ROWS - extra.shape[0]), (0, 0)))
        whole.append(jnp.broadcast_to(extra, (4 * n, *extra.shape)))
        head_own, head_other = jnp.split(jnp.concatenate(whole, axis=1), 2)
    (residual,) = kernel_call(
        residual_body, [((rows + 2 * HALO, channels), F32)], (d_res, token_info), 24
    )
    d_ups, head_own, head_other, residual = together(
        swap(as_payload(d_ups)), head_own, head_other, residual
    )
    core = (replica & 1).reshape(1)

    def slab_grads(payload, steps):
        part = (sum(slab) // 2 + SUM_ROWS, channels)
        return kernel_call(
            functools.partial(slab_grad_body, geo),
            [(part, BF)] * 2,
            (core, payload, steps),
            24,
            scalars=(0,),
            scratch=[pltpu.VMEM((2, *part), BF)],
        )

    def cut(x):
        at = x.shape[0] * 2 // 48 * 16
        return x[:at], x[at:]

    (partial,) = kernel_call(
        functools.partial(slab_in_body, geo), step_block, (d_ups, up_own), 24
    )
    up_mine, up_sent = slab_grads(d_ups, mixed_all)
    partial, up_got, head_got, up_mine = together(
        swap(partial), across(up_sent, "series", 1), across(head_other, "series", 1), up_mine
    )
    d_pair, d_iso = kernel_call(
        functools.partial(mix_back_body, geo),
        [(own_steps, F32), ((n, sum(m) + 8, channels), BF)],
        (partial, hidden_one, hidden_two, row(mix_gain)),
        8,
    )
    up_part = summed(up_mine, up_got)
    head_sum = summed(after(head_own, d_iso), head_got).reshape(n, 2, *half_blocks[1:])
    head_sum = lax.psum_scatter(head_sum, "tm", scatter_dimension=0)
    d_iso_all, up_got = together(swap(d_iso), across(up_part, "series", 2))
    (partial,) = kernel_call(
        functools.partial(iso_back_body, geo),
        step_block,
        (shifts, d_iso_all, *step_starts, *iso_wide),
        32,
        scalars=(0,),
    )
    part = (sum(iso_slab) // 2 + SUM_ROWS, channels)
    iso_mine, iso_sent = kernel_call(
        functools.partial(iso_grad_body, geo),
        [(part, BF)] * 2,
        (shifts, hidden_all, d_iso_all, *step_starts),
        32,
        scalars=(0,),
        scratch=[
            *(pltpu.VMEM((touched[b] * channels, channels), F32) for b in range(2)),
            pltpu.VMEM((2, *part), BF),
        ],
    )
    up_part = summed(up_part, up_got)
    partial, iso_got, up_got, iso_mine = together(
        swap(partial),
        across(iso_sent, "series", 1),
        across(up_part, "series", 1),
        iso_mine,
    )
    (d_conv,) = kernel_call(
        functools.partial(conv_back_body, geo), [((n, *own_steps), BF)], (partial, d_pair, hidden_one), 8
    )
    iso_part = summed(iso_mine, iso_got)

    def grads_of(part, got, sizes):
        return kernel_call(
            join_body,
            [((size, channels), F32) for size in (*sizes, 2 * SUM_ROWS)],
            (core, part, got),
            24,
            scalars=(0,),
        )

    ups = grads_of(after(up_part, d_conv), up_got, slab)
    d_conv_all, iso_a, *ups = together(
        swap(d_conv), across(cut(iso_part)[0], "series", 2), *ups
    )
    (d_windows,) = kernel_call(
        functools.partial(slab_out_body, geo), [(pay_shape, BF)], (d_conv_all, stride_own), 24
    )
    stride_mine, stride_sent = slab_grads(windows, d_conv_all)
    stride_part = summed(stride_mine, across(stride_sent, "series", 1))
    d_windows, iso_b, stride_a = together(
        swap(d_windows),
        across(cut(iso_part)[1], "series", 2),
        across(cut(stride_part)[0], "series", 2),
    )
    edge = ((HALO, channels), F32)
    own, to_left, to_right = kernel_call(
        functools.partial(input_back_body, geo),
        [((rows, channels), F32), edge, edge],
        (*as_taps(d_windows), *window_infos, residual),
        24,
    )
    iso_part = summed(after(iso_part, own), jnp.concatenate([iso_a, iso_b]))
    from_right, from_left, stride_b, iso_got, head_got = together(
        lax.ppermute(to_left, "tm", down_route),
        lax.ppermute(to_right, "tm", up_route),
        across(cut(stride_part)[1], "series", 2),
        across(iso_part, "series", 1),
        across(head_sum[1], "series", 2),
    )
    input_grad = jnp.concatenate(
        [own[:HALO] + from_left, own[HALO : rows - HALO], own[rows - HALO :] + from_right], axis=0
    ).astype(BF)
    stride_part = summed(stride_part, jnp.concatenate([stride_a, stride_b]))
    stride_got = across(stride_part, "series", 1)
    head_mine = summed(head_sum[0], head_got)
    at = sum(quarter_rows)
    head_y = across(head_mine[:at], "series", 2)
    head_y = jnp.where(
        bit_of("series", 2) == 0, jnp.stack([head_mine[:at], head_y]), jnp.stack([head_y, head_mine[:at]])
    )
    head_got = across(head_y, "series", 1)
    head_grad = jnp.where(
        bit_of("series", 1) == 0, jnp.stack([head_y, head_got], axis=1), jnp.stack([head_got, head_y], axis=1)
    )
    head_grad = head_grad.reshape(4, *head_grad.shape[2:]).astype(F32)
    head_grads = [
        g.reshape(-1, channels)
        for g in jnp.split(head_grad, [quarter_rows[0], sum(quarter_rows[:2])], axis=1)
    ]
    sums = head_mine[at:].astype(F32)
    count = expand_bias.shape[0] // channels
    expand_grad = sums[10 : 10 + count].reshape(-1)

    strides = grads_of(stride_part, stride_got, slab)
    isos = grads_of(iso_part, iso_got, iso_slab)
    return (
        result[None],
        input_grad[None],
        strides[0], strides[2][0], isos[0], isos[2][0], ups[0], sums[8],
        strides[1], strides[2][1], isos[1], isos[2][1], ups[1], sums[9],
        isos[2][2] + sums[6], isos[2][3] + sums[7],
        head_grads[0], sums[5], sums[3], sums[4],
        head_grads[1], expand_grad, head_grads[2], sums[2], sums[0], sums[1],
    )


def solution(mesh):
    tokens, weight, whole = P("series", "tm", None), P("tm", None), P()
    pair = (weight, whole)
    return jax.shard_map(
        on_device,
        mesh=mesh,
        in_specs=(
            tokens, P("series", None), *(pair * 6), whole, whole, *pair, whole, whole, *pair, *pair, whole, whole,
            tokens,
        ),
        out_specs=(tokens, tokens, *(pair * 6), whole, whole, *pair, whole, whole, *pair, *pair, whole, whole),
        check_vma=False,
    )
```

```python
import functools
import math

import jax
import jax.numpy as jnp
from jax import lax
from jax.experimental import pallas as pl
from jax.experimental.pallas import tpu as pltpu
from jax.sharding import PartitionSpec as P

SCALES = (12, 16)
AVERAGES = (13, 17)
TAPS = (16, 12)
UNIT = 48
EPSILON = 1e-05
HALO = 16
FFN_CHUNK = 512
SUM_ROWS = 16

BF = jnp.bfloat16
F32 = jnp.float32
I32 = jnp.int32


def dot(left, right):
    return lax.dot_general(left, right, (((1,), (0,)), ((), ())), preferred_element_type=F32)


def dot_nt(left, right):
    return lax.dot_general(left, right, (((1,), (1,)), ((), ())), preferred_element_type=F32)


def dot_tn(left, right):
    return lax.dot_general(left, right, (((0,), (0,)), ((), ())), preferred_element_type=F32)


def kernel_call(body, outs, args, mib, scalars=(), scratch=()):
    specs = [
        pl.BlockSpec(memory_space=pltpu.SMEM if i in scalars else pltpu.VMEM)
        for i in range(len(args))
    ]
    return pl.pallas_call(
        body,
        out_shape=[jax.ShapeDtypeStruct(shape, dtype) for shape, dtype in outs],
        in_specs=specs,
        out_specs=[pl.BlockSpec(memory_space=pltpu.VMEM) for _ in outs],
        scratch_shapes=list(scratch),
        compiler_params=pltpu.CompilerParams(vmem_limit_bytes=mib << 20),
    )(*args)


def tap_to_payload(x, scale, q, n):
    rows, channels = x.shape
    m, h = rows // scale, channels // q
    parts = [x[:, c * q : (c + 1) * q].reshape(scale, 1, m, q) for c in range(h)]
    whole = parts[0] if h == 1 else jnp.concatenate(parts, axis=1)
    return whole.reshape(n, scale * h * m // n, q)


def payload_to_tap(p, scale, channels):
    n, rows, q = p.shape
    h = channels // q
    m = n * rows // (scale * h)
    p = p.reshape(scale, h, m, q)
    parts = [p[:, c].reshape(scale * m, q) for c in range(h)]
    return parts[0] if h == 1 else jnp.concatenate(parts, axis=1)


def payload_units(p, m):
    n, rows, q = p.shape
    p = p.reshape(n, rows // m, m, q)
    return [p[:, i].reshape(n * m, q).astype(BF) for i in range(rows // m)]


def units_to_payload(units, n):
    parts = [u.reshape(n, u.shape[0] // n, u.shape[1]) for u in units]
    return parts[0] if len(parts) == 1 else jnp.concatenate(parts, axis=1)


def split_steps(ref, counts):
    whole = ref[...].astype(F32)
    n, _, channels = whole.shape
    first = whole[:, : counts[0], :].reshape(n * counts[0], channels)
    return [first, whole[:, counts[0] : sum(counts), :].reshape(n * counts[1], channels)]


def join_steps(parts, n):
    return jnp.concatenate([p.reshape(n, p.shape[0] // n, p.shape[1]) for p in parts], axis=1)


def norm_stats(v):
    mean = jnp.mean(v, axis=-1, keepdims=True)
    centered = v - mean
    rstd = lax.rsqrt(jnp.mean(centered * centered, axis=-1, keepdims=True) + EPSILON)
    return centered * rstd, rstd


def norm_back(d, gain, xhat, rstd):
    dg = d * gain
    mean_d = jnp.mean(dg, axis=-1, keepdims=True)
    mean_dx = jnp.mean(dg * xhat, axis=-1, keepdims=True)
    return rstd * (dg - mean_d - xhat * mean_dx)


def column_sum(v):
    return jnp.sum(v, axis=0, keepdims=True)


def average_counts(info, kernel, columns):
    place, first, last = info[:, 0:1], info[:, 1:2], info[:, 2:3]
    reach = kernel // 2
    column = lax.broadcasted_iota(I32, (info.shape[0], columns), 1)
    away = column - place
    inside = (jnp.abs(away) <= reach) & (column >= first) & (column <= last)
    counts = jnp.where(inside, 1, 0)
    counts = counts + jnp.where(column == first, jnp.maximum(reach - (place - first), 0), 0)
    counts = counts + jnp.where(column == last, jnp.maximum(reach - (last - place), 0), 0)
    return counts, away == 0


def season_matrix(info, kernel, columns):
    counts, own = average_counts(info, kernel, columns)
    values = jnp.where(own, kernel, 0) - counts
    values = jnp.where(info[:, 0:1] >= info[:, 1:2], values, 0)
    return values.astype(F32).astype(BF)


def token_order(rows, scale):
    m = rows // scale
    place = lax.broadcasted_iota(I32, (rows, rows), 0)
    column = lax.broadcasted_iota(I32, (rows, rows), 1)
    tap = jnp.zeros_like(column)
    for k in range(1, scale):
        tap = tap + jnp.where(column >= k * m, 1, 0)
    return jnp.where(place == scale * (column - tap * m) + tap, 1.0, 0.0).astype(BF)


def join_payload(geo, taps):
    return jnp.concatenate(
        [tap_to_payload(t, SCALES[b], geo["q"], geo["n"]) for b, t in enumerate(taps)], axis=1
    )


def split_payload(geo, payload, channels):
    low = geo["pay_rows"][0]
    parts = (payload[:, :low], payload[:, low:])
    return [payload_to_tap(p, SCALES[b], channels) for b, p in enumerate(parts)]


def store_taps(geo, outs, taps):
    if not geo["aligned"]:
        for out, tap in zip(outs, taps):
            out[...] = tap.astype(BF)
        return
    outs[0][...] = join_payload(geo, taps).astype(BF)


def load_taps(geo, pays, channels):
    if not geo["aligned"]:
        return [p[...] for p in pays]
    whole = pays[0][...].astype(F32)
    return [t.astype(BF) for t in split_payload(geo, whole, channels)]


def windows_body(geo, tok, left, right, info_one, info_two, *outs):
    x = jnp.concatenate([left[...], tok[...], right[...]], axis=0)
    parts = []
    for b, info in enumerate((info_one, info_two)):
        matrix = season_matrix(info[...], AVERAGES[b], x.shape[0])
        parts.append(dot(matrix, x) * (1.0 / AVERAGES[b]))
    store_taps(geo, outs, parts)


def season_body(tok, left, right, info, out):
    x = jnp.concatenate([left[...], tok[...], right[...]], axis=0)
    wide = tok[...].astype(F32)
    for b in range(2):
        counts, _ = average_counts(info[...], AVERAGES[b], x.shape[0])
        out[b] = wide - dot(counts.astype(F32).astype(BF), x) * (1.0 / AVERAGES[b])


def slab_starts(geo):
    return (0, geo["slab"][0])


def units_against(geo, payload, weight, totals):
    low = geo["pay_rows"][0]
    for b, p in enumerate((payload[:, :low], payload[:, low:])):
        q, start = geo["q"], slab_starts(geo)[b]
        for i, unit in enumerate(payload_units(p, geo["m"][b])):
            term = dot(unit, weight[start + i * q : start + (i + 1) * q, :])
            totals[b] = term if totals[b] is None else totals[b] + term


def slab_in_body(geo, payload, weight, out):
    totals = [None, None]
    units_against(geo, payload[...].astype(F32), weight, totals)
    out[...] = join_steps(totals, geo["n"]).astype(BF)


def steps_against(geo, lows, weight, n):
    q = geo["q"]
    parts = []
    for b, low in enumerate(lows):
        start = slab_starts(geo)[b]
        units = [
            dot_nt(low, weight[start + i * q : start + (i + 1) * q, :])
            for i in range(geo["slab"][b] // q)
        ]
        parts.append(units_to_payload(units, n))
    return jnp.concatenate(parts, axis=1).astype(BF)


def slab_out_body(geo, steps, own, out):
    lows = [x.astype(BF) for x in split_steps(steps, geo["m"])]
    out[...] = steps_against(geo, lows, own, geo["n"])


def store_halved(out, start, size, at, value):
    step = math.gcd(value.shape[0], size // 2)
    for i in range(0, value.shape[0], step):
        h, r = divmod(at + i, size // 2)
        out[h, start + r : start + r + step, :] = value[i : i + step].astype(BF)


def store_core_parts(core, halves, rows, own, sent):
    blank = jnp.zeros((SUM_ROWS - len(rows), halves.shape[2]), F32)
    halves[0, halves.shape[1] - SUM_ROWS :, :] = jnp.concatenate([*rows, blank], axis=0).astype(BF)
    halves[1, halves.shape[1] - SUM_ROWS :, :] = jnp.zeros((SUM_ROWS, halves.shape[2]), BF)
    own[...] = halves[core]
    sent[...] = halves[1 - core]


def slab_grad_body(geo, core, payload, steps, own, sent, halves):
    low, q, slab = geo["pay_rows"][0], geo["q"], geo["slab"]
    rights = split_steps(steps, geo["m"])
    wide = payload[...].astype(F32)
    for b in range(2):
        right = rights[b].astype(BF)
        part = wide[:, :low] if b == 0 else wide[:, low:]
        for i, unit in enumerate(payload_units(part, geo["m"][b])):
            store_halved(halves, slab_starts(geo)[b] // 2, slab[b], i * q, dot_tn(unit, right))
    store_core_parts(core[0], halves, [column_sum(r) for r in rights], own, sent)


def join_body(core, part, got, out_one, out_two, sums):
    at = 0
    for out in (out_one, out_two, sums):
        rows = out.shape[0] // 2
        for which, value in ((core[0], part), (1 - core[0], got)):
            begin = pl.multiple_of(which * rows, math.gcd(rows, 512))
            out[pl.ds(begin, rows), :] = value[at : at + rows, :].astype(F32)
        at += rows


def tap_inputs(geo, b, shifts, hidden, start):
    count = hidden.shape[0]
    step = lax.broadcasted_iota(I32, (count, 1), 0)
    pieces = []
    for i in range(geo["touched"][b]):
        shift = jnp.maximum(shifts[b] - i, 0)
        moved = pltpu.roll(hidden, shift, 0)
        pieces.append(jnp.where(step - shift >= start, moved, 0.0).astype(BF))
    return pieces


def iso_body(geo, shifts, steps, start_one, start_two, weight_one, weight_two, out):
    parts = []
    hiddens = split_steps(steps, geo["m"])
    for b, (start, weight) in enumerate(((start_one, weight_one), (start_two, weight_two))):
        total = None
        channels = hiddens[b].shape[1]
        for i, piece in enumerate(tap_inputs(geo, b, shifts, hiddens[b], start[...])):
            term = dot(piece, weight[i * channels : (i + 1) * channels, :])
            total = term if total is None else total + term
        parts.append(total)
    out[...] = join_steps(parts, geo["n"]).astype(BF)


def iso_back_body(geo, shifts, d_iso, start_one, start_two, weight_one, weight_two, out):
    parts = []
    for b, (d, start, weight) in enumerate(
        zip(split_steps(d_iso, geo["m"]), (start_one, start_two), (weight_one, weight_two))
    ):
        count, channels = d.shape
        low = d.astype(BF)
        step = lax.broadcasted_iota(I32, (count, 1), 0)
        total = None
        for i in range(geo["touched"][b]):
            shift = jnp.maximum(shifts[b] - i, 0)
            stacked = dot_nt(low, weight[i * channels : (i + 1) * channels, :])
            stacked = jnp.where(step - shift >= start[...], stacked, 0.0)
            moved = pltpu.roll(stacked, lax.rem(count - shift, count), 0)
            total = moved if total is None else total + moved
        parts.append(total)
    out[...] = join_steps(parts, geo["n"]).astype(BF)


def iso_grad_body(geo, shifts, steps, d_iso, start_one, start_two, own, sent, wide_one, wide_two, halves):
    hiddens, ds = split_steps(steps, geo["m"]), split_steps(d_iso, geo["m"])
    begin = 0
    for b, (start, wide) in enumerate(((start_one, wide_one), (start_two, wide_two))):
        channels = hiddens[b].shape[1]
        right = ds[b].astype(BF)
        for i, piece in enumerate(tap_inputs(geo, b, shifts, hiddens[b], start[...])):
            wide[i * channels : (i + 1) * channels, :] = dot_tn(piece, right)
        part = geo["iso_slab"][b] // 2
        for h in range(2):
            at = pl.multiple_of(shifts[2 + b] + h * part, math.gcd(geo["iso_q"][b], part))
            halves[h, begin : begin + part, :] = wide[pl.ds(at, part), :].astype(BF)
        begin += part
    at = sum(geo["m"])
    norm_sums = jnp.sum(d_iso[:, at:, :].astype(F32), axis=0)
    rows = [*(column_sum(d) for d in ds), norm_sums[0:1], norm_sums[1:2]]
    store_core_parts(shifts[4], halves, rows, own, sent)


def branch_rows(pair, counts):
    total = sum(counts)
    step = lax.broadcasted_iota(I32, (total, 1), 0)
    return jnp.where(step < counts[0], pair[0:1, :], pair[1:2, :])


def hidden_one_body(geo, parts, bias, hidden, low):
    value = jnp.tanh(jnp.sum(parts[...].astype(F32), axis=0) + branch_rows(bias, geo["m"]))
    hidden[...] = value
    low[...] = jnp.broadcast_to(value.astype(BF)[None], low.shape)


def mix_body(geo, parts, bias, hidden_one, gain, shift, hidden, mixed):
    value = jnp.tanh(jnp.sum(parts[...].astype(F32), axis=0) + branch_rows(bias, geo["m"]))
    hidden[...] = value
    xhat, _ = norm_stats(value + hidden_one[...])
    low = (xhat * gain[...] + shift[...]).astype(BF)
    mixed[...] = jnp.broadcast_to(low[None], mixed.shape)


def mix_back_body(geo, parts, hidden_one, hidden_two, gain, d_pair, d_iso):
    d = jnp.sum(parts[...].astype(F32), axis=0)
    two = hidden_two[...]
    xhat, rstd = norm_stats(two + hidden_one[...])
    pair = norm_back(d, gain[...], xhat, rstd)
    iso = (1.0 - two * two) * pair
    d_pair[...] = pair
    blank = jnp.zeros((d_iso.shape[1] - iso.shape[0] - 2, iso.shape[1]), F32)
    low = jnp.concatenate([iso, column_sum(d * xhat), column_sum(d), blank], axis=0).astype(BF)
    d_iso[...] = jnp.broadcast_to(low[None], d_iso.shape)


def conv_back_body(geo, parts, d_pair, hidden_one, d_conv):
    one = hidden_one[...]
    d = (jnp.sum(parts[...].astype(F32), axis=0) + d_pair[...]) * (1.0 - one * one)
    d_conv[...] = jnp.broadcast_to(d.astype(BF)[None], d_conv.shape)


def place_head(geo, order, pieces, merge, expand, project):
    m_rows, h_rows = geo["quarter_rows"][:2]
    block = 0
    for piece in pieces:
        for i in range(piece.shape[0]):
            at = pl.multiple_of(order[block] * m_rows, m_rows)
            merge[pl.ds(at, m_rows), :] = piece[i, :m_rows, :]
            at = pl.ds(pl.multiple_of(order[block] * h_rows, h_rows), h_rows)
            expand[at, :] = piece[i, m_rows : m_rows + h_rows, :]
            project[at, :] = piece[i, m_rows + h_rows :, :]
            block += 1


def head_body(geo, *refs):
    taps = geo["taps"]
    pays, refs = refs[:taps], refs[taps:]
    (
        season, cotangent, up_bias, mix_gain, mix_shift, merge_bias, feed_gain, feed_shift,
        expand_bias, project_bias, final_gain, final_shift,
    ) = refs[:12]
    refs = refs[12:]
    grads = 2 if geo["fits"] else 3
    if geo["fits"]:
        places, pieces, refs = refs[0], refs[1 : 1 + geo["pieces"]], refs[1 + geo["pieces"] :]
        merge_weight, expand_weight, project_weight = refs[-3:]
        refs = refs[:-3]
        place_head(geo, places, pieces, merge_weight, expand_weight, project_weight)
    else:
        (merge_weight, expand_weight, project_weight), refs = refs[:3], refs[3:]
    d_pays, (result, d_res_out, sums), refs = refs[:taps], refs[taps : taps + 3], refs[taps + 3 :]
    grad_outs, refs = refs[:grads], refs[grads:]
    slope, merge_in, normed_out, activ_out, d_sum_out, d_pre_out, d_merged_out = refs
    hidden_units = expand_weight.shape[0]
    rows, channels = cotangent.shape
    width = FFN_CHUNK
    chunks = expand_weight.shape[0] // width
    taps = load_taps(geo, pays, channels)
    ups, kept = [], []
    for b in range(2):
        order = token_order(rows, SCALES[b])
        up = jnp.tanh(dot(order, taps[b]) + up_bias[b : b + 1, :])
        xhat, rstd = norm_stats(up + season[b])
        ups.append(up)
        kept.append((xhat, rstd))
        merge_in[:, b * channels : (b + 1) * channels] = (
            xhat * mix_gain[...] + mix_shift[...]
        ).astype(BF)
    merged = dot(merge_in[...], merge_weight[...]) + merge_bias[...]
    feed_hat, feed_rstd = norm_stats(merged)
    normed_out[...] = (feed_hat * feed_gain[...] + feed_shift[...]).astype(BF)

    def forward_chunk(c, total):
        at = pl.ds(pl.multiple_of(c * width, width), width)
        pre = dot_nt(normed_out[...], expand_weight[at, :]) + expand_bias[:, at]
        half = 0.5 + 0.5 * lax.erf(pre * math.sqrt(0.5))
        slope[c] = half + pre * (jnp.exp(-0.5 * pre * pre) * (1.0 / math.sqrt(2.0 * math.pi)))
        activ_out[:, at] = (pre * half).astype(BF)
        return total + dot(activ_out[:, at], project_weight[at, :])

    summed = lax.fori_loop(0, chunks, forward_chunk, merged + project_bias[...])
    final_hat, final_rstd = norm_stats(summed)
    result[...] = (final_hat * final_gain[...] + final_shift[...]).astype(BF)

    d_out = cotangent[...].astype(F32)
    sums[0:1, :] = column_sum(d_out * final_hat)
    sums[1:2, :] = column_sum(d_out)
    d_sum = norm_back(d_out, final_gain[...], final_hat, final_rstd)
    sums[2:3, :] = column_sum(d_sum)
    d_sum_out[...] = d_sum.astype(BF)

    def backward_chunk(c, total):
        at = pl.ds(pl.multiple_of(c * width, width), width)
        d_pre = slope[c] * dot_nt(d_sum_out[...], project_weight[at, :])
        sums[pl.ds(10 + c, 1), :] = column_sum(d_pre)
        d_pre_out[:, at] = d_pre.astype(BF)
        return total + dot(d_pre_out[:, at], expand_weight[at, :])

    d_normed = lax.fori_loop(0, chunks, backward_chunk, jnp.zeros((rows, channels), F32))
    sums[3:4, :] = column_sum(d_normed * feed_hat)
    sums[4:5, :] = column_sum(d_normed)
    d_merged = d_sum + norm_back(d_normed, feed_gain[...], feed_hat, feed_rstd)
    sums[5:6, :] = column_sum(d_merged)
    d_merged_out[...] = d_merged.astype(BF)
    gain_sum, shift_sum = 0.0, 0.0
    d_taps = []
    for b in range(2):
        d = dot_nt(d_merged_out[...], merge_weight[b * channels : (b + 1) * channels, :])
        xhat, rstd = kept[b]
        gain_sum = gain_sum + column_sum(d * xhat)
        shift_sum = shift_sum + column_sum(d)
        d_res = norm_back(d, mix_gain[...], xhat, rstd)
        d_res_out[b] = d_res
        d_up = (1.0 - ups[b] * ups[b]) * d_res
        sums[8 + b : 9 + b, :] = column_sum(d_up)
        d_taps.append(dot_tn(token_order(rows, SCALES[b]), d_up.astype(BF)))
    sums[6:7, :] = gain_sum
    sums[7:8, :] = shift_sum
    store_taps(geo, d_pays, d_taps)

    count = 10 + chunks
    sums[count:, :] = jnp.zeros((SUM_ROWS - count, channels), F32)
    pairs = ((merge_in, d_merged_out), (d_pre_out, normed_out), (activ_out, d_sum_out))
    if not geo["fits"]:
        for out, (left, right) in zip(grad_outs, pairs):
            out[...] = dot_tn(left[...], right[...]).astype(BF)
        return
    start = 0
    for (left, right), grad, size in zip(
        pairs, (merge_weight, expand_weight, project_weight), geo["quarter_rows"]
    ):
        grad[...] = dot_tn(left[...], right[...]).astype(BF)
        for h, out in enumerate(grad_outs):
            blocks = out.shape[0]
            for i in range(blocks):
                begin = pl.multiple_of(places[h * blocks + i] * size, size)
                out[i, start : start + size, :] = grad[pl.ds(begin, size), :]
        start += size
    low = sums[...].astype(BF)
    for out in grad_outs:
        out[:, start:, :] = jnp.broadcast_to(low, (out.shape[0], *low.shape))


def residual_body(d_res, info, out):
    rows = d_res.shape[1]
    columns = rows + 2 * HALO
    total = jnp.zeros((columns, d_res.shape[2]), F32)
    for b in range(2):
        counts, _ = average_counts(info[...], AVERAGES[b], columns)
        adjoint = dot_tn(counts.astype(F32).astype(BF), d_res[b].astype(BF))
        total = total - adjoint * (1.0 / AVERAGES[b])
    out[0:HALO, :] = total[0:HALO]
    out[HALO : HALO + rows, :] = total[HALO : HALO + rows] + d_res[0] + d_res[1]
    out[HALO + rows :, :] = total[HALO + rows :]


def input_back_body(geo, *refs):
    pays = refs[: geo["taps"]]
    info_one, info_two, residual, own, left, right = refs[geo["taps"] :]
    columns, channels = residual.shape
    rows = columns - 2 * HALO
    taps = load_taps(geo, pays, channels)
    total = residual[...]
    for b, info in enumerate((info_one, info_two)):
        matrix = season_matrix(info[...], AVERAGES[b], columns)
        total = total + dot_tn(matrix, taps[b]) * (1.0 / AVERAGES[b])
    left[...] = total[0:HALO]
    own[...] = total[HALO : HALO + rows]
    right[...] = total[HALO + rows :]


def swap(x):
    return lax.all_to_all(x, "tm", 0, 0)


def together(*values):
    return lax.optimization_barrier(values)


def after(x, dep):
    return lax.optimization_barrier((x, dep))[0]


def across(x, axis, bit):
    return lax.ppermute(x, axis, [(i, i ^ bit) for i in range(lax.axis_size(axis))])


def bit_of(axis, bit):
    return (lax.axis_index(axis) & bit) // bit


def tm_bits():
    return [1 << i for i in range(lax.axis_size("tm").bit_length() - 1)]


def flipped(x):
    bits = [("series", 1), ("series", 2)] + [("tm", b) for b in tm_bits()]
    for at, (axis, bit) in enumerate(bits):
        x = jnp.where(bit_of(axis, bit) == 1, jnp.flip(x, at), x)
    return x


def natural_rows(x):
    bits = len(tm_bits())
    x = flipped(x.reshape([2] * (bits + 2) + list(x.shape[1:])))
    x = jnp.transpose(x, [*range(bits + 1, 1, -1), 1, 0, bits + 2, bits + 3])
    return x.reshape(-1, x.shape[-1])


def relative_blocks(x):
    bits = len(tm_bits())
    x = x.reshape([2] * (bits + 2) + [x.shape[0] >> (bits + 2), x.shape[1]])
    x = jnp.transpose(x, [bits + 1, bits, *range(bits - 1, -1, -1), bits + 2, bits + 3])
    return flipped(x).reshape(-1, *x.shape[-2:])


def summed(*parts):
    return sum(p.astype(F32) for p in parts).astype(BF)


def neighbours(n):
    up = [(i, i + 1) for i in range(n - 1)]
    return up, [(j, i) for i, j in up]


def on_device(
    inputs, lengths,
    stride_weight_twelve, stride_bias_twelve, isometric_weight_twelve, isometric_bias_twelve,
    upsample_weight_twelve, upsample_bias_twelve,
    stride_weight_sixteen, stride_bias_sixteen, isometric_weight_sixteen, isometric_bias_sixteen,
    upsample_weight_sixteen, upsample_bias_sixteen,
    mix_gain, mix_shift, merge_weight, merge_bias, feed_gain, feed_shift,
    expand_weight, expand_bias, project_weight, project_bias, final_gain, final_shift, cotangent,
):
    n = lax.axis_size("tm")
    me = lax.axis_index("tm")
    rows, channels = inputs.shape[1:]
    stride_weights = (stride_weight_twelve, stride_weight_sixteen)
    iso_weights = (isometric_weight_twelve, isometric_weight_sixteen)
    up_weights = (upsample_weight_twelve, upsample_weight_sixteen)
    m = [rows // s for s in SCALES]
    slab = [w.shape[0] for w in stride_weights]
    q = math.gcd(*slab, channels)
    pay_rows = [slab[b] // q * m[b] for b in range(2)]
    iso_slab = [w.shape[0] for w in iso_weights]
    iso_q = [math.gcd(r, channels) for r in iso_slab]
    touched = [-(-(iso_slab[b] + channels - iso_q[b]) // channels) for b in range(2)]
    half = n // 2
    geo = {
        "n": n, "half": half, "m": m, "q": q, "slab": slab, "pay_rows": pay_rows, "touched": touched,
        "iso_slab": iso_slab, "iso_q": iso_q,
        "aligned": q % 128 == 0,
    }
    geo["taps"] = 1 if geo["aligned"] else 2
    pay_shape = (n, sum(pay_rows), q)
    pay_outs = [(pay_shape, BF)] if geo["aligned"] else [((rows, channels), BF)] * 2

    def as_payload(parts):
        return parts[0] if geo["aligned"] else join_payload(geo, parts)

    def as_taps(payload):
        return [payload] if geo["aligned"] else split_payload(geo, payload, channels)

    def row(v):
        return v[None, :]

    lengths_row = lengths[0]
    count = lengths_row.shape[0]
    upto = jnp.arange(count)[None, :] <= jnp.arange(count)[:, None]
    ends = UNIT * jnp.sum(jnp.where(upto, lengths_row[None, :], 0), axis=1)
    starts = ends - UNIT * lengths_row

    def bounds(places):
        inside = (starts[None, :] <= places[:, None]) & (places[:, None] < ends[None, :])
        first = jnp.sum(jnp.where(inside, starts[None, :], 0), axis=1)
        return first, jnp.sum(jnp.where(inside, ends[None, :], 0), axis=1)

    base = me * rows
    local = jnp.arange(rows, dtype=I32)

    def info_of(places, anchors):
        first, last = bounds(anchors + base)
        shift = base - HALO
        return jnp.stack([places + HALO, first - shift, last - 1 - shift], axis=1)

    token_info = info_of(local, local)
    window_infos, step_starts = [], []
    for b in range(2):
        tap, step = local // m[b], local % m[b]
        anchor = SCALES[b] * step
        window_infos.append(info_of(anchor - SCALES[b] // 2 + tap, anchor))
        all_steps = jnp.arange(n * m[b], dtype=I32)
        step_starts.append((bounds(SCALES[b] * all_steps)[0] // SCALES[b])[:, None])

    replica = lax.axis_index("series")

    head_weights = (merge_weight, expand_weight, project_weight)
    head_rows = [w.shape[0] for w in head_weights]
    quarter_rows = [r // 4 for r in head_rows]
    geo["quarter_rows"] = quarter_rows
    geo["fits"] = all(r % 16 == 0 for r in quarter_rows)
    quarter = jnp.concatenate(
        [lax.dynamic_slice_in_dim(w, replica * r, r) for w, r in zip(head_weights, quarter_rows)], axis=0
    )
    stride_own = jnp.concatenate(stride_weights, axis=0)
    up_own = jnp.concatenate(up_weights, axis=0)

    far, bit = [0], half
    while bit > 1:
        far, bit = far + [o ^ bit for o in far], bit // 2
    near = [o ^ 1 for o in far]
    half_order = [(o, r) for r in (0, 2) for o in far + near]
    relative = half_order + [(o, r ^ 1) for o, r in half_order]
    order = jnp.stack([(me ^ o) * 4 + (replica ^ r) for o, r in relative]).astype(I32)

    iso_first = [(iso_slab[b] * me) // channels for b in range(2)]
    iso_offset = [iso_slab[b] * me - iso_first[b] * channels for b in range(2)]
    iso_wide = []
    for b in range(2):
        if touched[b] * channels == iso_slab[b]:
            iso_wide.append(iso_weights[b])
        else:
            blank = jnp.zeros((touched[b] * channels, channels), BF)
            iso_wide.append(lax.dynamic_update_slice(blank, iso_weights[b], (iso_offset[b], 0)))
    shifts = jnp.stack([*(TAPS[b] - 1 - iso_first[b] for b in range(2)), *iso_offset, replica & 1]).astype(I32)

    up_route, down_route = neighbours(n)
    tokens = inputs[0]
    step_block = [((n, sum(m), channels), BF)]
    own_steps = (sum(m), channels)
    blocks = quarter[None]
    left, right, got = together(
        lax.ppermute(tokens[rows - HALO :], "tm", up_route),
        lax.ppermute(tokens[:HALO], "tm", down_route),
        across(blocks, "tm", half),
    )
    blocks, bit = jnp.concatenate([blocks, got]), half // 2
    while bit > 2:
        blocks, bit = jnp.concatenate([blocks, across(blocks, "tm", bit)]), bit // 2
    windows = kernel_call(
        functools.partial(windows_body, geo), pay_outs, (tokens, left, right, *window_infos), 24
    )
    windows, got = together(swap(as_payload(windows)), across(blocks, "tm", bit))
    blocks = jnp.concatenate([blocks, got])
    middle = blocks.shape[0] // 2
    (partial,) = kernel_call(
        functools.partial(slab_in_body, geo), step_block, (windows, stride_own), 24
    )
    low_blocks, high_blocks = blocks[:middle], blocks[middle:]
    partial, x_low, y_high = together(
        swap(partial), across(low_blocks, "tm", 1), across(high_blocks, "series", 2)
    )
    hidden_one, hidden_low = kernel_call(
        functools.partial(hidden_one_body, geo),
        [(own_steps, F32), ((n, *own_steps), BF)],
        (partial, jnp.stack([stride_bias_twelve, stride_bias_sixteen])),
        8,
    )
    hidden_all, x_high, y_low, blocks_core = together(
        swap(hidden_low),
        across(high_blocks, "tm", 1),
        across(low_blocks, "series", 2),
        across(blocks, "series", 1),
    )
    (partial,) = kernel_call(
        functools.partial(iso_body, geo),
        step_block,
        (shifts, hidden_all, *step_starts, *iso_wide),
        32,
        scalars=(0,),
    )
    first = (x_low, x_high, y_low, y_high)
    partial, blocks_a, blocks_b, *core_first = together(
        swap(partial),
        across(x_low, "series", 2),
        across(y_high, "tm", 1),
        *(across(f, "series", 1) for f in first),
    )
    hidden_two, mixed_low = kernel_call(
        functools.partial(mix_body, geo),
        [(own_steps, F32), ((n, *own_steps), BF)],
        (
            partial,
            jnp.stack([isometric_bias_twelve, isometric_bias_sixteen]),
            hidden_one,
            row(mix_gain),
            row(mix_shift),
        ),
        8,
    )
    (season,) = kernel_call(
        season_body, [((2, rows, channels), F32)], (tokens, left, right, token_info), 24
    )
    mixed_all, season, core_a, core_b = together(
        swap(mixed_low), season, across(blocks_a, "series", 1), across(blocks_b, "series", 1)
    )
    (ups,) = kernel_call(
        functools.partial(slab_out_body, geo), [(pay_shape, BF)], (mixed_all, up_own), 24
    )
    ups = swap(ups)
    head_pieces = [
        blocks, *first, blocks_a, blocks_b, blocks_core, *core_first, core_a, core_b,
    ]
    geo["pieces"] = len(head_pieces)
    hidden_units = 4 * n * quarter_rows[1]
    head_args = [
        *as_taps(ups), season, cotangent[0], jnp.stack([upsample_bias_twelve, upsample_bias_sixteen]),
        row(mix_gain), row(mix_shift), row(merge_bias), row(feed_gain), row(feed_shift),
        row(expand_bias), row(project_bias), row(final_gain), row(final_shift),
    ]
    head_scratch = [
        pltpu.VMEM((hidden_units // FFN_CHUNK, rows, FFN_CHUNK), F32),
        *(
            pltpu.VMEM((rows, width), BF)
            for width in (2 * channels, channels, hidden_units, channels, hidden_units, channels)
        ),
    ]
    scalars = ()
    if geo["fits"]:
        scalars = (len(head_args),)
        head_args += [order, *head_pieces]
        head_scratch += [pltpu.VMEM((2 * channels, channels), BF)]
        head_scratch += [pltpu.VMEM((hidden_units, channels), BF)] * 2
    else:
        cuts = [quarter_rows[0], sum(quarter_rows[:2])]
        head_args += [natural_rows(w) for w in jnp.split(jnp.concatenate(head_pieces), cuts, axis=1)]
    half_blocks = (2 * n, sum(quarter_rows) + SUM_ROWS, channels)
    head = kernel_call(
        functools.partial(head_body, geo),
        [
            *pay_outs,
            ((rows, channels), BF),
            ((2, rows, channels), F32),
            ((SUM_ROWS, channels), F32),
            *(
                [(half_blocks, BF)] * 2
                if geo["fits"]
                else [((4 * r * n, channels), BF) for r in quarter_rows]
            ),
        ],
        head_args,
        60,
        scalars=scalars,
        scratch=head_scratch,
    )
    d_ups, (result, d_res, head_sums, *head_grads) = head[: geo["taps"]], head[geo["taps"] :]

    if geo["fits"]:
        head_own, head_other = head_grads
    else:
        whole = [relative_blocks(g) for g in head_grads]
        whole.append(jnp.broadcast_to(head_sums.astype(BF), (4 * n, *head_sums.shape)))
        head_own, head_other = jnp.split(jnp.concatenate(whole, axis=1), 2)
    (residual,) = kernel_call(
        residual_body, [((rows + 2 * HALO, channels), F32)], (d_res, token_info), 24
    )
    head_sum = summed(head_own, across(head_other, "series", 1))
    d_ups, head_sum, residual = together(swap(as_payload(d_ups)), head_sum, residual)
    head_sum = head_sum.reshape(2, 2, 2, len(far) // 2, *half_blocks[1:])
    core = (replica & 1).reshape(1)

    def slab_grads(payload, steps):
        part = (sum(slab) // 2 + SUM_ROWS, channels)
        return kernel_call(
            functools.partial(slab_grad_body, geo),
            [(part, BF)] * 2,
            (core, payload, steps),
            24,
            scalars=(0,),
            scratch=[pltpu.VMEM((2, *part), BF)],
        )

    def cut(x, thirds=2):
        at = x.shape[0] * thirds // 48 * 16
        return x[:at], x[at:]

    (partial,) = kernel_call(
        functools.partial(slab_in_body, geo), step_block, (d_ups, up_own), 24
    )
    up_mine, up_sent = slab_grads(d_ups, mixed_all)
    partial, x_1, y_1, up_mine, up_sent = together(
        swap(partial),
        across(head_sum[1, 1, 0], "tm", 1),
        across(head_sum[1, 1, 1], "series", 2),
        up_mine,
        up_sent,
    )
    d_pair, d_iso = kernel_call(
        functools.partial(mix_back_body, geo),
        [(own_steps, F32), ((n, sum(m) + 8, channels), BF)],
        (partial, hidden_one, hidden_two, row(mix_gain)),
        8,
    )
    up_part = summed(up_mine, across(up_sent, "series", 1))
    head_x = summed(head_sum[1, 0, 0], x_1)
    head_y = summed(head_sum[0, 1, 1], y_1)
    d_iso_all, up_part, x_0, y_0, head_x, head_y = together(
        swap(d_iso),
        up_part,
        across(after(head_sum[0, 1, 0], d_iso), "tm", 1),
        across(after(head_sum[1, 0, 1], d_iso), "series", 2),
        head_x,
        head_y,
    )
    (partial,) = kernel_call(
        functools.partial(iso_back_body, geo),
        step_block,
        (shifts, d_iso_all, *step_starts, *iso_wide),
        32,
        scalars=(0,),
    )
    part = (sum(iso_slab) // 2 + SUM_ROWS, channels)
    iso_mine, iso_sent = kernel_call(
        functools.partial(iso_grad_body, geo),
        [(part, BF)] * 2,
        (shifts, hidden_all, d_iso_all, *step_starts),
        32,
        scalars=(0,),
        scratch=[
            *(pltpu.VMEM((touched[b] * channels, channels), F32) for b in range(2)),
            pltpu.VMEM((2, *part), BF),
        ],
    )
    head_sum = (
        summed(head_sum[0, 0, 0], x_0, across(head_x, "series", 2)),
        summed(head_sum[0, 0, 1], y_0, across(head_y, "tm", 1)),
    )
    up_low, up_high = cut(up_part, 1)
    partial, iso_mine, iso_sent, up_a, *head_sum = together(
        swap(partial), iso_mine, iso_sent, across(up_low, "series", 2), *head_sum
    )
    (d_conv,) = kernel_call(
        functools.partial(conv_back_body, geo), [((n, *own_steps), BF)], (partial, d_pair, hidden_one), 8
    )
    iso_part = summed(after(iso_mine, d_conv), across(iso_sent, "series", 1))
    head_sum, bit = summed(head_sum[0], across(after(head_sum[1], d_conv), "tm", 2)), 4
    while bit < half:
        head_sum, got = jnp.split(head_sum, 2)
        head_sum, bit = summed(head_sum, across(got, "tm", bit)), 2 * bit
    d_conv_all, up_b, head_sum, iso_part = together(
        swap(d_conv), across(up_high, "series", 2), head_sum, iso_part
    )

    def grads_of(part, got, sizes):
        return kernel_call(
            join_body,
            [((size, channels), F32) for size in (*sizes, 2 * SUM_ROWS)],
            (core, part, got),
            24,
            scalars=(0,),
        )

    (d_windows,) = kernel_call(
        functools.partial(slab_out_body, geo), [(pay_shape, BF)], (d_conv_all, stride_own), 24
    )
    stride_mine, stride_sent = slab_grads(windows, d_conv_all)
    stride_part = summed(stride_mine, across(stride_sent, "series", 1))
    at = sum(quarter_rows)
    up_part = summed(after(up_part, d_windows), jnp.concatenate([up_a, up_b]))
    iso_low, iso_high = cut(after(iso_part, d_windows))
    d_windows, iso_a, stride_a, up_part, up_got = together(
        swap(d_windows),
        across(iso_low, "series", 2),
        across(cut(stride_part, 1)[0], "series", 2),
        up_part,
        across(up_part, "series", 1),
    )
    edge = ((HALO, channels), F32)
    own, to_left, to_right = kernel_call(
        functools.partial(input_back_body, geo),
        [((rows, channels), F32), edge, edge],
        (*as_taps(d_windows), *window_infos, residual),
        24,
    )
    iso_b = across(iso_high, "series", 2)
    iso_part = summed(after(iso_part, own), jnp.concatenate([iso_a, iso_b]))
    head_mine = summed(head_sum[0], across(after(head_sum[1], own), "tm", half))
    from_right, from_left, stride_b, iso_part, head_mine = together(
        lax.ppermute(to_left, "tm", down_route),
        lax.ppermute(to_right, "tm", up_route),
        across(cut(stride_part, 1)[1], "series", 2),
        iso_part,
        head_mine,
    )
    ups = grads_of(after(up_part, own), up_got, slab)
    input_grad = jnp.concatenate(
        [own[:HALO] + from_left, own[HALO : rows - HALO], own[rows - HALO :] + from_right], axis=0
    ).astype(BF)
    stride_part = summed(stride_part, jnp.concatenate([stride_a, stride_b]))
    stride_got, iso_got = across(stride_part, "series", 1), across(iso_part, "series", 1)
    head_y = across(head_mine[:at], "series", 2)
    head_y = jnp.where(
        bit_of("series", 2) == 0, jnp.stack([head_mine[:at], head_y]), jnp.stack([head_y, head_mine[:at]])
    )
    head_got = across(head_y, "series", 1)
    head_grad = jnp.where(
        bit_of("series", 1) == 0, jnp.stack([head_y, head_got], axis=1), jnp.stack([head_got, head_y], axis=1)
    )
    head_grad = head_grad.reshape(4, *head_grad.shape[2:]).astype(F32)
    head_grads = [
        g.reshape(-1, channels)
        for g in jnp.split(head_grad, [quarter_rows[0], sum(quarter_rows[:2])], axis=1)
    ]
    sums = head_mine[at:].astype(F32)
    count = expand_bias.shape[0] // channels
    expand_grad = sums[10 : 10 + count].reshape(-1)

    strides = grads_of(stride_part, stride_got, slab)
    isos = grads_of(iso_part, iso_got, iso_slab)
    return (
        result[None],
        input_grad[None],
        strides[0], strides[2][0], isos[0], isos[2][0], ups[0], sums[8],
        strides[1], strides[2][1], isos[1], isos[2][1], ups[1], sums[9],
        isos[2][2] + sums[6], isos[2][3] + sums[7],
        head_grads[0], sums[5], sums[3], sums[4],
        head_grads[1], expand_grad, head_grads[2], sums[2], sums[0], sums[1],
    )


def solution(mesh):
    tokens, weight, whole = P("series", "tm", None), P("tm", None), P()
    pair = (weight, whole)
    return jax.shard_map(
        on_device,
        mesh=mesh,
        in_specs=(
            tokens, P("series", None), *(pair * 6), whole, whole, *pair, whole, whole, *pair, *pair, whole, whole,
            tokens,
        ),
        out_specs=(tokens, tokens, *(pair * 6), whole, whole, *pair, whole, whole, *pair, *pair, whole, whole),
        check_vma=False,
    )
```

```python
import functools
import math

import jax
import jax.numpy as jnp
from jax import lax
from jax.experimental import pallas as pl
from jax.experimental.pallas import tpu as pltpu
from jax.sharding import PartitionSpec as P

SCALES = (12, 16)
AVERAGES = (13, 17)
TAPS = (16, 12)
UNIT = 48
EPSILON = 1e-05
HALO = 16
FFN_CHUNK = 512
SUM_ROWS = 16

BF = jnp.bfloat16
F32 = jnp.float32
I32 = jnp.int32


def dot(left, right):
    return lax.dot_general(left, right, (((1,), (0,)), ((), ())), preferred_element_type=F32)


def dot_nt(left, right):
    return lax.dot_general(left, right, (((1,), (1,)), ((), ())), preferred_element_type=F32)


def dot_tn(left, right):
    return lax.dot_general(left, right, (((0,), (0,)), ((), ())), preferred_element_type=F32)


def kernel_call(body, outs, args, mib, scalars=(), scratch=()):
    specs = [
        pl.BlockSpec(memory_space=pltpu.SMEM if i in scalars else pltpu.VMEM)
        for i in range(len(args))
    ]
    return pl.pallas_call(
        body,
        out_shape=[jax.ShapeDtypeStruct(shape, dtype) for shape, dtype in outs],
        in_specs=specs,
        out_specs=[pl.BlockSpec(memory_space=pltpu.VMEM) for _ in outs],
        scratch_shapes=list(scratch),
        compiler_params=pltpu.CompilerParams(vmem_limit_bytes=mib << 20),
    )(*args)


def tap_to_payload(x, scale, q, n):
    rows, channels = x.shape
    m, h = rows // scale, channels // q
    parts = [x[:, c * q : (c + 1) * q].reshape(scale, 1, m, q) for c in range(h)]
    whole = parts[0] if h == 1 else jnp.concatenate(parts, axis=1)
    return whole.reshape(n, scale * h * m // n, q)


def payload_to_tap(p, scale, channels):
    n, rows, q = p.shape
    h = channels // q
    m = n * rows // (scale * h)
    p = p.reshape(scale, h, m, q)
    parts = [p[:, c].reshape(scale * m, q) for c in range(h)]
    return parts[0] if h == 1 else jnp.concatenate(parts, axis=1)


def payload_units(p, m):
    n, rows, q = p.shape
    p = p.reshape(n, rows // m, m, q)
    return [p[:, i].reshape(n * m, q).astype(BF) for i in range(rows // m)]


def units_to_payload(units, n):
    parts = [u.reshape(n, u.shape[0] // n, u.shape[1]) for u in units]
    return parts[0] if len(parts) == 1 else jnp.concatenate(parts, axis=1)


def split_steps(ref, counts):
    whole = ref[...].astype(F32)
    n, _, channels = whole.shape
    first = whole[:, : counts[0], :].reshape(n * counts[0], channels)
    return [first, whole[:, counts[0] : sum(counts), :].reshape(n * counts[1], channels)]


def join_steps(parts, n):
    return jnp.concatenate([p.reshape(n, p.shape[0] // n, p.shape[1]) for p in parts], axis=1)


def norm_stats(v):
    mean = jnp.mean(v, axis=-1, keepdims=True)
    centered = v - mean
    rstd = lax.rsqrt(jnp.mean(centered * centered, axis=-1, keepdims=True) + EPSILON)
    return centered * rstd, rstd


def norm_back(d, gain, xhat, rstd):
    dg = d * gain
    mean_d = jnp.mean(dg, axis=-1, keepdims=True)
    mean_dx = jnp.mean(dg * xhat, axis=-1, keepdims=True)
    return rstd * (dg - mean_d - xhat * mean_dx)


def column_sum(v):
    return jnp.sum(v, axis=0, keepdims=True)


def average_counts(info, kernel, columns):
    place, first, last = info[:, 0:1], info[:, 1:2], info[:, 2:3]
    reach = kernel // 2
    column = lax.broadcasted_iota(I32, (info.shape[0], columns), 1)
    away = column - place
    inside = (jnp.abs(away) <= reach) & (column >= first) & (column <= last)
    counts = jnp.where(inside, 1, 0)
    counts = counts + jnp.where(column == first, jnp.maximum(reach - (place - first), 0), 0)
    counts = counts + jnp.where(column == last, jnp.maximum(reach - (last - place), 0), 0)
    return counts, away == 0


def season_matrix(info, kernel, columns):
    counts, own = average_counts(info, kernel, columns)
    values = jnp.where(own, kernel, 0) - counts
    values = jnp.where(info[:, 0:1] >= info[:, 1:2], values, 0)
    return values.astype(F32).astype(BF)


def token_order(rows, scale):
    m = rows // scale
    place = lax.broadcasted_iota(I32, (rows, rows), 0)
    column = lax.broadcasted_iota(I32, (rows, rows), 1)
    tap = jnp.zeros_like(column)
    for k in range(1, scale):
        tap = tap + jnp.where(column >= k * m, 1, 0)
    return jnp.where(place == scale * (column - tap * m) + tap, 1.0, 0.0).astype(BF)


def join_payload(geo, taps):
    return jnp.concatenate(
        [tap_to_payload(t, SCALES[b], geo["q"], geo["n"]) for b, t in enumerate(taps)], axis=1
    )


def split_payload(geo, payload, channels):
    low = geo["pay_rows"][0]
    parts = (payload[:, :low], payload[:, low:])
    return [payload_to_tap(p, SCALES[b], channels) for b, p in enumerate(parts)]


def store_taps(geo, outs, taps):
    if not geo["aligned"]:
        for out, tap in zip(outs, taps):
            out[...] = tap.astype(BF)
        return
    outs[0][...] = join_payload(geo, taps).astype(BF)


def load_taps(geo, pays, channels):
    if not geo["aligned"]:
        return [p[...] for p in pays]
    whole = pays[0][...].astype(F32)
    return [t.astype(BF) for t in split_payload(geo, whole, channels)]


def matrices_body(info_one, info_two, matrices, orders):
    for b, info in enumerate((info_one, info_two)):
        matrices[b] = season_matrix(info[...], AVERAGES[b], matrices.shape[2])
        orders[b] = token_order(orders.shape[1], SCALES[b])


def windows_body(geo, tok, left, right, matrices, *outs):
    x = jnp.concatenate([left[...], tok[...], right[...]], axis=0)
    parts = [dot(matrices[b], x) * (1.0 / AVERAGES[b]) for b in range(2)]
    store_taps(geo, outs, parts)


def season_body(tok, left, right, info, out):
    x = jnp.concatenate([left[...], tok[...], right[...]], axis=0)
    wide = tok[...].astype(F32)
    for b in range(2):
        counts, _ = average_counts(info[...], AVERAGES[b], x.shape[0])
        out[b] = wide - dot(counts.astype(F32).astype(BF), x) * (1.0 / AVERAGES[b])


def slab_starts(geo):
    return (0, geo["slab"][0])


def units_against(geo, payload, weight, totals):
    low = geo["pay_rows"][0]
    for b, p in enumerate((payload[:, :low], payload[:, low:])):
        q, start = geo["q"], slab_starts(geo)[b]
        for i, unit in enumerate(payload_units(p, geo["m"][b])):
            term = dot(unit, weight[start + i * q : start + (i + 1) * q, :])
            totals[b] = term if totals[b] is None else totals[b] + term


def slab_in_body(geo, payload, weight, out):
    totals = [None, None]
    units_against(geo, payload[...].astype(F32), weight, totals)
    out[...] = join_steps(totals, geo["n"]).astype(BF)


def steps_against(geo, lows, weight, n):
    q = geo["q"]
    parts = []
    for b, low in enumerate(lows):
        start = slab_starts(geo)[b]
        units = [
            dot_nt(low, weight[start + i * q : start + (i + 1) * q, :])
            for i in range(geo["slab"][b] // q)
        ]
        parts.append(units_to_payload(units, n))
    return jnp.concatenate(parts, axis=1).astype(BF)


def slab_out_body(geo, steps, own, out):
    lows = [x.astype(BF) for x in split_steps(steps, geo["m"])]
    out[...] = steps_against(geo, lows, own, geo["n"])


def store_halved(out, start, size, at, value):
    step = math.gcd(value.shape[0], size // 2)
    for i in range(0, value.shape[0], step):
        h, r = divmod(at + i, size // 2)
        out[h, start + r : start + r + step, :] = value[i : i + step].astype(BF)


def store_core_parts(core, halves, rows, own, sent):
    blank = jnp.zeros((SUM_ROWS - len(rows), halves.shape[2]), F32)
    halves[0, halves.shape[1] - SUM_ROWS :, :] = jnp.concatenate([*rows, blank], axis=0).astype(BF)
    halves[1, halves.shape[1] - SUM_ROWS :, :] = jnp.zeros((SUM_ROWS, halves.shape[2]), BF)
    own[...] = halves[core]
    sent[...] = halves[1 - core]


def slab_grad_body(geo, core, payload, steps, own, sent, halves):
    low, q, slab = geo["pay_rows"][0], geo["q"], geo["slab"]
    rights = split_steps(steps, geo["m"])
    wide = payload[...].astype(F32)
    for b in range(2):
        right = rights[b].astype(BF)
        part = wide[:, :low] if b == 0 else wide[:, low:]
        for i, unit in enumerate(payload_units(part, geo["m"][b])):
            store_halved(halves, slab_starts(geo)[b] // 2, slab[b], i * q, dot_tn(unit, right))
    store_core_parts(core[0], halves, [column_sum(r) for r in rights], own, sent)


def join_body(core, part, got, out_one, out_two, sums):
    at = 0
    for out in (out_one, out_two, sums):
        rows = out.shape[0] // 2
        for which, value in ((core[0], part), (1 - core[0], got)):
            begin = pl.multiple_of(which * rows, math.gcd(rows, 512))
            out[pl.ds(begin, rows), :] = value[at : at + rows, :].astype(F32)
        at += rows


def tap_inputs(geo, b, shifts, hidden, start):
    count = hidden.shape[0]
    step = lax.broadcasted_iota(I32, (count, 1), 0)
    pieces = []
    for i in range(geo["touched"][b]):
        shift = jnp.maximum(shifts[b] - i, 0)
        moved = pltpu.roll(hidden, shift, 0)
        pieces.append(jnp.where(step - shift >= start, moved, 0.0).astype(BF))
    return pieces


def iso_body(geo, shifts, steps, start_one, start_two, weight_one, weight_two, out):
    parts = []
    hiddens = split_steps(steps, geo["m"])
    for b, (start, weight) in enumerate(((start_one, weight_one), (start_two, weight_two))):
        total = None
        channels = hiddens[b].shape[1]
        for i, piece in enumerate(tap_inputs(geo, b, shifts, hiddens[b], start[...])):
            term = dot(piece, weight[i * channels : (i + 1) * channels, :])
            total = term if total is None else total + term
        parts.append(total)
    out[...] = join_steps(parts, geo["n"]).astype(BF)


def iso_back_body(geo, shifts, d_iso, start_one, start_two, weight_one, weight_two, out):
    parts = []
    for b, (d, start, weight) in enumerate(
        zip(split_steps(d_iso, geo["m"]), (start_one, start_two), (weight_one, weight_two))
    ):
        count, channels = d.shape
        low = d.astype(BF)
        step = lax.broadcasted_iota(I32, (count, 1), 0)
        total = None
        for i in range(geo["touched"][b]):
            shift = jnp.maximum(shifts[b] - i, 0)
            stacked = dot_nt(low, weight[i * channels : (i + 1) * channels, :])
            stacked = jnp.where(step - shift >= start[...], stacked, 0.0)
            moved = pltpu.roll(stacked, lax.rem(count - shift, count), 0)
            total = moved if total is None else total + moved
        parts.append(total)
    out[...] = join_steps(parts, geo["n"]).astype(BF)


def iso_grad_body(geo, shifts, steps, d_iso, start_one, start_two, own, sent, wide_one, wide_two, halves):
    hiddens, ds = split_steps(steps, geo["m"]), split_steps(d_iso, geo["m"])
    begin = 0
    for b, (start, wide) in enumerate(((start_one, wide_one), (start_two, wide_two))):
        channels = hiddens[b].shape[1]
        right = ds[b].astype(BF)
        for i, piece in enumerate(tap_inputs(geo, b, shifts, hiddens[b], start[...])):
            wide[i * channels : (i + 1) * channels, :] = dot_tn(piece, right)
        part = geo["iso_slab"][b] // 2
        for h in range(2):
            at = pl.multiple_of(shifts[2 + b] + h * part, math.gcd(geo["iso_q"][b], part))
            halves[h, begin : begin + part, :] = wide[pl.ds(at, part), :].astype(BF)
        begin += part
    at = sum(geo["m"])
    norm_sums = jnp.sum(d_iso[:, at:, :].astype(F32), axis=0)
    rows = [*(column_sum(d) for d in ds), norm_sums[0:1], norm_sums[1:2]]
    store_core_parts(shifts[4], halves, rows, own, sent)


def branch_rows(pair, counts):
    total = sum(counts)
    step = lax.broadcasted_iota(I32, (total, 1), 0)
    return jnp.where(step < counts[0], pair[0:1, :], pair[1:2, :])


def hidden_one_body(geo, parts, bias, hidden, low):
    value = jnp.tanh(jnp.sum(parts[...].astype(F32), axis=0) + branch_rows(bias, geo["m"]))
    hidden[...] = value
    low[...] = jnp.broadcast_to(value.astype(BF)[None], low.shape)


def mix_body(geo, parts, bias, hidden_one, gain, shift, hidden, mixed):
    value = jnp.tanh(jnp.sum(parts[...].astype(F32), axis=0) + branch_rows(bias, geo["m"]))
    hidden[...] = value
    xhat, _ = norm_stats(value + hidden_one[...])
    low = (xhat * gain[...] + shift[...]).astype(BF)
    mixed[...] = jnp.broadcast_to(low[None], mixed.shape)


def mix_back_body(geo, parts, hidden_one, hidden_two, gain, d_pair, d_iso):
    d = jnp.sum(parts[...].astype(F32), axis=0)
    two = hidden_two[...]
    xhat, rstd = norm_stats(two + hidden_one[...])
    pair = norm_back(d, gain[...], xhat, rstd)
    iso = (1.0 - two * two) * pair
    d_pair[...] = pair
    blank = jnp.zeros((d_iso.shape[1] - iso.shape[0] - 2, iso.shape[1]), F32)
    low = jnp.concatenate([iso, column_sum(d * xhat), column_sum(d), blank], axis=0).astype(BF)
    d_iso[...] = jnp.broadcast_to(low[None], d_iso.shape)


def conv_back_body(geo, parts, d_pair, hidden_one, d_conv):
    one = hidden_one[...]
    d = (jnp.sum(parts[...].astype(F32), axis=0) + d_pair[...]) * (1.0 - one * one)
    d_conv[...] = jnp.broadcast_to(d.astype(BF)[None], d_conv.shape)


def place_head(geo, order, pieces, merge, expand, project):
    m_rows, h_rows = geo["quarter_rows"][:2]
    block = 0
    for piece in pieces:
        for i in range(piece.shape[0]):
            at = pl.multiple_of(order[block] * m_rows, m_rows)
            merge[pl.ds(at, m_rows), :] = piece[i, :m_rows, :]
            at = pl.ds(pl.multiple_of(order[block] * h_rows, h_rows), h_rows)
            expand[at, :] = piece[i, m_rows : m_rows + h_rows, :]
            project[at, :] = piece[i, m_rows + h_rows :, :]
            block += 1


def head_body(geo, *refs):
    taps = geo["taps"]
    pays, refs = refs[:taps], refs[taps:]
    (
        season, cotangent, up_bias, mix_gain, mix_shift, merge_bias, feed_gain, feed_shift,
        expand_bias, project_bias, final_gain, final_shift, orders,
    ) = refs[:13]
    refs = refs[13:]
    grads = 2 if geo["fits"] else 3
    if geo["fits"]:
        places, pieces, refs = refs[0], refs[1 : 1 + geo["pieces"]], refs[1 + geo["pieces"] :]
        merge_weight, expand_weight, project_weight = refs[-3:]
        refs = refs[:-3]
        place_head(geo, places, pieces, merge_weight, expand_weight, project_weight)
    else:
        (merge_weight, expand_weight, project_weight), refs = refs[:3], refs[3:]
    d_pays, (result, d_res_out, sums), refs = refs[:taps], refs[taps : taps + 3], refs[taps + 3 :]
    grad_outs, refs = refs[:grads], refs[grads:]
    slope, merge_in, normed_out, activ_out, d_sum_out, d_pre_out, d_merged_out = refs
    hidden_units = expand_weight.shape[0]
    rows, channels = cotangent.shape
    width = FFN_CHUNK
    chunks = expand_weight.shape[0] // width
    taps = load_taps(geo, pays, channels)
    ups, kept = [], []
    for b in range(2):
        up = jnp.tanh(dot(orders[b], taps[b]) + up_bias[b : b + 1, :])
        xhat, rstd = norm_stats(up + season[b])
        ups.append(up)
        kept.append((xhat, rstd))
        merge_in[:, b * channels : (b + 1) * channels] = (
            xhat * mix_gain[...] + mix_shift[...]
        ).astype(BF)
    merged = dot(merge_in[...], merge_weight[...]) + merge_bias[...]
    feed_hat, feed_rstd = norm_stats(merged)
    normed_out[...] = (feed_hat * feed_gain[...] + feed_shift[...]).astype(BF)

    def forward_chunk(c, total):
        at = pl.ds(pl.multiple_of(c * width, width), width)
        pre = dot_nt(normed_out[...], expand_weight[at, :]) + expand_bias[:, at]
        half = 0.5 + 0.5 * lax.erf(pre * math.sqrt(0.5))
        slope[c] = half + pre * (jnp.exp(-0.5 * pre * pre) * (1.0 / math.sqrt(2.0 * math.pi)))
        activ_out[:, at] = (pre * half).astype(BF)
        return total + dot(activ_out[:, at], project_weight[at, :])

    summed = lax.fori_loop(0, chunks, forward_chunk, merged + project_bias[...])
    final_hat, final_rstd = norm_stats(summed)
    result[...] = (final_hat * final_gain[...] + final_shift[...]).astype(BF)

    d_out = cotangent[...].astype(F32)
    sums[0:1, :] = column_sum(d_out * final_hat)
    sums[1:2, :] = column_sum(d_out)
    d_sum = norm_back(d_out, final_gain[...], final_hat, final_rstd)
    sums[2:3, :] = column_sum(d_sum)
    d_sum_out[...] = d_sum.astype(BF)

    def backward_chunk(c, total):
        at = pl.ds(pl.multiple_of(c * width, width), width)
        d_pre = slope[c] * dot_nt(d_sum_out[...], project_weight[at, :])
        sums[pl.ds(10 + c, 1), :] = column_sum(d_pre)
        d_pre_out[:, at] = d_pre.astype(BF)
        return total + dot(d_pre_out[:, at], expand_weight[at, :])

    d_normed = lax.fori_loop(0, chunks, backward_chunk, jnp.zeros((rows, channels), F32))
    sums[3:4, :] = column_sum(d_normed * feed_hat)
    sums[4:5, :] = column_sum(d_normed)
    d_merged = d_sum + norm_back(d_normed, feed_gain[...], feed_hat, feed_rstd)
    sums[5:6, :] = column_sum(d_merged)
    d_merged_out[...] = d_merged.astype(BF)
    gain_sum, shift_sum = 0.0, 0.0
    d_taps = []
    for b in range(2):
        d = dot_nt(d_merged_out[...], merge_weight[b * channels : (b + 1) * channels, :])
        xhat, rstd = kept[b]
        gain_sum = gain_sum + column_sum(d * xhat)
        shift_sum = shift_sum + column_sum(d)
        d_res = norm_back(d, mix_gain[...], xhat, rstd)
        d_res_out[b] = d_res
        d_up = (1.0 - ups[b] * ups[b]) * d_res
        sums[8 + b : 9 + b, :] = column_sum(d_up)
        d_taps.append(dot_tn(orders[b], d_up.astype(BF)))
    sums[6:7, :] = gain_sum
    sums[7:8, :] = shift_sum
    store_taps(geo, d_pays, d_taps)

    count = 10 + chunks
    sums[count:, :] = jnp.zeros((SUM_ROWS - count, channels), F32)
    pairs = ((merge_in, d_merged_out), (d_pre_out, normed_out), (activ_out, d_sum_out))
    if not geo["fits"]:
        for out, (left, right) in zip(grad_outs, pairs):
            out[...] = dot_tn(left[...], right[...]).astype(BF)
        return
    start = 0
    for (left, right), grad, size in zip(
        pairs, (merge_weight, expand_weight, project_weight), geo["quarter_rows"]
    ):
        grad[...] = dot_tn(left[...], right[...]).astype(BF)
        for h, out in enumerate(grad_outs):
            blocks = out.shape[0]
            for i in range(blocks):
                begin = pl.multiple_of(places[h * blocks + i] * size, size)
                out[i, start : start + size, :] = grad[pl.ds(begin, size), :]
        start += size
    low = sums[...].astype(BF)
    for out in grad_outs:
        out[:, start:, :] = jnp.broadcast_to(low, (out.shape[0], *low.shape))


def residual_body(d_res, info, out):
    rows = d_res.shape[1]
    columns = rows + 2 * HALO
    total = jnp.zeros((columns, d_res.shape[2]), F32)
    for b in range(2):
        counts, _ = average_counts(info[...], AVERAGES[b], columns)
        adjoint = dot_tn(counts.astype(F32).astype(BF), d_res[b].astype(BF))
        total = total - adjoint * (1.0 / AVERAGES[b])
    out[0:HALO, :] = total[0:HALO]
    out[HALO : HALO + rows, :] = total[HALO : HALO + rows] + d_res[0] + d_res[1]
    out[HALO + rows :, :] = total[HALO + rows :]


def input_back_body(geo, *refs):
    pays = refs[: geo["taps"]]
    matrices, residual, own, left, right = refs[geo["taps"] :]
    columns, channels = residual.shape
    rows = columns - 2 * HALO
    taps = load_taps(geo, pays, channels)
    total = residual[...]
    for b in range(2):
        total = total + dot_tn(matrices[b], taps[b]) * (1.0 / AVERAGES[b])
    left[...] = total[0:HALO]
    own[...] = total[HALO : HALO + rows]
    right[...] = total[HALO + rows :]


def swap(x):
    return lax.all_to_all(x, "tm", 0, 0)


def together(*values):
    return lax.optimization_barrier(values)


def after(x, dep):
    return lax.optimization_barrier((x, dep))[0]


def across(x, axis, bit):
    return lax.ppermute(x, axis, [(i, i ^ bit) for i in range(lax.axis_size(axis))])


def bit_of(axis, bit):
    return (lax.axis_index(axis) & bit) // bit


def tm_bits():
    return [1 << i for i in range(lax.axis_size("tm").bit_length() - 1)]


def flipped(x):
    bits = [("series", 1), ("series", 2)] + [("tm", b) for b in tm_bits()]
    for at, (axis, bit) in enumerate(bits):
        x = jnp.where(bit_of(axis, bit) == 1, jnp.flip(x, at), x)
    return x


def natural_rows(x):
    bits = len(tm_bits())
    x = flipped(x.reshape([2] * (bits + 2) + list(x.shape[1:])))
    x = jnp.transpose(x, [*range(bits + 1, 1, -1), 1, 0, bits + 2, bits + 3])
    return x.reshape(-1, x.shape[-1])


def relative_blocks(x):
    bits = len(tm_bits())
    x = x.reshape([2] * (bits + 2) + [x.shape[0] >> (bits + 2), x.shape[1]])
    x = jnp.transpose(x, [bits + 1, bits, *range(bits - 1, -1, -1), bits + 2, bits + 3])
    return flipped(x).reshape(-1, *x.shape[-2:])


def summed(*parts):
    return sum(p.astype(F32) for p in parts).astype(BF)


def neighbours(n):
    up = [(i, i + 1) for i in range(n - 1)]
    return up, [(j, i) for i, j in up]


def on_device(
    inputs, lengths,
    stride_weight_twelve, stride_bias_twelve, isometric_weight_twelve, isometric_bias_twelve,
    upsample_weight_twelve, upsample_bias_twelve,
    stride_weight_sixteen, stride_bias_sixteen, isometric_weight_sixteen, isometric_bias_sixteen,
    upsample_weight_sixteen, upsample_bias_sixteen,
    mix_gain, mix_shift, merge_weight, merge_bias, feed_gain, feed_shift,
    expand_weight, expand_bias, project_weight, project_bias, final_gain, final_shift, cotangent,
):
    n = lax.axis_size("tm")
    me = lax.axis_index("tm")
    rows, channels = inputs.shape[1:]
    stride_weights = (stride_weight_twelve, stride_weight_sixteen)
    iso_weights = (isometric_weight_twelve, isometric_weight_sixteen)
    up_weights = (upsample_weight_twelve, upsample_weight_sixteen)
    m = [rows // s for s in SCALES]
    slab = [w.shape[0] for w in stride_weights]
    q = math.gcd(*slab, channels)
    pay_rows = [slab[b] // q * m[b] for b in range(2)]
    iso_slab = [w.shape[0] for w in iso_weights]
    iso_q = [math.gcd(r, channels) for r in iso_slab]
    touched = [-(-(iso_slab[b] + channels - iso_q[b]) // channels) for b in range(2)]
    half = n // 2
    geo = {
        "n": n, "half": half, "m": m, "q": q, "slab": slab, "pay_rows": pay_rows, "touched": touched,
        "iso_slab": iso_slab, "iso_q": iso_q,
        "aligned": q % 128 == 0,
    }
    geo["taps"] = 1 if geo["aligned"] else 2
    pay_shape = (n, sum(pay_rows), q)
    pay_outs = [(pay_shape, BF)] if geo["aligned"] else [((rows, channels), BF)] * 2

    def as_payload(parts):
        return parts[0] if geo["aligned"] else join_payload(geo, parts)

    def as_taps(payload):
        return [payload] if geo["aligned"] else split_payload(geo, payload, channels)

    def row(v):
        return v[None, :]

    lengths_row = lengths[0]
    count = lengths_row.shape[0]
    upto = jnp.arange(count)[None, :] <= jnp.arange(count)[:, None]
    ends = UNIT * jnp.sum(jnp.where(upto, lengths_row[None, :], 0), axis=1)
    starts = ends - UNIT * lengths_row

    def bounds(places):
        inside = (starts[None, :] <= places[:, None]) & (places[:, None] < ends[None, :])
        first = jnp.sum(jnp.where(inside, starts[None, :], 0), axis=1)
        return first, jnp.sum(jnp.where(inside, ends[None, :], 0), axis=1)

    base = me * rows
    local = jnp.arange(rows, dtype=I32)

    def info_of(places, anchors):
        first, last = bounds(anchors + base)
        shift = base - HALO
        return jnp.stack([places + HALO, first - shift, last - 1 - shift], axis=1)

    token_info = info_of(local, local)
    window_infos, step_starts = [], []
    for b in range(2):
        tap, step = local // m[b], local % m[b]
        anchor = SCALES[b] * step
        window_infos.append(info_of(anchor - SCALES[b] // 2 + tap, anchor))
        all_steps = jnp.arange(n * m[b], dtype=I32)
        step_starts.append((bounds(SCALES[b] * all_steps)[0] // SCALES[b])[:, None])

    replica = lax.axis_index("series")

    head_weights = (merge_weight, expand_weight, project_weight)
    head_rows = [w.shape[0] for w in head_weights]
    quarter_rows = [r // 4 for r in head_rows]
    geo["quarter_rows"] = quarter_rows
    geo["fits"] = all(r % 16 == 0 for r in quarter_rows)
    quarter = jnp.concatenate(
        [lax.dynamic_slice_in_dim(w, replica * r, r) for w, r in zip(head_weights, quarter_rows)], axis=0
    )
    stride_own = jnp.concatenate(stride_weights, axis=0)
    up_own = jnp.concatenate(up_weights, axis=0)

    far, bit = [0], half
    while bit > 1:
        far, bit = far + [o ^ bit for o in far], bit // 2
    near = [o ^ 1 for o in far]
    half_order = [(o, r) for r in (0, 2) for o in far + near]
    relative = half_order + [(o, r ^ 1) for o, r in half_order]
    order = jnp.stack([(me ^ o) * 4 + (replica ^ r) for o, r in relative]).astype(I32)

    iso_first = [(iso_slab[b] * me) // channels for b in range(2)]
    iso_offset = [iso_slab[b] * me - iso_first[b] * channels for b in range(2)]
    iso_wide = []
    for b in range(2):
        if touched[b] * channels == iso_slab[b]:
            iso_wide.append(iso_weights[b])
        else:
            blank = jnp.zeros((touched[b] * channels, channels), BF)
            iso_wide.append(lax.dynamic_update_slice(blank, iso_weights[b], (iso_offset[b], 0)))
    shifts = jnp.stack([*(TAPS[b] - 1 - iso_first[b] for b in range(2)), *iso_offset, replica & 1]).astype(I32)

    up_route, down_route = neighbours(n)
    tokens = inputs[0]
    step_block = [((n, sum(m), channels), BF)]
    own_steps = (sum(m), channels)
    blocks = quarter[None]
    left, right, got = together(
        lax.ppermute(tokens[rows - HALO :], "tm", up_route),
        lax.ppermute(tokens[:HALO], "tm", down_route),
        across(blocks, "tm", half),
    )
    blocks, bit = jnp.concatenate([blocks, got]), half // 2
    while bit > 2:
        blocks, bit = jnp.concatenate([blocks, across(blocks, "tm", bit)]), bit // 2
    matrices, orders = kernel_call(
        matrices_body,
        [((2, rows, rows + 2 * HALO), BF), ((2, rows, rows), BF)],
        window_infos,
        24,
    )
    windows = kernel_call(
        functools.partial(windows_body, geo), pay_outs, (tokens, left, right, matrices), 24
    )
    windows, got = together(swap(as_payload(windows)), across(blocks, "tm", bit))
    blocks = jnp.concatenate([blocks, got])
    middle = blocks.shape[0] // 2
    (partial,) = kernel_call(
        functools.partial(slab_in_body, geo), step_block, (windows, stride_own), 24
    )
    low_blocks, high_blocks = blocks[:middle], blocks[middle:]
    partial, x_low, y_high = together(
        swap(partial), across(low_blocks, "tm", 1), across(high_blocks, "series", 2)
    )
    hidden_one, hidden_low = kernel_call(
        functools.partial(hidden_one_body, geo),
        [(own_steps, F32), ((n, *own_steps), BF)],
        (partial, jnp.stack([stride_bias_twelve, stride_bias_sixteen])),
        8,
    )
    hidden_all, x_high, y_low = together(
        swap(hidden_low), across(high_blocks, "tm", 1), across(low_blocks, "series", 2)
    )
    (partial,) = kernel_call(
        functools.partial(iso_body, geo),
        step_block,
        (shifts, hidden_all, *step_starts, *iso_wide),
        32,
        scalars=(0,),
    )
    first = (x_low, x_high, y_low, y_high)
    partial, blocks_a, blocks_b = together(
        swap(partial), across(x_low, "series", 2), across(y_high, "tm", 1)
    )
    hidden_two, mixed_low = kernel_call(
        functools.partial(mix_body, geo),
        [(own_steps, F32), ((n, *own_steps), BF)],
        (
            partial,
            jnp.stack([isometric_bias_twelve, isometric_bias_sixteen]),
            hidden_one,
            row(mix_gain),
            row(mix_shift),
        ),
        8,
    )
    (season,) = kernel_call(
        season_body, [((2, rows, channels), F32)], (tokens, left, right, token_info), 24
    )
    mixed_all, season = together(swap(mixed_low), season)
    (ups,) = kernel_call(
        functools.partial(slab_out_body, geo), [(pay_shape, BF)], (mixed_all, up_own), 24
    )
    head_pieces = [blocks, *first, blocks_a, blocks_b]
    ups, *other_pieces = together(swap(ups), *(across(p, "series", 1) for p in head_pieces))
    head_pieces += other_pieces
    geo["pieces"] = len(head_pieces)
    hidden_units = 4 * n * quarter_rows[1]
    head_args = [
        *as_taps(ups), season, cotangent[0], jnp.stack([upsample_bias_twelve, upsample_bias_sixteen]),
        row(mix_gain), row(mix_shift), row(merge_bias), row(feed_gain), row(feed_shift),
        row(expand_bias), row(project_bias), row(final_gain), row(final_shift), orders,
    ]
    head_scratch = [
        pltpu.VMEM((hidden_units // FFN_CHUNK, rows, FFN_CHUNK), F32),
        *(
            pltpu.VMEM((rows, width), BF)
            for width in (2 * channels, channels, hidden_units, channels, hidden_units, channels)
        ),
    ]
    scalars = ()
    if geo["fits"]:
        scalars = (len(head_args),)
        head_args += [order, *head_pieces]
        head_scratch += [pltpu.VMEM((2 * channels, channels), BF)]
        head_scratch += [pltpu.VMEM((hidden_units, channels), BF)] * 2
    else:
        cuts = [quarter_rows[0], sum(quarter_rows[:2])]
        head_args += [natural_rows(w) for w in jnp.split(jnp.concatenate(head_pieces), cuts, axis=1)]
    half_blocks = (2 * n, sum(quarter_rows) + SUM_ROWS, channels)
    head = kernel_call(
        functools.partial(head_body, geo),
        [
            *pay_outs,
            ((rows, channels), BF),
            ((2, rows, channels), F32),
            ((SUM_ROWS, channels), F32),
            *(
                [(half_blocks, BF)] * 2
                if geo["fits"]
                else [((4 * r * n, channels), BF) for r in quarter_rows]
            ),
        ],
        head_args,
        60,
        scalars=scalars,
        scratch=head_scratch,
    )
    d_ups, (result, d_res, head_sums, *head_grads) = head[: geo["taps"]], head[geo["taps"] :]

    if geo["fits"]:
        head_own, head_other = head_grads
    else:
        whole = [relative_blocks(g) for g in head_grads]
        whole.append(jnp.broadcast_to(head_sums.astype(BF), (4 * n, *head_sums.shape)))
        head_own, head_other = jnp.split(jnp.concatenate(whole, axis=1), 2)
    (residual,) = kernel_call(
        residual_body, [((rows + 2 * HALO, channels), F32)], (d_res, token_info), 24
    )
    head_sum = summed(head_own, across(head_other, "series", 1))
    head_sum = head_sum.reshape(2, 2, 2, len(far) // 2, *half_blocks[1:])
    d_ups, head_sum, residual, x_1, y_1 = together(
        swap(as_payload(d_ups)),
        head_sum,
        residual,
        across(head_sum[1, 1, 0], "tm", 1),
        across(head_sum[1, 1, 1], "series", 2),
    )
    core = (replica & 1).reshape(1)

    def slab_grads(payload, steps):
        part = (sum(slab) // 2 + SUM_ROWS, channels)
        return kernel_call(
            functools.partial(slab_grad_body, geo),
            [(part, BF)] * 2,
            (core, payload, steps),
            24,
            scalars=(0,),
            scratch=[pltpu.VMEM((2, *part), BF)],
        )

    def cut(x, thirds=2):
        at = x.shape[0] * thirds // 48 * 16
        return x[:at], x[at:]

    (partial,) = kernel_call(
        functools.partial(slab_in_body, geo), step_block, (d_ups, up_own), 24
    )
    up_mine, up_sent = slab_grads(d_ups, mixed_all)
    head_x = summed(head_sum[1, 0, 0], x_1)
    head_y = summed(head_sum[0, 1, 1], y_1)
    partial, x_0, y_0, up_mine, up_sent, head_x, head_y = together(
        swap(partial),
        across(head_sum[0, 1, 0], "tm", 1),
        across(head_sum[1, 0, 1], "series", 2),
        up_mine,
        up_sent,
        head_x,
        head_y,
    )
    d_pair, d_iso = kernel_call(
        functools.partial(mix_back_body, geo),
        [(own_steps, F32), ((n, sum(m) + 8, channels), BF)],
        (partial, hidden_one, hidden_two, row(mix_gain)),
        8,
    )
    up_part = summed(up_mine, across(up_sent, "series", 1))
    head_sum = (
        summed(head_sum[0, 0, 0], x_0, across(after(head_x, d_iso), "series", 2)),
        summed(head_sum[0, 0, 1], y_0, across(after(head_y, d_iso), "tm", 1)),
    )
    d_iso_all, up_part, *head_sum = together(swap(d_iso), up_part, *head_sum)
    (partial,) = kernel_call(
        functools.partial(iso_back_body, geo),
        step_block,
        (shifts, d_iso_all, *step_starts, *iso_wide),
        32,
        scalars=(0,),
    )
    part = (sum(iso_slab) // 2 + SUM_ROWS, channels)
    iso_mine, iso_sent = kernel_call(
        functools.partial(iso_grad_body, geo),
        [(part, BF)] * 2,
        (shifts, hidden_all, d_iso_all, *step_starts),
        32,
        scalars=(0,),
        scratch=[
            *(pltpu.VMEM((touched[b] * channels, channels), F32) for b in range(2)),
            pltpu.VMEM((2, *part), BF),
        ],
    )
    head_sum, bit = summed(head_sum[0], across(after(head_sum[1], partial), "tm", 2)), 4
    while bit < half:
        head_sum, got = jnp.split(head_sum, 2)
        head_sum, bit = summed(head_sum, across(got, "tm", bit)), 2 * bit
    partial, iso_mine, iso_sent, up_a, head_sum = together(
        swap(partial), iso_mine, iso_sent, across(up_part, "series", 2), head_sum
    )
    (d_conv,) = kernel_call(
        functools.partial(conv_back_body, geo), [((n, *own_steps), BF)], (partial, d_pair, hidden_one), 8
    )
    iso_part = summed(after(iso_mine, d_conv), across(iso_sent, "series", 1))
    up_part = summed(after(up_part, d_conv), up_a)
    iso_low, iso_high = cut(iso_part, 1)
    d_conv_all, up_part, iso_part, iso_high, iso_a = together(
        swap(d_conv), up_part, iso_part, iso_high, across(iso_low, "series", 2)
    )

    def grads_of(part, got, sizes):
        return kernel_call(
            join_body,
            [((size, channels), F32) for size in (*sizes, 2 * SUM_ROWS)],
            (core, part, got),
            24,
            scalars=(0,),
        )

    (d_windows,) = kernel_call(
        functools.partial(slab_out_body, geo), [(pay_shape, BF)], (d_conv_all, stride_own), 24
    )
    stride_mine, stride_sent = slab_grads(windows, d_conv_all)
    stride_part = summed(stride_mine, across(stride_sent, "series", 1))
    iso_b = across(iso_high, "series", 2)
    stride_y = across(stride_part, "series", 2)
    d_windows, up_part, up_got = together(
        swap(d_windows), up_part, across(up_part, "series", 1)
    )
    edge = ((HALO, channels), F32)
    own, to_left, to_right = kernel_call(
        functools.partial(input_back_body, geo),
        [((rows, channels), F32), edge, edge],
        (*as_taps(d_windows), matrices, residual),
        24,
    )
    iso_part = summed(after(iso_part, own), jnp.concatenate([iso_a, iso_b]))
    head_mine = summed(head_sum[0], across(after(head_sum[1], d_windows), "tm", half))
    at = sum(quarter_rows)
    head_y = across(head_mine[:at], "series", 2)
    from_right, from_left = together(
        lax.ppermute(to_left, "tm", down_route), lax.ppermute(to_right, "tm", up_route)
    )
    ups = grads_of(after(up_part, own), up_got, slab)
    input_grad = jnp.concatenate(
        [own[:HALO] + from_left, own[HALO : rows - HALO], own[rows - HALO :] + from_right], axis=0
    ).astype(BF)
    stride_part = summed(stride_part, stride_y)
    stride_got, iso_got = across(stride_part, "series", 1), across(iso_part, "series", 1)
    head_y = jnp.where(
        bit_of("series", 2) == 0, jnp.stack([head_mine[:at], head_y]), jnp.stack([head_y, head_mine[:at]])
    )
    head_got = across(head_y, "series", 1)
    head_grad = jnp.where(
        bit_of("series", 1) == 0, jnp.stack([head_y, head_got], axis=1), jnp.stack([head_got, head_y], axis=1)
    )
    head_grad = head_grad.reshape(4, *head_grad.shape[2:]).astype(F32)
    head_grads = [
        g.reshape(-1, channels)
        for g in jnp.split(head_grad, [quarter_rows[0], sum(quarter_rows[:2])], axis=1)
    ]
    sums = head_mine[at:].astype(F32)
    count = expand_bias.shape[0] // channels
    expand_grad = sums[10 : 10 + count].reshape(-1)

    strides = grads_of(stride_part, stride_got, slab)
    isos = grads_of(iso_part, iso_got, iso_slab)
    return (
        result[None],
        input_grad[None],
        strides[0], strides[2][0], isos[0], isos[2][0], ups[0], sums[8],
        strides[1], strides[2][1], isos[1], isos[2][1], ups[1], sums[9],
        isos[2][2] + sums[6], isos[2][3] + sums[7],
        head_grads[0], sums[5], sums[3], sums[4],
        head_grads[1], expand_grad, head_grads[2], sums[2], sums[0], sums[1],
    )


def solution(mesh):
    tokens, weight, whole = P("series", "tm", None), P("tm", None), P()
    pair = (weight, whole)
    return jax.shard_map(
        on_device,
        mesh=mesh,
        in_specs=(
            tokens, P("series", None), *(pair * 6), whole, whole, *pair, whole, whole, *pair, *pair, whole, whole,
            tokens,
        ),
        out_specs=(tokens, tokens, *(pair * 6), whole, whole, *pair, whole, whole, *pair, *pair, whole, whole),
        check_vma=False,
    )
```

```python
import functools
import math

import jax
import jax.numpy as jnp
from jax import lax
from jax.experimental import pallas as pl
from jax.experimental.pallas import tpu as pltpu
from jax.sharding import PartitionSpec as P

SCALES = (12, 16)
AVERAGES = (13, 17)
TAPS = (16, 12)
UNIT = 48
EPSILON = 1e-05
HALO = 16
FFN_CHUNK = 512
SUM_ROWS = 16

BF = jnp.bfloat16
F32 = jnp.float32
I32 = jnp.int32


def dot(left, right):
    return lax.dot_general(left, right, (((1,), (0,)), ((), ())), preferred_element_type=F32)


def dot_nt(left, right):
    return lax.dot_general(left, right, (((1,), (1,)), ((), ())), preferred_element_type=F32)


def dot_tn(left, right):
    return lax.dot_general(left, right, (((0,), (0,)), ((), ())), preferred_element_type=F32)


def kernel_call(body, outs, args, mib, scalars=(), scratch=()):
    specs = [
        pl.BlockSpec(memory_space=pltpu.SMEM if i in scalars else pltpu.VMEM)
        for i in range(len(args))
    ]
    return pl.pallas_call(
        body,
        out_shape=[jax.ShapeDtypeStruct(shape, dtype) for shape, dtype in outs],
        in_specs=specs,
        out_specs=[pl.BlockSpec(memory_space=pltpu.VMEM) for _ in outs],
        scratch_shapes=list(scratch),
        compiler_params=pltpu.CompilerParams(vmem_limit_bytes=mib << 20),
    )(*args)


def tap_to_payload(x, scale, q, n):
    rows, channels = x.shape
    m, h = rows // scale, channels // q
    parts = [x[:, c * q : (c + 1) * q].reshape(scale, 1, m, q) for c in range(h)]
    whole = parts[0] if h == 1 else jnp.concatenate(parts, axis=1)
    return whole.reshape(n, scale * h * m // n, q)


def payload_to_tap(p, scale, channels):
    n, rows, q = p.shape
    h = channels // q
    m = n * rows // (scale * h)
    p = p.reshape(scale, h, m, q)
    parts = [p[:, c].reshape(scale * m, q) for c in range(h)]
    return parts[0] if h == 1 else jnp.concatenate(parts, axis=1)


def payload_units(p, m):
    n, rows, q = p.shape
    p = p.reshape(n, rows // m, m, q)
    return [p[:, i].reshape(n * m, q).astype(BF) for i in range(rows // m)]


def units_to_payload(units, n):
    parts = [u.reshape(n, u.shape[0] // n, u.shape[1]) for u in units]
    return parts[0] if len(parts) == 1 else jnp.concatenate(parts, axis=1)


def split_steps(ref, counts):
    whole = ref[...].astype(F32)
    n, _, channels = whole.shape
    first = whole[:, : counts[0], :].reshape(n * counts[0], channels)
    return [first, whole[:, counts[0] : sum(counts), :].reshape(n * counts[1], channels)]


def join_steps(parts, n):
    return jnp.concatenate([p.reshape(n, p.shape[0] // n, p.shape[1]) for p in parts], axis=1)


def norm_stats(v):
    mean = jnp.mean(v, axis=-1, keepdims=True)
    centered = v - mean
    rstd = lax.rsqrt(jnp.mean(centered * centered, axis=-1, keepdims=True) + EPSILON)
    return centered * rstd, rstd


def norm_back(d, gain, xhat, rstd):
    dg = d * gain
    mean_d = jnp.mean(dg, axis=-1, keepdims=True)
    mean_dx = jnp.mean(dg * xhat, axis=-1, keepdims=True)
    return rstd * (dg - mean_d - xhat * mean_dx)


def column_sum(v):
    return jnp.sum(v, axis=0, keepdims=True)


def average_counts(info, kernel, columns):
    place, first, last = info[:, 0:1], info[:, 1:2], info[:, 2:3]
    reach = kernel // 2
    column = lax.broadcasted_iota(I32, (info.shape[0], columns), 1)
    away = column - place
    inside = (jnp.abs(away) <= reach) & (column >= first) & (column <= last)
    counts = jnp.where(inside, 1, 0)
    counts = counts + jnp.where(column == first, jnp.maximum(reach - (place - first), 0), 0)
    counts = counts + jnp.where(column == last, jnp.maximum(reach - (last - place), 0), 0)
    return counts, away == 0


def season_matrix(info, kernel, columns):
    counts, own = average_counts(info, kernel, columns)
    values = jnp.where(own, kernel, 0) - counts
    values = jnp.where(info[:, 0:1] >= info[:, 1:2], values, 0)
    return values.astype(F32).astype(BF)


def token_order(rows, scale):
    m = rows // scale
    place = lax.broadcasted_iota(I32, (rows, rows), 0)
    column = lax.broadcasted_iota(I32, (rows, rows), 1)
    tap = jnp.zeros_like(column)
    for k in range(1, scale):
        tap = tap + jnp.where(column >= k * m, 1, 0)
    return jnp.where(place == scale * (column - tap * m) + tap, 1.0, 0.0).astype(BF)


def join_payload(geo, taps):
    return jnp.concatenate(
        [tap_to_payload(t, SCALES[b], geo["q"], geo["n"]) for b, t in enumerate(taps)], axis=1
    )


def split_payload(geo, payload, channels):
    low = geo["pay_rows"][0]
    parts = (payload[:, :low], payload[:, low:])
    return [payload_to_tap(p, SCALES[b], channels) for b, p in enumerate(parts)]


def store_taps(geo, outs, taps):
    if not geo["aligned"]:
        for out, tap in zip(outs, taps):
            out[...] = tap.astype(BF)
        return
    outs[0][...] = join_payload(geo, taps).astype(BF)


def load_taps(geo, pays, channels):
    if not geo["aligned"]:
        return [p[...] for p in pays]
    whole = pays[0][...].astype(F32)
    return [t.astype(BF) for t in split_payload(geo, whole, channels)]


def matrices_body(info_one, info_two, matrices, orders):
    for b, info in enumerate((info_one, info_two)):
        matrices[b] = season_matrix(info[...], AVERAGES[b], matrices.shape[2])
        orders[b] = token_order(orders.shape[1], SCALES[b])


def windows_body(geo, tok, left, right, matrices, *outs):
    x = jnp.concatenate([left[...], tok[...], right[...]], axis=0)
    parts = [dot(matrices[b], x) * (1.0 / AVERAGES[b]) for b in range(2)]
    store_taps(geo, outs, parts)


def season_body(tok, left, right, info, out):
    x = jnp.concatenate([left[...], tok[...], right[...]], axis=0)
    wide = tok[...].astype(F32)
    for b in range(2):
        counts, _ = average_counts(info[...], AVERAGES[b], x.shape[0])
        out[b] = wide - dot(counts.astype(F32).astype(BF), x) * (1.0 / AVERAGES[b])


def slab_starts(geo):
    return (0, geo["slab"][0])


def units_against(geo, payload, weight, totals):
    low = geo["pay_rows"][0]
    for b, p in enumerate((payload[:, :low], payload[:, low:])):
        q, start = geo["q"], slab_starts(geo)[b]
        for i, unit in enumerate(payload_units(p, geo["m"][b])):
            term = dot(unit, weight[start + i * q : start + (i + 1) * q, :])
            totals[b] = term if totals[b] is None else totals[b] + term


def slab_in_body(geo, payload, weight, out):
    totals = [None, None]
    units_against(geo, payload[...].astype(F32), weight, totals)
    out[...] = join_steps(totals, geo["n"]).astype(BF)


def steps_against(geo, lows, weight, n):
    q = geo["q"]
    parts = []
    for b, low in enumerate(lows):
        start = slab_starts(geo)[b]
        units = [
            dot_nt(low, weight[start + i * q : start + (i + 1) * q, :])
            for i in range(geo["slab"][b] // q)
        ]
        parts.append(units_to_payload(units, n))
    return jnp.concatenate(parts, axis=1).astype(BF)


def slab_out_body(geo, steps, own, out):
    lows = [x.astype(BF) for x in split_steps(steps, geo["m"])]
    out[...] = steps_against(geo, lows, own, geo["n"])


def store_halved(out, start, size, at, value):
    step = math.gcd(value.shape[0], size // 2)
    for i in range(0, value.shape[0], step):
        h, r = divmod(at + i, size // 2)
        out[h, start + r : start + r + step, :] = value[i : i + step].astype(BF)


def store_core_parts(core, halves, rows, own, sent):
    blank = jnp.zeros((SUM_ROWS - len(rows), halves.shape[2]), F32)
    halves[0, halves.shape[1] - SUM_ROWS :, :] = jnp.concatenate([*rows, blank], axis=0).astype(BF)
    halves[1, halves.shape[1] - SUM_ROWS :, :] = jnp.zeros((SUM_ROWS, halves.shape[2]), BF)
    own[...] = halves[core]
    sent[...] = halves[1 - core]


def slab_grad_body(geo, core, payload, steps, own, sent, halves):
    low, q, slab = geo["pay_rows"][0], geo["q"], geo["slab"]
    rights = split_steps(steps, geo["m"])
    wide = payload[...].astype(F32)
    for b in range(2):
        right = rights[b].astype(BF)
        part = wide[:, :low] if b == 0 else wide[:, low:]
        for i, unit in enumerate(payload_units(part, geo["m"][b])):
            store_halved(halves, slab_starts(geo)[b] // 2, slab[b], i * q, dot_tn(unit, right))
    store_core_parts(core[0], halves, [column_sum(r) for r in rights], own, sent)


def join_body(core, part, got, out_one, out_two, sums):
    at = 0
    for out in (out_one, out_two, sums):
        rows = out.shape[0] // 2
        for which, value in ((core[0], part), (1 - core[0], got)):
            begin = pl.multiple_of(which * rows, math.gcd(rows, 512))
            out[pl.ds(begin, rows), :] = value[at : at + rows, :].astype(F32)
        at += rows


def tap_inputs(geo, b, shifts, hidden, start):
    count = hidden.shape[0]
    step = lax.broadcasted_iota(I32, (count, 1), 0)
    pieces = []
    for i in range(geo["touched"][b]):
        shift = jnp.maximum(shifts[b] - i, 0)
        moved = pltpu.roll(hidden, shift, 0)
        pieces.append(jnp.where(step - shift >= start, moved, 0.0).astype(BF))
    return pieces


def iso_body(geo, shifts, steps, start_one, start_two, weight_one, weight_two, out):
    parts = []
    hiddens = split_steps(steps, geo["m"])
    for b, (start, weight) in enumerate(((start_one, weight_one), (start_two, weight_two))):
        total = None
        channels = hiddens[b].shape[1]
        for i, piece in enumerate(tap_inputs(geo, b, shifts, hiddens[b], start[...])):
            term = dot(piece, weight[i * channels : (i + 1) * channels, :])
            total = term if total is None else total + term
        parts.append(total)
    out[...] = join_steps(parts, geo["n"]).astype(BF)


def iso_back_body(geo, shifts, d_iso, start_one, start_two, weight_one, weight_two, out):
    parts = []
    for b, (d, start, weight) in enumerate(
        zip(split_steps(d_iso, geo["m"]), (start_one, start_two), (weight_one, weight_two))
    ):
        count, channels = d.shape
        low = d.astype(BF)
        step = lax.broadcasted_iota(I32, (count, 1), 0)
        total = None
        for i in range(geo["touched"][b]):
            shift = jnp.maximum(shifts[b] - i, 0)
            stacked = dot_nt(low, weight[i * channels : (i + 1) * channels, :])
            stacked = jnp.where(step - shift >= start[...], stacked, 0.0)
            moved = pltpu.roll(stacked, lax.rem(count - shift, count), 0)
            total = moved if total is None else total + moved
        parts.append(total)
    out[...] = join_steps(parts, geo["n"]).astype(BF)


def iso_grad_body(geo, shifts, steps, d_iso, start_one, start_two, own, sent, wide_one, wide_two, halves):
    hiddens, ds = split_steps(steps, geo["m"]), split_steps(d_iso, geo["m"])
    begin = 0
    for b, (start, wide) in enumerate(((start_one, wide_one), (start_two, wide_two))):
        channels = hiddens[b].shape[1]
        right = ds[b].astype(BF)
        for i, piece in enumerate(tap_inputs(geo, b, shifts, hiddens[b], start[...])):
            wide[i * channels : (i + 1) * channels, :] = dot_tn(piece, right)
        part = geo["iso_slab"][b] // 2
        for h in range(2):
            at = pl.multiple_of(shifts[2 + b] + h * part, math.gcd(geo["iso_q"][b], part))
            halves[h, begin : begin + part, :] = wide[pl.ds(at, part), :].astype(BF)
        begin += part
    at = sum(geo["m"])
    norm_sums = jnp.sum(d_iso[:, at:, :].astype(F32), axis=0)
    rows = [*(column_sum(d) for d in ds), norm_sums[0:1], norm_sums[1:2]]
    store_core_parts(shifts[4], halves, rows, own, sent)


def branch_rows(pair, counts):
    total = sum(counts)
    step = lax.broadcasted_iota(I32, (total, 1), 0)
    return jnp.where(step < counts[0], pair[0:1, :], pair[1:2, :])


def hidden_one_body(geo, parts, bias, hidden, low):
    value = jnp.tanh(jnp.sum(parts[...].astype(F32), axis=0) + branch_rows(bias, geo["m"]))
    hidden[...] = value
    low[...] = jnp.broadcast_to(value.astype(BF)[None], low.shape)


def mix_body(geo, parts, bias, hidden_one, gain, shift, hidden, mixed):
    value = jnp.tanh(jnp.sum(parts[...].astype(F32), axis=0) + branch_rows(bias, geo["m"]))
    hidden[...] = value
    xhat, _ = norm_stats(value + hidden_one[...])
    low = (xhat * gain[...] + shift[...]).astype(BF)
    mixed[...] = jnp.broadcast_to(low[None], mixed.shape)


def mix_back_body(geo, parts, hidden_one, hidden_two, gain, d_pair, d_iso):
    d = jnp.sum(parts[...].astype(F32), axis=0)
    two = hidden_two[...]
    xhat, rstd = norm_stats(two + hidden_one[...])
    pair = norm_back(d, gain[...], xhat, rstd)
    iso = (1.0 - two * two) * pair
    d_pair[...] = pair
    blank = jnp.zeros((d_iso.shape[1] - iso.shape[0] - 2, iso.shape[1]), F32)
    low = jnp.concatenate([iso, column_sum(d * xhat), column_sum(d), blank], axis=0).astype(BF)
    d_iso[...] = jnp.broadcast_to(low[None], d_iso.shape)


def conv_back_body(geo, parts, d_pair, hidden_one, d_conv):
    one = hidden_one[...]
    d = (jnp.sum(parts[...].astype(F32), axis=0) + d_pair[...]) * (1.0 - one * one)
    d_conv[...] = jnp.broadcast_to(d.astype(BF)[None], d_conv.shape)


def place_head(geo, order, pieces, merge, expand, project):
    m_rows, h_rows = geo["quarter_rows"][:2]
    block = 0
    for piece in pieces:
        for i in range(piece.shape[0]):
            at = pl.multiple_of(order[block] * m_rows, m_rows)
            merge[pl.ds(at, m_rows), :] = piece[i, :m_rows, :]
            at = pl.ds(pl.multiple_of(order[block] * h_rows, h_rows), h_rows)
            expand[at, :] = piece[i, m_rows : m_rows + h_rows, :]
            project[at, :] = piece[i, m_rows + h_rows :, :]
            block += 1


def head_body(geo, *refs):
    taps = geo["taps"]
    pays, refs = refs[:taps], refs[taps:]
    (
        season, cotangent, up_bias, mix_gain, mix_shift, merge_bias, feed_gain, feed_shift,
        expand_bias, project_bias, final_gain, final_shift, orders,
    ) = refs[:13]
    refs = refs[13:]
    grads = 2 if geo["fits"] else 3
    if geo["fits"]:
        places, pieces, refs = refs[0], refs[1 : 1 + geo["pieces"]], refs[1 + geo["pieces"] :]
        merge_weight, expand_weight, project_weight = refs[-3:]
        refs = refs[:-3]
        place_head(geo, places, pieces, merge_weight, expand_weight, project_weight)
    else:
        (merge_weight, expand_weight, project_weight), refs = refs[:3], refs[3:]
    d_pays, (result, d_res_out, sums), refs = refs[:taps], refs[taps : taps + 3], refs[taps + 3 :]
    grad_outs, refs = refs[:grads], refs[grads:]
    slope, merge_in, normed_out, activ_out, d_sum_out, d_pre_out, d_merged_out = refs
    hidden_units = expand_weight.shape[0]
    rows, channels = cotangent.shape
    width = FFN_CHUNK
    chunks = expand_weight.shape[0] // width
    taps = load_taps(geo, pays, channels)
    ups, kept = [], []
    for b in range(2):
        up = jnp.tanh(dot(orders[b], taps[b]) + up_bias[b : b + 1, :])
        xhat, rstd = norm_stats(up + season[b])
        ups.append(up)
        kept.append((xhat, rstd))
        merge_in[:, b * channels : (b + 1) * channels] = (
            xhat * mix_gain[...] + mix_shift[...]
        ).astype(BF)
    merged = dot(merge_in[...], merge_weight[...]) + merge_bias[...]
    feed_hat, feed_rstd = norm_stats(merged)
    normed_out[...] = (feed_hat * feed_gain[...] + feed_shift[...]).astype(BF)

    def forward_chunk(c, total):
        at = pl.ds(pl.multiple_of(c * width, width), width)
        pre = dot_nt(normed_out[...], expand_weight[at, :]) + expand_bias[:, at]
        half = 0.5 + 0.5 * lax.erf(pre * math.sqrt(0.5))
        slope[c] = half + pre * (jnp.exp(-0.5 * pre * pre) * (1.0 / math.sqrt(2.0 * math.pi)))
        activ_out[:, at] = (pre * half).astype(BF)
        return total + dot(activ_out[:, at], project_weight[at, :])

    summed = lax.fori_loop(0, chunks, forward_chunk, merged + project_bias[...])
    final_hat, final_rstd = norm_stats(summed)
    result[...] = (final_hat * final_gain[...] + final_shift[...]).astype(BF)

    d_out = cotangent[...].astype(F32)
    sums[0:1, :] = column_sum(d_out * final_hat)
    sums[1:2, :] = column_sum(d_out)
    d_sum = norm_back(d_out, final_gain[...], final_hat, final_rstd)
    sums[2:3, :] = column_sum(d_sum)
    d_sum_out[...] = d_sum.astype(BF)

    def backward_chunk(c, total):
        at = pl.ds(pl.multiple_of(c * width, width), width)
        d_pre = slope[c] * dot_nt(d_sum_out[...], project_weight[at, :])
        sums[pl.ds(10 + c, 1), :] = column_sum(d_pre)
        d_pre_out[:, at] = d_pre.astype(BF)
        return total + dot(d_pre_out[:, at], expand_weight[at, :])

    d_normed = lax.fori_loop(0, chunks, backward_chunk, jnp.zeros((rows, channels), F32))
    sums[3:4, :] = column_sum(d_normed * feed_hat)
    sums[4:5, :] = column_sum(d_normed)
    d_merged = d_sum + norm_back(d_normed, feed_gain[...], feed_hat, feed_rstd)
    sums[5:6, :] = column_sum(d_merged)
    d_merged_out[...] = d_merged.astype(BF)
    gain_sum, shift_sum = 0.0, 0.0
    d_taps = []
    for b in range(2):
        d = dot_nt(d_merged_out[...], merge_weight[b * channels : (b + 1) * channels, :])
        xhat, rstd = kept[b]
        gain_sum = gain_sum + column_sum(d * xhat)
        shift_sum = shift_sum + column_sum(d)
        d_res = norm_back(d, mix_gain[...], xhat, rstd)
        d_res_out[b] = d_res
        d_up = (1.0 - ups[b] * ups[b]) * d_res
        sums[8 + b : 9 + b, :] = column_sum(d_up)
        d_taps.append(dot_tn(orders[b], d_up.astype(BF)))
    sums[6:7, :] = gain_sum
    sums[7:8, :] = shift_sum
    store_taps(geo, d_pays, d_taps)

    count = 10 + chunks
    sums[count:, :] = jnp.zeros((SUM_ROWS - count, channels), F32)
    pairs = ((merge_in, d_merged_out), (d_pre_out, normed_out), (activ_out, d_sum_out))
    if not geo["fits"]:
        for out, (left, right) in zip(grad_outs, pairs):
            out[...] = dot_tn(left[...], right[...]).astype(BF)
        return
    start = 0
    for (left, right), grad, size in zip(
        pairs, (merge_weight, expand_weight, project_weight), geo["quarter_rows"]
    ):
        grad[...] = dot_tn(left[...], right[...]).astype(BF)
        for h, out in enumerate(grad_outs):
            blocks = out.shape[0]
            for i in range(blocks):
                begin = pl.multiple_of(places[h * blocks + i] * size, size)
                out[i, start : start + size, :] = grad[pl.ds(begin, size), :]
        start += size
    low = sums[...].astype(BF)
    for out in grad_outs:
        out[:, start:, :] = jnp.broadcast_to(low, (out.shape[0], *low.shape))


def residual_body(d_res, info, out):
    rows = d_res.shape[1]
    columns = rows + 2 * HALO
    total = jnp.zeros((columns, d_res.shape[2]), F32)
    for b in range(2):
        counts, _ = average_counts(info[...], AVERAGES[b], columns)
        adjoint = dot_tn(counts.astype(F32).astype(BF), d_res[b].astype(BF))
        total = total - adjoint * (1.0 / AVERAGES[b])
    out[0:HALO, :] = total[0:HALO]
    out[HALO : HALO + rows, :] = total[HALO : HALO + rows] + d_res[0] + d_res[1]
    out[HALO + rows :, :] = total[HALO + rows :]


def input_back_body(geo, *refs):
    pays = refs[: geo["taps"]]
    matrices, residual, own, left, right = refs[geo["taps"] :]
    columns, channels = residual.shape
    rows = columns - 2 * HALO
    taps = load_taps(geo, pays, channels)
    total = residual[...]
    for b in range(2):
        total = total + dot_tn(matrices[b], taps[b]) * (1.0 / AVERAGES[b])
    left[...] = total[0:HALO]
    own[...] = total[HALO : HALO + rows]
    right[...] = total[HALO + rows :]


def swap(x):
    return lax.all_to_all(x, "tm", 0, 0)


def together(*values):
    return lax.optimization_barrier(values)


def after(x, dep):
    return lax.optimization_barrier((x, dep))[0]


def across(x, axis, bit):
    return lax.ppermute(x, axis, [(i, i ^ bit) for i in range(lax.axis_size(axis))])


def bit_of(axis, bit):
    return (lax.axis_index(axis) & bit) // bit


def tm_bits():
    return [1 << i for i in range(lax.axis_size("tm").bit_length() - 1)]


def flipped(x):
    bits = [("series", 1), ("series", 2)] + [("tm", b) for b in tm_bits()]
    for at, (axis, bit) in enumerate(bits):
        x = jnp.where(bit_of(axis, bit) == 1, jnp.flip(x, at), x)
    return x


def natural_rows(x):
    bits = len(tm_bits())
    x = flipped(x.reshape([2] * (bits + 2) + list(x.shape[1:])))
    x = jnp.transpose(x, [*range(bits + 1, 1, -1), 1, 0, bits + 2, bits + 3])
    return x.reshape(-1, x.shape[-1])


def relative_blocks(x):
    bits = len(tm_bits())
    x = x.reshape([2] * (bits + 2) + [x.shape[0] >> (bits + 2), x.shape[1]])
    x = jnp.transpose(x, [bits + 1, bits, *range(bits - 1, -1, -1), bits + 2, bits + 3])
    return flipped(x).reshape(-1, *x.shape[-2:])


def summed(*parts):
    return sum(p.astype(F32) for p in parts).astype(BF)


def neighbours(n):
    up = [(i, i + 1) for i in range(n - 1)]
    return up, [(j, i) for i, j in up]


def on_device(
    inputs, lengths,
    stride_weight_twelve, stride_bias_twelve, isometric_weight_twelve, isometric_bias_twelve,
    upsample_weight_twelve, upsample_bias_twelve,
    stride_weight_sixteen, stride_bias_sixteen, isometric_weight_sixteen, isometric_bias_sixteen,
    upsample_weight_sixteen, upsample_bias_sixteen,
    mix_gain, mix_shift, merge_weight, merge_bias, feed_gain, feed_shift,
    expand_weight, expand_bias, project_weight, project_bias, final_gain, final_shift, cotangent,
):
    n = lax.axis_size("tm")
    me = lax.axis_index("tm")
    rows, channels = inputs.shape[1:]
    stride_weights = (stride_weight_twelve, stride_weight_sixteen)
    iso_weights = (isometric_weight_twelve, isometric_weight_sixteen)
    up_weights = (upsample_weight_twelve, upsample_weight_sixteen)
    m = [rows // s for s in SCALES]
    slab = [w.shape[0] for w in stride_weights]
    q = math.gcd(*slab, channels)
    pay_rows = [slab[b] // q * m[b] for b in range(2)]
    iso_slab = [w.shape[0] for w in iso_weights]
    iso_q = [math.gcd(r, channels) for r in iso_slab]
    touched = [-(-(iso_slab[b] + channels - iso_q[b]) // channels) for b in range(2)]
    half = n // 2
    geo = {
        "n": n, "half": half, "m": m, "q": q, "slab": slab, "pay_rows": pay_rows, "touched": touched,
        "iso_slab": iso_slab, "iso_q": iso_q,
        "aligned": q % 128 == 0,
    }
    geo["taps"] = 1 if geo["aligned"] else 2
    pay_shape = (n, sum(pay_rows), q)
    pay_outs = [(pay_shape, BF)] if geo["aligned"] else [((rows, channels), BF)] * 2

    def as_payload(parts):
        return parts[0] if geo["aligned"] else join_payload(geo, parts)

    def as_taps(payload):
        return [payload] if geo["aligned"] else split_payload(geo, payload, channels)

    def row(v):
        return v[None, :]

    lengths_row = lengths[0]
    count = lengths_row.shape[0]
    upto = jnp.arange(count)[None, :] <= jnp.arange(count)[:, None]
    ends = UNIT * jnp.sum(jnp.where(upto, lengths_row[None, :], 0), axis=1)
    starts = ends - UNIT * lengths_row

    def bounds(places):
        inside = (starts[None, :] <= places[:, None]) & (places[:, None] < ends[None, :])
        first = jnp.sum(jnp.where(inside, starts[None, :], 0), axis=1)
        return first, jnp.sum(jnp.where(inside, ends[None, :], 0), axis=1)

    base = me * rows
    local = jnp.arange(rows, dtype=I32)

    def info_of(places, anchors):
        first, last = bounds(anchors + base)
        shift = base - HALO
        return jnp.stack([places + HALO, first - shift, last - 1 - shift], axis=1)

    token_info = info_of(local, local)
    window_infos, step_starts = [], []
    for b in range(2):
        tap, step = local // m[b], local % m[b]
        anchor = SCALES[b] * step
        window_infos.append(info_of(anchor - SCALES[b] // 2 + tap, anchor))
        all_steps = jnp.arange(n * m[b], dtype=I32)
        step_starts.append((bounds(SCALES[b] * all_steps)[0] // SCALES[b])[:, None])

    replica = lax.axis_index("series")

    head_weights = (merge_weight, expand_weight, project_weight)
    head_rows = [w.shape[0] for w in head_weights]
    quarter_rows = [r // 4 for r in head_rows]
    geo["quarter_rows"] = quarter_rows
    geo["fits"] = all(r % 16 == 0 for r in quarter_rows)
    quarter = jnp.concatenate(
        [lax.dynamic_slice_in_dim(w, replica * r, r) for w, r in zip(head_weights, quarter_rows)], axis=0
    )
    stride_own = jnp.concatenate(stride_weights, axis=0)
    up_own = jnp.concatenate(up_weights, axis=0)

    far, bit = [0], half
    while bit > 1:
        far, bit = far + [o ^ bit for o in far], bit // 2
    near = [o ^ 1 for o in far]
    half_order = [(o, r) for r in (0, 2) for o in far + near]
    relative = half_order + [(o, r ^ 1) for o, r in half_order]
    order = jnp.stack([(me ^ o) * 4 + (replica ^ r) for o, r in relative]).astype(I32)

    iso_first = [(iso_slab[b] * me) // channels for b in range(2)]
    iso_offset = [iso_slab[b] * me - iso_first[b] * channels for b in range(2)]
    iso_wide = []
    for b in range(2):
        if touched[b] * channels == iso_slab[b]:
            iso_wide.append(iso_weights[b])
        else:
            blank = jnp.zeros((touched[b] * channels, channels), BF)
            iso_wide.append(lax.dynamic_update_slice(blank, iso_weights[b], (iso_offset[b], 0)))
    shifts = jnp.stack([*(TAPS[b] - 1 - iso_first[b] for b in range(2)), *iso_offset, replica & 1]).astype(I32)

    up_route, down_route = neighbours(n)
    tokens = inputs[0]
    step_block = [((n, sum(m), channels), BF)]
    own_steps = (sum(m), channels)
    blocks = quarter[None]
    left, right, got = together(
        lax.ppermute(tokens[rows - HALO :], "tm", up_route),
        lax.ppermute(tokens[:HALO], "tm", down_route),
        across(blocks, "tm", half),
    )
    blocks, bit = jnp.concatenate([blocks, got]), half // 2
    while bit > 2:
        blocks, bit = jnp.concatenate([blocks, across(blocks, "tm", bit)]), bit // 2
    matrices, orders = kernel_call(
        matrices_body,
        [((2, rows, rows + 2 * HALO), BF), ((2, rows, rows), BF)],
        window_infos,
        24,
    )
    windows = kernel_call(
        functools.partial(windows_body, geo), pay_outs, (tokens, left, right, matrices), 24
    )
    windows, got = together(swap(as_payload(windows)), across(blocks, "tm", bit))
    blocks = jnp.concatenate([blocks, got])
    middle = blocks.shape[0] // 2
    (partial,) = kernel_call(
        functools.partial(slab_in_body, geo), step_block, (windows, stride_own), 24
    )
    low_blocks, high_blocks = blocks[:middle], blocks[middle:]
    partial, x_low, y_high = together(
        swap(partial), across(low_blocks, "tm", 1), across(high_blocks, "series", 2)
    )
    hidden_one, hidden_low = kernel_call(
        functools.partial(hidden_one_body, geo),
        [(own_steps, F32), ((n, *own_steps), BF)],
        (partial, jnp.stack([stride_bias_twelve, stride_bias_sixteen])),
        8,
    )
    hidden_all, y_low = together(swap(hidden_low), across(low_blocks, "series", 2))
    (partial,) = kernel_call(
        functools.partial(iso_body, geo),
        step_block,
        (shifts, hidden_all, *step_starts, *iso_wide),
        32,
        scalars=(0,),
    )
    partial, x_high = together(swap(partial), across(after(high_blocks, partial), "tm", 1))
    first = (x_low, x_high, y_low, y_high)
    hidden_two, mixed_low = kernel_call(
        functools.partial(mix_body, geo),
        [(own_steps, F32), ((n, *own_steps), BF)],
        (
            partial,
            jnp.stack([isometric_bias_twelve, isometric_bias_sixteen]),
            hidden_one,
            row(mix_gain),
            row(mix_shift),
        ),
        8,
    )
    (season,) = kernel_call(
        season_body, [((2, rows, channels), F32)], (tokens, left, right, token_info), 24
    )
    mixed_all, season, blocks_a, blocks_b = together(
        swap(mixed_low),
        season,
        across(after(x_low, mixed_low), "series", 2),
        across(after(y_high, mixed_low), "tm", 1),
    )
    (ups,) = kernel_call(
        functools.partial(slab_out_body, geo), [(pay_shape, BF)], (mixed_all, up_own), 24
    )
    head_pieces = [blocks, *first, blocks_a, blocks_b]
    ups, *other_pieces = together(swap(ups), *(across(p, "series", 1) for p in head_pieces))
    head_pieces += other_pieces
    geo["pieces"] = len(head_pieces)
    hidden_units = 4 * n * quarter_rows[1]
    head_args = [
        *as_taps(ups), season, cotangent[0], jnp.stack([upsample_bias_twelve, upsample_bias_sixteen]),
        row(mix_gain), row(mix_shift), row(merge_bias), row(feed_gain), row(feed_shift),
        row(expand_bias), row(project_bias), row(final_gain), row(final_shift), orders,
    ]
    head_scratch = [
        pltpu.VMEM((hidden_units // FFN_CHUNK, rows, FFN_CHUNK), F32),
        *(
            pltpu.VMEM((rows, width), BF)
            for width in (2 * channels, channels, hidden_units, channels, hidden_units, channels)
        ),
    ]
    scalars = ()
    if geo["fits"]:
        scalars = (len(head_args),)
        head_args += [order, *head_pieces]
        head_scratch += [pltpu.VMEM((2 * channels, channels), BF)]
        head_scratch += [pltpu.VMEM((hidden_units, channels), BF)] * 2
    else:
        cuts = [quarter_rows[0], sum(quarter_rows[:2])]
        head_args += [natural_rows(w) for w in jnp.split(jnp.concatenate(head_pieces), cuts, axis=1)]
    half_blocks = (2 * n, sum(quarter_rows) + SUM_ROWS, channels)
    head = kernel_call(
        functools.partial(head_body, geo),
        [
            *pay_outs,
            ((rows, channels), BF),
            ((2, rows, channels), F32),
            ((SUM_ROWS, channels), F32),
            *(
                [(half_blocks, BF)] * 2
                if geo["fits"]
                else [((4 * r * n, channels), BF) for r in quarter_rows]
            ),
        ],
        head_args,
        60,
        scalars=scalars,
        scratch=head_scratch,
    )
    d_ups, (result, d_res, head_sums, *head_grads) = head[: geo["taps"]], head[geo["taps"] :]

    if geo["fits"]:
        head_own, head_other = head_grads
    else:
        whole = [relative_blocks(g) for g in head_grads]
        whole.append(jnp.broadcast_to(head_sums.astype(BF), (4 * n, *head_sums.shape)))
        head_own, head_other = jnp.split(jnp.concatenate(whole, axis=1), 2)
    (residual,) = kernel_call(
        residual_body, [((rows + 2 * HALO, channels), F32)], (d_res, token_info), 24
    )
    head_sum = summed(head_own, across(head_other, "series", 1))
    head_sum = head_sum.reshape(2, 2, 2, len(far) // 2, *half_blocks[1:])
    d_ups, head_sum, residual, x_1, y_1 = together(
        swap(as_payload(d_ups)),
        head_sum,
        residual,
        across(head_sum[1, 1, 0], "tm", 1),
        across(head_sum[1, 1, 1], "series", 2),
    )
    core = (replica & 1).reshape(1)

    def slab_grads(payload, steps):
        part = (sum(slab) // 2 + SUM_ROWS, channels)
        return kernel_call(
            functools.partial(slab_grad_body, geo),
            [(part, BF)] * 2,
            (core, payload, steps),
            24,
            scalars=(0,),
            scratch=[pltpu.VMEM((2, *part), BF)],
        )

    def cut(x, thirds=2):
        at = x.shape[0] * thirds // 48 * 16
        return x[:at], x[at:]

    (partial,) = kernel_call(
        functools.partial(slab_in_body, geo), step_block, (d_ups, up_own), 24
    )
    up_mine, up_sent = slab_grads(d_ups, mixed_all)
    head_x = summed(head_sum[1, 0, 0], x_1)
    head_y = summed(head_sum[0, 1, 1], y_1)
    partial, x_0, y_0, up_mine, up_sent, head_x, head_y = together(
        swap(partial),
        across(head_sum[0, 1, 0], "tm", 1),
        across(head_sum[1, 0, 1], "series", 2),
        up_mine,
        up_sent,
        head_x,
        head_y,
    )
    d_pair, d_iso = kernel_call(
        functools.partial(mix_back_body, geo),
        [(own_steps, F32), ((n, sum(m) + 8, channels), BF)],
        (partial, hidden_one, hidden_two, row(mix_gain)),
        8,
    )
    up_part = summed(up_mine, across(up_sent, "series", 1))
    head_sum = (
        summed(head_sum[0, 0, 0], x_0, across(after(head_x, d_iso), "series", 2)),
        summed(head_sum[0, 0, 1], y_0, across(after(head_y, d_iso), "tm", 1)),
    )
    d_iso_all, up_part, *head_sum = together(swap(d_iso), up_part, *head_sum)
    (partial,) = kernel_call(
        functools.partial(iso_back_body, geo),
        step_block,
        (shifts, d_iso_all, *step_starts, *iso_wide),
        32,
        scalars=(0,),
    )
    part = (sum(iso_slab) // 2 + SUM_ROWS, channels)
    iso_mine, iso_sent = kernel_call(
        functools.partial(iso_grad_body, geo),
        [(part, BF)] * 2,
        (shifts, hidden_all, d_iso_all, *step_starts),
        32,
        scalars=(0,),
        scratch=[
            *(pltpu.VMEM((touched[b] * channels, channels), F32) for b in range(2)),
            pltpu.VMEM((2, *part), BF),
        ],
    )
    head_sum, bit = summed(head_sum[0], across(after(head_sum[1], partial), "tm", 2)), 4
    while bit < half:
        head_sum, got = jnp.split(head_sum, 2)
        head_sum, bit = summed(head_sum, across(got, "tm", bit)), 2 * bit
    partial, iso_mine, iso_sent, up_a, head_sum = together(
        swap(partial), iso_mine, iso_sent, across(up_part, "series", 2), head_sum
    )
    (d_conv,) = kernel_call(
        functools.partial(conv_back_body, geo), [((n, *own_steps), BF)], (partial, d_pair, hidden_one), 8
    )
    iso_part = summed(after(iso_mine, d_conv), across(iso_sent, "series", 1))
    up_part = summed(after(up_part, d_conv), up_a)
    iso_low, iso_high = cut(iso_part, 1)
    d_conv_all, up_part, iso_part, iso_high, iso_a = together(
        swap(d_conv), up_part, iso_part, iso_high, across(iso_low, "series", 2)
    )

    def grads_of(part, got, sizes):
        return kernel_call(
            join_body,
            [((size, channels), F32) for size in (*sizes, 2 * SUM_ROWS)],
            (core, part, got),
            24,
            scalars=(0,),
        )

    (d_windows,) = kernel_call(
        functools.partial(slab_out_body, geo), [(pay_shape, BF)], (d_conv_all, stride_own), 24
    )
    stride_mine, stride_sent = slab_grads(windows, d_conv_all)
    stride_part = summed(stride_mine, across(stride_sent, "series", 1))
    iso_b = across(iso_high, "series", 2)
    stride_y = across(stride_part, "series", 2)
    d_windows, up_part, up_got = together(
        swap(d_windows), up_part, across(up_part, "series", 1)
    )
    edge = ((HALO, channels), F32)
    own, to_left, to_right = kernel_call(
        functools.partial(input_back_body, geo),
        [((rows, channels), F32), edge, edge],
        (*as_taps(d_windows), matrices, residual),
        24,
    )
    iso_part = summed(after(iso_part, own), jnp.concatenate([iso_a, iso_b]))
    head_mine = summed(head_sum[0], across(after(head_sum[1], d_windows), "tm", half))
    at = sum(quarter_rows)
    head_y = across(head_mine[:at], "series", 2)
    from_right, from_left = together(
        lax.ppermute(to_left, "tm", down_route), lax.ppermute(to_right, "tm", up_route)
    )
    ups = grads_of(after(up_part, own), up_got, slab)
    input_grad = jnp.concatenate(
        [own[:HALO] + from_left, own[HALO : rows - HALO], own[rows - HALO :] + from_right], axis=0
    ).astype(BF)
    stride_part = summed(stride_part, stride_y)
    stride_got, iso_got = across(stride_part, "series", 1), across(iso_part, "series", 1)
    head_y = jnp.where(
        bit_of("series", 2) == 0, jnp.stack([head_mine[:at], head_y]), jnp.stack([head_y, head_mine[:at]])
    )
    head_got = across(head_y, "series", 1)
    head_grad = jnp.where(
        bit_of("series", 1) == 0, jnp.stack([head_y, head_got], axis=1), jnp.stack([head_got, head_y], axis=1)
    )
    head_grad = head_grad.reshape(4, *head_grad.shape[2:]).astype(F32)
    head_grads = [
        g.reshape(-1, channels)
        for g in jnp.split(head_grad, [quarter_rows[0], sum(quarter_rows[:2])], axis=1)
    ]
    sums = head_mine[at:].astype(F32)
    count = expand_bias.shape[0] // channels
    expand_grad = sums[10 : 10 + count].reshape(-1)

    strides = grads_of(stride_part, stride_got, slab)
    isos = grads_of(iso_part, iso_got, iso_slab)
    return (
        result[None],
        input_grad[None],
        strides[0], strides[2][0], isos[0], isos[2][0], ups[0], sums[8],
        strides[1], strides[2][1], isos[1], isos[2][1], ups[1], sums[9],
        isos[2][2] + sums[6], isos[2][3] + sums[7],
        head_grads[0], sums[5], sums[3], sums[4],
        head_grads[1], expand_grad, head_grads[2], sums[2], sums[0], sums[1],
    )


def solution(mesh):
    tokens, weight, whole = P("series", "tm", None), P("tm", None), P()
    pair = (weight, whole)
    return jax.shard_map(
        on_device,
        mesh=mesh,
        in_specs=(
            tokens, P("series", None), *(pair * 6), whole, whole, *pair, whole, whole, *pair, *pair, whole, whole,
            tokens,
        ),
        out_specs=(tokens, tokens, *(pair * 6), whole, whole, *pair, whole, whole, *pair, *pair, whole, whole),
        check_vma=False,
    )
```
